32 devices in a mesh: groups: 2 (over y), image: 2 (over x), space: 4 (over z), yslab: 2 (over core).
Axes of the slice: x: 2, y: 2, z: 4, core: 2. Of those that a mesh axis runs over, the one named last changes fastest.
Arguments:
- images: float32 [8, 64, 128, 256], P(('groups', 'image'), 'space', 'yslab'), parts along dimension 0, may hold values from -4 to 4, as said below
Outputs:
- new_band: float32 [8, 64, 128, 256], P(('groups', 'image'), 'space', 'yslab'), parts along dimension 0
- parallel: float32 [8], P(('groups', 'image')), parts along dimension 0
The draws below stay inside these ranges and needn't reach their ends.
There are 2 independent parts, one for each index of `groups`. The reference program is written for one: setup_inputs(seed, part) draws one part's arguments, and reference() takes and returns one part's arrays. A program takes and returns all parts, laid end to end along the dimension named above; each array names one. Nothing has to cross between parts.
Inputs may be any that keep to these rules, and one draw needn't show every extreme that they name: `images`: concentration fields of a path between two end states.
All inputs are finite; a program needn't handle non-finite values.
Results may differ from the reference program's by a relative error of at most 0.0001.
Values sent between devices are 32-bit elements; how exact they have to be, the bound alone decides.
No kernel may reach another device: no remote copies, remote signals or barrier semaphores. Data moves between devices by JAX's collectives and lax.ppermute only.
A program may use at most 64 MiB of HBM per device.

```python
import jax
import jax.numpy as jnp
from jax import lax

NX = 256
ITERS = 2
IMAGES = 4
NZ = 64
NY = 128


def draw_images(key, part):
    key_base = jax.random.fold_in(key, 11)
    key_rough = jax.random.fold_in(key, 12)
    key_spacing = jax.random.fold_in(key, 13)
    key_noise = jax.random.fold_in(key, 14)
    z_frac = (jnp.arange(NZ, dtype=jnp.float32) / NZ)[:, None, None]
    y_frac = (jnp.arange(NY, dtype=jnp.float32) / NY)[None, :, None]
    x_frac = (jnp.arange(NX, dtype=jnp.float32) / NX)[None, None, :]
    amplitude = 0.1 * jnp.power(10.0, 0.7 * z_frac + 0.15 * y_frac + 0.15 * x_frac)
    rough_part = jax.random.uniform(key_rough, (NZ, NY, NX), jnp.float32, -1.7, 1.7)
    base_field = 0.3 * jax.random.uniform(key_base, (NZ, NY, NX), jnp.float32, -1.0, 1.0)
    image_pos = jnp.arange(IMAGES, dtype=jnp.float32)
    jitter = jax.random.uniform(key_spacing, (IMAGES,), jnp.float32, -0.35, 0.35)
    interior = (image_pos > 0.5) & (image_pos < IMAGES - 1.5)
    along_path = (image_pos + jnp.where(interior, jitter, 0.0)) / (IMAGES - 1)
    noise = 0.05 * jax.random.uniform(key_noise, (IMAGES, NZ, NY, NX), jnp.float32, -1.0, 1.0) * amplitude
    return base_field[None] + along_path[:, None, None, None] * (amplitude * rough_part)[None] + noise


def setup_inputs(seed: int = 0, part: int = 0) -> dict:
    streams_of = jax.random.split(jax.random.key(seed), 2)
    own_keys = jax.random.split(jax.random.fold_in(streams_of[1], part), 2)
    images = draw_images(jax.random.fold_in(jax.random.fold_in(streams_of[1], part), 71), part)
    return dict(images=images)


GRADIENT_COEF = 1.0
MOBILITY = 0.004
SPRING_K = 1.0
STEP_SIZE = 0.5
EPSILON = 1e-06

def laplace(field):
    neighbours = jnp.roll(field, -1, 0) + jnp.roll(field, 1, 0)
    neighbours = neighbours + jnp.roll(field, -1, 1) + jnp.roll(field, 1, 1)
    neighbours = neighbours + jnp.roll(field, -1, 2) + jnp.roll(field, 1, 2)
    return neighbours - 6.0 * field

def force_of(field):
    potential = field * field * field - field - GRADIENT_COEF * laplace(field)
    return MOBILITY * laplace(potential)

def reference(images):
    current = images
    image_ids = jnp.arange(IMAGES, dtype=jnp.int32)
    interior = (image_ids > 0) & (image_ids < IMAGES - 1)
    cell_total = float(NX * NY * NZ)
    parallel = jnp.zeros((IMAGES,), jnp.float32)
    for iteration in range(ITERS):
        driving = lax.map(force_of, current)
        blank = jnp.zeros_like(current[:1])
        ahead = jnp.concatenate([current[1:], blank], 0)
        behind = jnp.concatenate([blank, current[:-1]], 0)
        forward = ahead - current
        backward = current - behind
        tangent = forward + backward
        plus_sq = lax.optimization_barrier(jnp.sum(forward * forward, axis=(1, 2, 3)))
        minus_sq = lax.optimization_barrier(jnp.sum(backward * backward, axis=(1, 2, 3)))
        tangent_sq = lax.optimization_barrier(jnp.sum(tangent * tangent, axis=(1, 2, 3)))
        parallel_sum = lax.optimization_barrier(jnp.sum(driving * tangent, axis=(1, 2, 3)))
        project_coef = parallel_sum / (tangent_sq + EPSILON)
        spring = SPRING_K * (jnp.sqrt(plus_sq) - jnp.sqrt(minus_sq)) / jnp.sqrt(tangent_sq + EPSILON)
        update = driving - project_coef[:, None, None, None] * tangent + spring[:, None, None, None] * tangent
        current = jnp.where(interior[:, None, None, None], current + STEP_SIZE * update, current)
        parallel = jnp.where(interior, parallel_sum / jnp.sqrt((tangent_sq + EPSILON) * cell_total), jnp.float32(0.0))
    return (current, parallel)
```

```python
import functools

import jax
import jax.numpy as jnp
from jax import lax
from jax.experimental import pallas as pl
from jax.experimental.pallas import tpu as pltpu
from jax.sharding import PartitionSpec as P

ITERS = 2


GRADIENT_COEF = 1.0
MOBILITY = 0.004
SPRING_K = 1.0
STEP_SIZE = 0.5
EPSILON = 1e-06

PAD = 8
VMEM_LIMIT = 48 * 2**20


def passed_along(array, axis, by):
    peers = lax.axis_size(axis)
    pairs = [(i, i + by) for i in range(peers) if 0 <= i + by < peers]
    return lax.ppermute(array, axis, pairs)


def extended(cells, sides, width):
    for axis, dim in sides:
        count = lax.axis_size(axis)
        head = lax.slice_in_dim(cells, 0, width, axis=dim)
        tail = lax.slice_in_dim(cells, cells.shape[dim] - width, cells.shape[dim], axis=dim)
        cells = jnp.concatenate(
            [
                lax.ppermute(tail, axis, [(i, (i + 1) % count) for i in range(count)]),
                cells,
                lax.ppermute(head, axis, [((i + 1) % count, i) for i in range(count)]),
            ],
            axis=dim,
        )
    return cells


def stencil(padded):
    middle = padded[:, 1:-1, 1:-1]
    neighbours = padded[:, 2:, 1:-1] + padded[:, :-2, 1:-1]
    neighbours = neighbours + padded[:, 1:-1, 2:] + padded[:, 1:-1, :-2]
    neighbours = neighbours + jnp.roll(middle, -1, 3) + jnp.roll(middle, 1, 3)
    return neighbours - 6.0 * middle


def sum_cells(field):
    return jnp.sum(field, axis=(1, 2, 3))


def body_any(images):
    current = images
    per_device = current.shape[0]
    total_images = per_device * lax.axis_size("image")
    cell_total = float(
        current.shape[1]
        * lax.axis_size("space")
        * current.shape[2]
        * lax.axis_size("yslab")
        * current.shape[3]
    )
    image_ids = lax.axis_index("image") * per_device + jnp.arange(per_device, dtype=jnp.int32)
    interior = (image_ids > 0) & (image_ids < total_images - 1)
    parallel = jnp.zeros((per_device,), jnp.float32)
    for iteration in range(ITERS):
        next_first = passed_along(current[0], "image", -1)
        prev_last = passed_along(current[-1], "image", 1)
        ahead = jnp.concatenate([current[1:], next_first[None]], 0)
        behind = jnp.concatenate([prev_last[None], current[:-1]], 0)
        forward = ahead - current
        backward = current - behind
        tangent = forward + backward
        plus_sq, minus_sq, tangent_sq = lax.psum(
            (
                sum_cells(forward * forward),
                sum_cells(backward * backward),
                sum_cells(tangent * tangent),
            ),
            ("space", "yslab"),
        )
        wide_pad = extended(current, (("space", 1), ("yslab", 2)), 2)
        inner_field = wide_pad[:, 1:-1, 1:-1]
        potential = (
            inner_field * inner_field * inner_field
            - inner_field
            - GRADIENT_COEF * stencil(wide_pad)
        )
        driving = MOBILITY * stencil(potential)
        parallel_sum = lax.psum(sum_cells(driving * tangent), ("space", "yslab"))
        project_coef = parallel_sum / (tangent_sq + EPSILON)
        spring = (
            SPRING_K * (jnp.sqrt(plus_sq) - jnp.sqrt(minus_sq)) / jnp.sqrt(tangent_sq + EPSILON)
        )
        update = (
            driving
            - project_coef[:, None, None, None] * tangent
            + spring[:, None, None, None] * tangent
        )
        current = jnp.where(interior[:, None, None, None], current + STEP_SIZE * update, current)
        parallel = jnp.where(
            interior, parallel_sum / jnp.sqrt((tangent_sq + EPSILON) * cell_total), jnp.float32(0.0)
        )
    return (current, parallel)


def call(kernel, out_shape, scratch=(), name=None, vmem_out=None, **kw):
    return pl.pallas_call(
        kernel,
        out_shape=out_shape,
        scratch_shapes=list(scratch),
        name=name,
        compiler_params=pltpu.CompilerParams(vmem_limit_bytes=VMEM_LIMIT),
        **kw,
    )


def shape(*dims):
    return jax.ShapeDtypeStruct(dims, jnp.float32)


def lap(below, here, above):
    rows, lanes = here.shape
    ys = pltpu.roll(here, 1, 0) + pltpu.roll(here, rows - 1, 0)
    xs = pltpu.roll(here, 1, 1) + pltpu.roll(here, lanes - 1, 1)
    return (below + above) + ys + xs - 6.0 * here


def driving_layers(field, pot, count, emit):
    def first(k, carry):
        here = field[k + 1]
        pot[k] = here * here * here - here - GRADIENT_COEF * lap(field[k], here, field[k + 2])
        return carry

    lax.fori_loop(0, count + 2, first, 0)

    def second(k, carry):
        return emit(k, MOBILITY * lap(pot[k], pot[k + 1], pot[k + 2]), carry)

    return second


def rows_sum(field):
    rows, lanes = field.shape
    return jnp.sum(field.reshape(rows // 8, 8, lanes), axis=0)


def lane_row(total):
    lanes = total.shape[1]
    folded = jnp.sum(total.reshape(8, lanes // 128, 128), axis=1)
    return jnp.sum(folded, axis=0, keepdims=True)


def fill_padded(dst, low, mid, high, sides, sides_at):
    rows = mid.shape[1]
    n_low, n_mid, n_high = low.shape[0], mid.shape[0], high.shape[0]
    dst[0:n_low, PAD : PAD + rows] = low[...]
    dst[n_low : n_low + n_mid, PAD : PAD + rows] = mid[...]
    dst[n_low + n_mid : n_low + n_mid + n_high, PAD : PAD + rows] = high[...]
    layers = n_low + n_mid + n_high
    dst[:, 0:PAD] = sides[sides_at : sides_at + layers, PAD : 2 * PAD]
    dst[:, PAD + rows : 2 * PAD + rows] = sides[sides_at : sides_at + layers, 0:PAD]


def split_kernel(images, mine, end, up, down, sems):
    which = 1 - lax.axis_index("image")
    nz = mine.shape[0]
    copies = [
        pltpu.make_async_copy(src, dst, sems.at[i])
        for i, (src, dst) in enumerate(
            [
                (images.at[which], mine),
                (images.at[which, pl.ds(nz - 4, 4)], up.at[pl.ds(0, 4)]),
                (images.at[1 - which, pl.ds(nz - 2, 2)], up.at[pl.ds(4, 2)]),
                (images.at[which, pl.ds(0, 4)], down.at[pl.ds(0, 4)]),
                (images.at[1 - which, pl.ds(0, 2)], down.at[pl.ds(4, 2)]),
                (images.at[1 - which], end),
            ]
        )
    ]
    for c in copies:
        c.start()
    for c in copies:
        c.wait()


def first_step_kernel(mine, end, low, high, sides, step_out, drive_out, end_out, field, pot):
    nz, rows, _ = mine.shape
    fill_padded(field, low.at[0:4], mine, high.at[0:4], sides, 0)
    fill_padded(end_out, low.at[4:6], end, high.at[4:6], sides, nz + 8)

    def emit(k, drive, carry):
        step_out[k] = field[k + 2] + STEP_SIZE * drive

        @pl.when((k >= 2) & (k < nz + 2))
        def _():
            drive_out[k - 2] = drive[PAD : PAD + rows]

        return carry

    lax.fori_loop(0, nz + 4, driving_layers(field, pot, nz + 4, emit), 0)


def sums_of(count, lanes, fields):
    def one(k, totals):
        plus, minus, tangent, drive = fields(k)
        terms = (plus * plus, minus * minus, tangent * tangent, drive * tangent)
        return tuple(t + rows_sum(v) for t, v in zip(totals, terms))

    zero = jnp.zeros((8, lanes), jnp.float32)
    return lax.fori_loop(0, count, one, (zero,) * 4)


def write_sums(out, totals):
    out[...] = jnp.zeros_like(out)
    for i, total in enumerate(totals):
        out[i : i + 1] = lane_row(total)


def first_sums_kernel(other, mine, end, drive, out):
    nz, _, lanes = mine.shape

    def fields(k):
        m, o, e = mine[k], other[k], end[k]
        return o - m, m - e, o - e, drive[k]

    write_sums(out, sums_of(nz, lanes, fields))


def coefficient(parts, base, count):
    total = parts[base]
    for i in range(1, count):
        total = total + parts[base + i]
    total = jnp.sum(total, axis=1, keepdims=True)
    plus_sq, minus_sq, tangent_sq, par = (total[i : i + 1] for i in range(4))
    safe = tangent_sq + EPSILON
    spring = SPRING_K * (jnp.sqrt(plus_sq) - jnp.sqrt(minus_sq)) / jnp.sqrt(safe)
    return STEP_SIZE * (spring - par / safe), par, safe


def other_step_kernel(other, low, high, sides, step_out, field_out, pot):
    nz, rows, _ = other.shape
    fill_padded(field_out, low, other, high, sides, 0)

    def emit(k, drive, carry):
        step_out[k] = other[k] + STEP_SIZE * drive[PAD : PAD + rows]
        return carry

    lax.fori_loop(0, nz, driving_layers(field_out, pot, nz, emit), 0)


def second_step_kernel(parts, step, end_wide, other_wide, moved_out, drive_out, field, pot):
    nz, rows, _ = drive_out.shape
    half = parts.shape[0] // 2
    coef, _, _ = coefficient(parts, half * lax.axis_index("image"), half)

    def move(k, carry):
        field[k] = step[k] + coef * (other_wide[k] - end_wide[k])
        return carry

    lax.fori_loop(0, nz + 4, move, 0)

    def emit(k, drive, carry):
        drive_out[k] = drive[PAD : PAD + rows]
        moved_out[k] = field[k + 2][PAD : PAD + rows]
        return carry

    lax.fori_loop(0, nz, driving_layers(field, pot, nz, emit), 0)


def second_sums_kernel(parts, far, mine, end, other_step, moved, drive, tangent_out, out):
    nz, _, lanes = mine.shape
    half = parts.shape[0] // 2
    coef, _, _ = coefficient(parts, half * (1 - lax.axis_index("image")), half)

    def fields(k):
        o = other_step[k] + coef * (mine[k] - far[k])
        m, e = moved[k], end[k]
        tangent = o - e
        tangent_out[k] = tangent
        return o - m, m - e, tangent, drive[k]

    write_sums(out, sums_of(nz, lanes, fields))


def last_kernel(cells, parts, moved, drive, tangent, base, out, par_out, buf, sems):
    del base
    nz = moved.shape[0]
    at = lax.axis_index("image")
    which = 1 - at
    coef, par, safe = coefficient(parts, 0, parts.shape[0])
    copies = []
    for k in range(nz):
        buf[k] = moved[k] + STEP_SIZE * drive[k] + coef * tangent[k]
        if k % 4 == 3:
            where = pl.ds(k - 3, 4)
            copies.append(
                pltpu.make_async_copy(buf.at[where], out.at[which, where], sems.at[k // 4])
            )
            copies[-1].start()
    value = (par / jnp.sqrt(safe * cells))[0, 0]
    sign = jnp.where(at == 0, 1.0, -1.0).astype(jnp.float32)
    par_out[which] = value * sign
    par_out[1 - which] = jnp.float32(0.0)
    for c in copies:
        c.wait()


ANY = pl.BlockSpec(memory_space=pl.ANY)
VMEM = pl.BlockSpec(memory_space=pltpu.VMEM)
SMEM = pl.BlockSpec(memory_space=pltpu.SMEM)
DMA = pltpu.SemaphoreType.DMA
SWAP = [(0, 1), (1, 0)]


def copy_kernel(src, dst, sem):
    c = pltpu.make_async_copy(src, dst, sem)
    c.start()
    c.wait()


def from_z(up, down):
    count = lax.axis_size("space")
    low = lax.ppermute(up, "space", [(i, (i + 1) % count) for i in range(count)])
    high = lax.ppermute(down, "space", [((i + 1) % count, i) for i in range(count)])
    return low, high


def y_sides(*pieces):
    rows = pieces[0].shape[1]
    ends = [jnp.concatenate([p[:, :PAD], p[:, rows - PAD :]], 1) for p in pieces]
    return lax.ppermute(jnp.concatenate(ends, 0), "yslab", SWAP)


def to_all(sums, axes):
    peers = lax.axis_size(axes)
    spread = jnp.broadcast_to(sums[None], (peers,) + sums.shape)
    return lax.all_to_all(spread, axes, 0, 0, tiled=True)


def body_pair(images):
    _, nz, ny, nx = images.shape
    wide = ny + 2 * PAD
    cells = float(nz * lax.axis_size("space") * ny * lax.axis_size("yslab") * nx)
    block = shape(nz, ny, nx)

    mine, end, up, down = call(
        split_kernel,
        [block, block, shape(6, ny, nx), shape(6, ny, nx)],
        [DMA((6,))],
        "split",
        in_specs=[ANY],
        out_specs=[ANY] * 4,
    )(images)

    other = lax.ppermute(mine, "image", SWAP)
    low, high = from_z(up, down)
    end_later, low, high = lax.optimization_barrier((end, low, high))
    far = lax.ppermute(end_later, "image", SWAP)

    base = call(
        copy_kernel,
        jax.ShapeDtypeStruct(images.shape, images.dtype),
        [DMA],
        "base",
        in_specs=[ANY],
        out_specs=ANY,
    )(images)

    sides = y_sides(low[:4], mine, high[:4], low[4:], end, high[4:])
    step, drive, end_wide = call(
        first_step_kernel,
        [shape(nz + 4, wide, nx), block, shape(nz + 4, wide, nx)],
        [pltpu.VMEM((nz + 8, wide, nx), jnp.float32), pltpu.VMEM((nz + 6, wide, nx), jnp.float32)],
        "first_step",
    )(mine, end, low, high, sides)

    sums = call(first_sums_kernel, shape(8, 128), name="first_sums")(other, mine, end, drive)
    parts = to_all(sums, ("image", "space", "yslab"))

    o_low, o_high = from_z(other[nz - 2 :], other[:2])
    o_sides = y_sides(o_low, other, o_high)
    other_step, other_wide = call(
        other_step_kernel,
        [block, shape(nz + 4, wide, nx)],
        [pltpu.VMEM((nz + 2, wide, nx), jnp.float32)],
        "other_step",
    )(other, o_low, o_high, o_sides)

    moved, drive2 = call(
        second_step_kernel,
        [block, block],
        [pltpu.VMEM((nz + 4, wide, nx), jnp.float32), pltpu.VMEM((nz + 2, wide, nx), jnp.float32)],
        "second_step",
    )(parts, step, end_wide, other_wide)

    tangent, sums = call(second_sums_kernel, [block, shape(8, 128)], name="second_sums")(
        parts, far, mine, end, other_step, moved, drive2
    )
    parts = to_all(sums, ("space", "yslab"))

    return call(
        functools.partial(last_kernel, cells),
        [jax.ShapeDtypeStruct(images.shape, images.dtype), shape(2)],
        [pltpu.VMEM(block.shape, jnp.float32), DMA((nz // 4,))],
        "last",
        in_specs=[VMEM] * 4 + [ANY],
        out_specs=[ANY, SMEM],
        input_output_aliases={4: 0},
    )(parts, moved, drive2, tangent, base)


def body(images):
    pair = lax.axis_size("image") == 2 and lax.axis_size("yslab") == 2 and images.shape[0] == 2
    return body_pair(images) if pair else body_any(images)


def solution(mesh):
    in_specs = (P(("groups", "image"), "space", "yslab", None),)
    out_specs = (P(("groups", "image"), "space", "yslab", None), P(("groups", "image")))
    return jax.shard_map(body, mesh=mesh, in_specs=in_specs, out_specs=out_specs, check_vma=False)
```

```python
import functools
import math

import jax
import jax.numpy as jnp
from jax import lax
from jax.experimental import pallas as pl
from jax.experimental.pallas import tpu as pltpu
from jax.sharding import PartitionSpec as P

ITERS = 2


GRADIENT_COEF = 1.0
MOBILITY = 0.004
SPRING_K = 1.0
STEP_SIZE = 0.5
EPSILON = 1e-06

PAD = 8
VMEM_ROOM = 2 * 2**20
UNROLL = 4


def passed_along(array, axis, by):
    peers = lax.axis_size(axis)
    pairs = [(i, i + by) for i in range(peers) if 0 <= i + by < peers]
    return lax.ppermute(array, axis, pairs)


def extended(cells, sides, width):
    for axis, dim in sides:
        count = lax.axis_size(axis)
        head = lax.slice_in_dim(cells, 0, width, axis=dim)
        tail = lax.slice_in_dim(cells, cells.shape[dim] - width, cells.shape[dim], axis=dim)
        cells = jnp.concatenate(
            [
                lax.ppermute(tail, axis, [(i, (i + 1) % count) for i in range(count)]),
                cells,
                lax.ppermute(head, axis, [((i + 1) % count, i) for i in range(count)]),
            ],
            axis=dim,
        )
    return cells


def stencil(padded):
    middle = padded[:, 1:-1, 1:-1]
    neighbours = padded[:, 2:, 1:-1] + padded[:, :-2, 1:-1]
    neighbours = neighbours + padded[:, 1:-1, 2:] + padded[:, 1:-1, :-2]
    neighbours = neighbours + jnp.roll(middle, -1, 3) + jnp.roll(middle, 1, 3)
    return neighbours - 6.0 * middle


def sum_cells(field):
    return jnp.sum(field, axis=(1, 2, 3))


def body_any(images):
    current = images
    per_device = current.shape[0]
    total_images = per_device * lax.axis_size("image")
    cell_total = float(
        current.shape[1]
        * lax.axis_size("space")
        * current.shape[2]
        * lax.axis_size("yslab")
        * current.shape[3]
    )
    image_ids = lax.axis_index("image") * per_device + jnp.arange(per_device, dtype=jnp.int32)
    interior = (image_ids > 0) & (image_ids < total_images - 1)
    parallel = jnp.zeros((per_device,), jnp.float32)
    for iteration in range(ITERS):
        next_first = passed_along(current[0], "image", -1)
        prev_last = passed_along(current[-1], "image", 1)
        ahead = jnp.concatenate([current[1:], next_first[None]], 0)
        behind = jnp.concatenate([prev_last[None], current[:-1]], 0)
        forward = ahead - current
        backward = current - behind
        tangent = forward + backward
        plus_sq, minus_sq, tangent_sq = lax.psum(
            (
                sum_cells(forward * forward),
                sum_cells(backward * backward),
                sum_cells(tangent * tangent),
            ),
            ("space", "yslab"),
        )
        wide_pad = extended(current, (("space", 1), ("yslab", 2)), 2)
        inner_field = wide_pad[:, 1:-1, 1:-1]
        potential = (
            inner_field * inner_field * inner_field
            - inner_field
            - GRADIENT_COEF * stencil(wide_pad)
        )
        driving = MOBILITY * stencil(potential)
        parallel_sum = lax.psum(sum_cells(driving * tangent), ("space", "yslab"))
        project_coef = parallel_sum / (tangent_sq + EPSILON)
        spring = (
            SPRING_K * (jnp.sqrt(plus_sq) - jnp.sqrt(minus_sq)) / jnp.sqrt(tangent_sq + EPSILON)
        )
        update = (
            driving
            - project_coef[:, None, None, None] * tangent
            + spring[:, None, None, None] * tangent
        )
        current = jnp.where(interior[:, None, None, None], current + STEP_SIZE * update, current)
        parallel = jnp.where(
            interior, parallel_sum / jnp.sqrt((tangent_sq + EPSILON) * cell_total), jnp.float32(0.0)
        )
    return (current, parallel)


def call(kernel, out_shape, scratch=(), name=None, **kw):
    return pl.pallas_call(
        kernel,
        out_shape=out_shape,
        scratch_shapes=list(scratch),
        name=name,
        compiler_params=pltpu.CompilerParams(
            vmem_limit_bytes=VMEM_ROOM + sum(4 * math.prod(s.shape) for s in scratch if s is not DMA)
        ),
        **kw,
    )


def shape(*dims):
    return jax.ShapeDtypeStruct(dims, jnp.float32)


def lap(below, here, above):
    rows, lanes = here.shape
    ys = pltpu.roll(here, 1, 0) + pltpu.roll(here, rows - 1, 0)
    xs = pltpu.roll(here, 1, 1) + pltpu.roll(here, lanes - 1, 1)
    return (below + above) + ys + xs - 6.0 * here


def layer_loop(start, stop, body):
    def step(k, carry):
        body(k)
        return carry

    lax.fori_loop(start, stop, step, 0, unroll=min(UNROLL, stop - start))


def potentials(field, pot, count):
    def one(k):
        here = field[k + 1]
        pot[k] = here * here * here - here - GRADIENT_COEF * lap(field[k], here, field[k + 2])

    layer_loop(0, count, one)


def driving(pot, k):
    return MOBILITY * lap(pot[k], pot[k + 1], pot[k + 2])


def rows_sum(field):
    rows, lanes = field.shape
    return jnp.sum(field.reshape(rows // 8, 8, lanes), axis=0)


def lane_row(total):
    lanes = total.shape[1]
    folded = jnp.sum(total.reshape(8, lanes // 128, 128), axis=1)
    return jnp.sum(folded, axis=0, keepdims=True)


def fill_padded(dst, low, mid, high, sides, sides_at):
    rows = mid.shape[1]
    n_low, n_mid, n_high = low.shape[0], mid.shape[0], high.shape[0]
    dst[0:n_low, PAD : PAD + rows] = low[...]
    dst[n_low : n_low + n_mid, PAD : PAD + rows] = mid[...]
    dst[n_low + n_mid : n_low + n_mid + n_high, PAD : PAD + rows] = high[...]
    layers = n_low + n_mid + n_high
    dst[:, 0:PAD] = sides[sides_at : sides_at + layers, PAD : 2 * PAD]
    dst[:, PAD + rows : 2 * PAD + rows] = sides[sides_at : sides_at + layers, 0:PAD]


def split_kernel(images, mine, end, up, down, sems):
    which = 1 - lax.axis_index("image")
    nz = mine.shape[0]
    copies = [
        pltpu.make_async_copy(src, dst, sems.at[i])
        for i, (src, dst) in enumerate(
            [
                (images.at[which], mine),
                (images.at[which, pl.ds(nz - 4, 4)], up.at[pl.ds(0, 4)]),
                (images.at[1 - which, pl.ds(nz - 2, 2)], up.at[pl.ds(4, 2)]),
                (images.at[which, pl.ds(0, 4)], down.at[pl.ds(0, 4)]),
                (images.at[1 - which, pl.ds(0, 2)], down.at[pl.ds(4, 2)]),
                (images.at[1 - which], end),
            ]
        )
    ]
    for c in copies:
        c.start()
    for c in copies:
        c.wait()


def first_step_kernel(mine, end, low, high, sides, step_out, drive_out, end_out, field, pot):
    nz, rows, _ = mine.shape
    fill_padded(field, low.at[0:4], mine, high.at[0:4], sides, 0)
    fill_padded(end_out, low.at[4:6], end, high.at[4:6], sides, nz + 8)

    potentials(field, pot, nz + 6)

    def edge(k):
        step_out[k] = field[k + 2] + STEP_SIZE * driving(pot, k)

    def inner(k):
        drive = driving(pot, k)
        step_out[k] = field[k + 2] + STEP_SIZE * drive
        drive_out[k - 2] = drive[PAD : PAD + rows]

    layer_loop(0, 2, edge)
    layer_loop(2, nz + 2, inner)
    layer_loop(nz + 2, nz + 4, edge)


def sums_of(count, lanes, fields):
    def one(k, totals):
        plus, minus, tangent, drive = fields(k)
        terms = (plus * plus, minus * minus, tangent * tangent, drive * tangent)
        return tuple(t + rows_sum(v) for t, v in zip(totals, terms))

    zero = jnp.zeros((8, lanes), jnp.float32)
    return lax.fori_loop(0, count, one, (zero,) * 4, unroll=UNROLL)


def write_sums(out, totals):
    table = jnp.concatenate([lane_row(t) for t in totals] + [jnp.zeros((4, 128), jnp.float32)], 0)
    for peer in range(out.shape[0]):
        out[peer] = table


def first_sums_kernel(other, mine, end, drive, out):
    nz, _, lanes = mine.shape

    def fields(k):
        m, o, e = mine[k], other[k], end[k]
        return o - m, m - e, o - e, drive[k]

    write_sums(out, sums_of(nz, lanes, fields))


def coefficient(parts, base, count):
    total = parts[base]
    for i in range(1, count):
        total = total + parts[base + i]
    total = jnp.sum(total, axis=1, keepdims=True)
    plus_sq, minus_sq, tangent_sq, par = (total[i : i + 1] for i in range(4))
    safe = tangent_sq + EPSILON
    spring = SPRING_K * (jnp.sqrt(plus_sq) - jnp.sqrt(minus_sq)) / jnp.sqrt(safe)
    return STEP_SIZE * (spring - par / safe), par, safe


def other_step_kernel(other, low, high, sides, step_out, field_out, pot):
    nz, rows, _ = other.shape
    fill_padded(field_out, low, other, high, sides, 0)

    potentials(field_out, pot, nz + 2)

    def one(k):
        step_out[k] = other[k] + STEP_SIZE * driving(pot, k)[PAD : PAD + rows]

    layer_loop(0, nz, one)


def second_step_kernel(parts, step, end_wide, other_wide, moved_out, drive_out, field, pot):
    nz, rows, _ = drive_out.shape
    half = parts.shape[0] // 2
    coef, _, _ = coefficient(parts, half * lax.axis_index("image"), half)

    def move(k):
        field[k] = step[k] + coef * (other_wide[k] - end_wide[k])

    layer_loop(0, nz + 4, move)
    potentials(field, pot, nz + 2)

    def one(k):
        drive_out[k] = driving(pot, k)[PAD : PAD + rows]
        moved_out[k] = field[k + 2][PAD : PAD + rows]

    layer_loop(0, nz, one)


def second_sums_kernel(parts, far, mine, end, other_step, moved, drive, tangent_out, out):
    nz, _, lanes = mine.shape
    half = parts.shape[0] // 2
    coef, _, _ = coefficient(parts, half * (1 - lax.axis_index("image")), half)

    def fields(k):
        o = other_step[k] + coef * (mine[k] - far[k])
        m, e = moved[k], end[k]
        tangent = o - e
        tangent_out[k] = tangent
        return o - m, m - e, tangent, drive[k]

    write_sums(out, sums_of(nz, lanes, fields))


def last_kernel(cells, parts, moved, drive, tangent, base, out, par_out, buf, sems):
    del base
    nz = moved.shape[0]
    at = lax.axis_index("image")
    which = 1 - at
    coef, par, safe = coefficient(parts, 0, parts.shape[0])
    copies = []
    for k in range(nz):
        buf[k] = moved[k] + STEP_SIZE * drive[k] + coef * tangent[k]
        if k % 4 == 3:
            where = pl.ds(k - 3, 4)
            copies.append(
                pltpu.make_async_copy(buf.at[where], out.at[which, where], sems.at[k // 4])
            )
            copies[-1].start()
    value = (par / jnp.sqrt(safe * cells))[0, 0]
    sign = jnp.where(at == 0, 1.0, -1.0).astype(jnp.float32)
    par_out[which] = value * sign
    par_out[1 - which] = jnp.float32(0.0)
    for c in copies:
        c.wait()


ANY = pl.BlockSpec(memory_space=pl.ANY)
VMEM = pl.BlockSpec(memory_space=pltpu.VMEM)
SMEM = pl.BlockSpec(memory_space=pltpu.SMEM)
DMA = pltpu.SemaphoreType.DMA
SWAP = [(0, 1), (1, 0)]


def copy_kernel(src, dst, sem):
    c = pltpu.make_async_copy(src, dst, sem)
    c.start()
    c.wait()


def from_z(up, down):
    count = lax.axis_size("space")
    low = lax.ppermute(up, "space", [(i, (i + 1) % count) for i in range(count)])
    high = lax.ppermute(down, "space", [((i + 1) % count, i) for i in range(count)])
    return low, high


def y_sides(*pieces):
    rows = pieces[0].shape[1]
    ends = [jnp.concatenate([p[:, :PAD], p[:, rows - PAD :]], 1) for p in pieces]
    return lax.ppermute(jnp.concatenate(ends, 0), "yslab", SWAP)


def to_all(sums, axes):
    return lax.all_to_all(sums, axes, 0, 0, tiled=True)


def body_pair(images):
    _, nz, ny, nx = images.shape
    wide = ny + 2 * PAD
    cells = float(nz * lax.axis_size("space") * ny * lax.axis_size("yslab") * nx)
    block = shape(nz, ny, nx)

    mine, end, up, down = call(
        split_kernel,
        [block, block, shape(6, ny, nx), shape(6, ny, nx)],
        [DMA((6,))],
        "split",
        in_specs=[ANY],
        out_specs=[ANY] * 4,
    )(images)

    other = lax.ppermute(mine, "image", SWAP)
    low, high = from_z(up, down)
    end_later, low, high = lax.optimization_barrier((end, low, high))
    far = lax.ppermute(end_later, "image", SWAP)

    base = call(
        copy_kernel,
        jax.ShapeDtypeStruct(images.shape, images.dtype),
        [DMA],
        "base",
        in_specs=[ANY],
        out_specs=ANY,
    )(images)

    sides = y_sides(low[:4], mine, high[:4], low[4:], end, high[4:])
    step, drive, end_wide = call(
        first_step_kernel,
        [shape(nz + 4, wide, nx), block, shape(nz + 4, wide, nx)],
        [pltpu.VMEM((nz + 8, wide, nx), jnp.float32), pltpu.VMEM((nz + 6, wide, nx), jnp.float32)],
        "first_step",
    )(mine, end, low, high, sides)

    everyone = ("image", "space", "yslab")
    partners = ("space", "yslab")
    other, drive = lax.optimization_barrier((other, drive))
    o_low, o_high = from_z(other[nz - 2 :], other[:2])
    sums = call(first_sums_kernel, shape(lax.axis_size(everyone), 8, 128), name="first_sums")(
        other, mine, end, drive
    )
    parts = to_all(sums, everyone)

    o_sides = y_sides(o_low, other, o_high)
    other_step, other_wide = call(
        other_step_kernel,
        [block, shape(nz + 4, wide, nx)],
        [pltpu.VMEM((nz + 2, wide, nx), jnp.float32)],
        "other_step",
    )(other, o_low, o_high, o_sides)

    moved, drive2 = call(
        second_step_kernel,
        [block, block],
        [pltpu.VMEM((nz + 4, wide, nx), jnp.float32), pltpu.VMEM((nz + 2, wide, nx), jnp.float32)],
        "second_step",
    )(parts, step, end_wide, other_wide)

    tangent, sums = call(
        second_sums_kernel, [block, shape(lax.axis_size(partners), 8, 128)], name="second_sums"
    )(parts, far, mine, end, other_step, moved, drive2)
    parts = to_all(sums, partners)

    return call(
        functools.partial(last_kernel, cells),
        [jax.ShapeDtypeStruct(images.shape, images.dtype), shape(2)],
        [pltpu.VMEM(block.shape, jnp.float32), DMA((nz // 4,))],
        "last",
        in_specs=[VMEM] * 4 + [ANY],
        out_specs=[ANY, SMEM],
        input_output_aliases={4: 0},
    )(parts, moved, drive2, tangent, base)


def body(images):
    pair = lax.axis_size("image") == 2 and lax.axis_size("yslab") == 2 and images.shape[0] == 2
    return body_pair(images) if pair else body_any(images)


def solution(mesh):
    in_specs = (P(("groups", "image"), "space", "yslab", None),)
    out_specs = (P(("groups", "image"), "space", "yslab", None), P(("groups", "image")))
    return jax.shard_map(body, mesh=mesh, in_specs=in_specs, out_specs=out_specs, check_vma=False)
```

```python
import functools
import math

import jax
import jax.numpy as jnp
from jax import lax
from jax.experimental import pallas as pl
from jax.experimental.pallas import tpu as pltpu
from jax.sharding import PartitionSpec as P

ITERS = 2


GRADIENT_COEF = 1.0
MOBILITY = 0.004
SPRING_K = 1.0
STEP_SIZE = 0.5
EPSILON = 1e-06

PAD = 8
VMEM_ROOM = 2 * 2**20
UNROLL = 4


def passed_along(array, axis, by):
    peers = lax.axis_size(axis)
    pairs = [(i, i + by) for i in range(peers) if 0 <= i + by < peers]
    return lax.ppermute(array, axis, pairs)


def extended(cells, sides, width):
    for axis, dim in sides:
        count = lax.axis_size(axis)
        head = lax.slice_in_dim(cells, 0, width, axis=dim)
        tail = lax.slice_in_dim(cells, cells.shape[dim] - width, cells.shape[dim], axis=dim)
        cells = jnp.concatenate(
            [
                lax.ppermute(tail, axis, [(i, (i + 1) % count) for i in range(count)]),
                cells,
                lax.ppermute(head, axis, [((i + 1) % count, i) for i in range(count)]),
            ],
            axis=dim,
        )
    return cells


def stencil(padded):
    middle = padded[:, 1:-1, 1:-1]
    neighbours = padded[:, 2:, 1:-1] + padded[:, :-2, 1:-1]
    neighbours = neighbours + padded[:, 1:-1, 2:] + padded[:, 1:-1, :-2]
    neighbours = neighbours + jnp.roll(middle, -1, 3) + jnp.roll(middle, 1, 3)
    return neighbours - 6.0 * middle


def sum_cells(field):
    return jnp.sum(field, axis=(1, 2, 3))


def body_any(images):
    current = images
    per_device = current.shape[0]
    total_images = per_device * lax.axis_size("image")
    cell_total = float(
        current.shape[1]
        * lax.axis_size("space")
        * current.shape[2]
        * lax.axis_size("yslab")
        * current.shape[3]
    )
    image_ids = lax.axis_index("image") * per_device + jnp.arange(per_device, dtype=jnp.int32)
    interior = (image_ids > 0) & (image_ids < total_images - 1)
    parallel = jnp.zeros((per_device,), jnp.float32)
    for iteration in range(ITERS):
        next_first = passed_along(current[0], "image", -1)
        prev_last = passed_along(current[-1], "image", 1)
        ahead = jnp.concatenate([current[1:], next_first[None]], 0)
        behind = jnp.concatenate([prev_last[None], current[:-1]], 0)
        forward = ahead - current
        backward = current - behind
        tangent = forward + backward
        plus_sq, minus_sq, tangent_sq = lax.psum(
            (
                sum_cells(forward * forward),
                sum_cells(backward * backward),
                sum_cells(tangent * tangent),
            ),
            ("space", "yslab"),
        )
        wide_pad = extended(current, (("space", 1), ("yslab", 2)), 2)
        inner_field = wide_pad[:, 1:-1, 1:-1]
        potential = (
            inner_field * inner_field * inner_field
            - inner_field
            - GRADIENT_COEF * stencil(wide_pad)
        )
        driving = MOBILITY * stencil(potential)
        parallel_sum = lax.psum(sum_cells(driving * tangent), ("space", "yslab"))
        project_coef = parallel_sum / (tangent_sq + EPSILON)
        spring = (
            SPRING_K * (jnp.sqrt(plus_sq) - jnp.sqrt(minus_sq)) / jnp.sqrt(tangent_sq + EPSILON)
        )
        update = (
            driving
            - project_coef[:, None, None, None] * tangent
            + spring[:, None, None, None] * tangent
        )
        current = jnp.where(interior[:, None, None, None], current + STEP_SIZE * update, current)
        parallel = jnp.where(
            interior, parallel_sum / jnp.sqrt((tangent_sq + EPSILON) * cell_total), jnp.float32(0.0)
        )
    return (current, parallel)


def call(kernel, out_shape, scratch=(), name=None, **kw):
    return pl.pallas_call(
        kernel,
        out_shape=out_shape,
        scratch_shapes=list(scratch),
        name=name,
        compiler_params=pltpu.CompilerParams(
            vmem_limit_bytes=VMEM_ROOM + sum(4 * math.prod(s.shape) for s in scratch if s is not DMA)
        ),
        **kw,
    )


def shape(*dims):
    return jax.ShapeDtypeStruct(dims, jnp.float32)


def lap(below, here, above):
    rows, lanes = here.shape
    ys = pltpu.roll(here, 1, 0) + pltpu.roll(here, rows - 1, 0)
    xs = pltpu.roll(here, 1, 1) + pltpu.roll(here, lanes - 1, 1)
    return (below + above) + ys + xs - 6.0 * here


def layer_loop(start, stop, body):
    def step(k, carry):
        body(k)
        return carry

    lax.fori_loop(start, stop, step, 0, unroll=min(UNROLL, stop - start))


def potentials(field, pot, count):
    def one(k):
        here = field[k + 1]
        pot[k] = here * here * here - here - GRADIENT_COEF * lap(field[k], here, field[k + 2])

    layer_loop(0, count, one)


def driving(pot, k):
    return MOBILITY * lap(pot[k], pot[k + 1], pot[k + 2])


def rows_sum(field):
    rows, lanes = field.shape
    return jnp.sum(field.reshape(rows // 8, 8, lanes), axis=0)


def lane_row(total):
    lanes = total.shape[1]
    folded = jnp.sum(total.reshape(8, lanes // 128, 128), axis=1)
    return jnp.sum(folded, axis=0, keepdims=True)


def fill_padded(dst, pieces, sides, sides_at):
    at = 0
    for piece in pieces:
        layers, rows, _ = piece.shape
        dst[at : at + layers, PAD : PAD + rows] = piece[...]
        at += layers
    dst[:, 0:PAD] = sides[sides_at : sides_at + at, PAD : 2 * PAD]
    dst[:, PAD + rows : 2 * PAD + rows] = sides[sides_at : sides_at + at, 0:PAD]


def split_kernel(images, mine, end, edges, middle, up, down, sems):
    which = 1 - lax.axis_index("image")
    nz = mine.shape[0]
    copies = [
        pltpu.make_async_copy(src, dst, sems.at[i])
        for i, (src, dst) in enumerate(
            [
                (images.at[which, pl.ds(0, 2)], edges.at[pl.ds(0, 2)]),
                (images.at[which, pl.ds(nz - 2, 2)], edges.at[pl.ds(2, 2)]),
                (images.at[which, pl.ds(2, nz - 4)], middle),
                (images.at[which, pl.ds(nz - 4, 4)], up),
                (images.at[which, pl.ds(0, 4)], down),
                (images.at[which], mine),
                (images.at[1 - which], end),
            ]
        )
    ]
    for c in copies:
        c.start()
    for c in copies:
        c.wait()


def first_step_kernel(mine, low, high, sides, step_out, drive_out, field, pot):
    nz, rows, _ = mine.shape
    fill_padded(field, (low, mine, high), sides, 0)
    potentials(field, pot, nz + 6)

    def edge(k):
        step_out[k] = field[k + 2] + STEP_SIZE * driving(pot, k)

    def inner(k):
        drive = driving(pot, k)
        step_out[k] = field[k + 2] + STEP_SIZE * drive
        drive_out[k - 2] = drive[PAD : PAD + rows]

    layer_loop(0, 2, edge)
    layer_loop(2, nz + 2, inner)
    layer_loop(nz + 2, nz + 4, edge)


CHUNK = 16


def sums_of(start, stop, rows, fields, totals):
    def one(k, totals):
        for r in range(0, rows, CHUNK):
            plus, minus, tangent, drive = fields(k, pl.ds(r, CHUNK))
            terms = (plus * plus, minus * minus, tangent * tangent, drive * tangent)
            totals = tuple(t + rows_sum(v) for t, v in zip(totals, terms))
        return totals

    return lax.fori_loop(start, stop, one, totals, unroll=min(UNROLL, stop - start))


def no_sums(lanes):
    return (jnp.zeros((8, lanes), jnp.float32),) * 4


def write_sums(out, totals):
    out[...] = jnp.concatenate(
        [lane_row(t) for t in totals] + [jnp.zeros((4, 128), jnp.float32)], 0
    )


def first_sums_kernel(edges, middle, mine, end, drive, out):
    nz, rows, lanes = mine.shape

    def fields_from(other, shift):
        def fields(k, r):
            m, o, e = mine[k, r], other[k + shift, r], end[k, r]
            return o - m, m - e, o - e, drive[k, r]

        return fields

    totals = sums_of(0, 2, rows, fields_from(edges, 0), no_sums(lanes))
    totals = sums_of(2, nz - 2, rows, fields_from(middle, -2), totals)
    totals = sums_of(nz - 2, nz, rows, fields_from(edges, 4 - nz), totals)
    write_sums(out, totals)


def coefficient(sums):
    total = jnp.sum(sums[...], axis=1, keepdims=True)
    plus_sq, minus_sq, tangent_sq, par = (total[i : i + 1] for i in range(4))
    safe = tangent_sq + EPSILON
    spring = SPRING_K * (jnp.sqrt(plus_sq) - jnp.sqrt(minus_sq)) / jnp.sqrt(safe)
    return STEP_SIZE * (spring - par / safe), par, safe


def other_step_kernel(edges, middle, end, low, high, sides, step_out, tangent_out, field, pot):
    nz, rows, _ = end.shape
    first, last = edges.at[0:2], edges.at[2:4]
    fill_padded(field, (low.at[0:2], first, middle, last, high.at[0:2]), sides, 0)
    fill_padded(tangent_out, (low.at[2:4], end, high.at[2:4]), sides, nz + 4)
    potentials(field, pot, nz + 2)

    def widen(k):
        tangent_out[k] = field[k] - tangent_out[k]

    def one(k):
        moved = field[k + 2] + STEP_SIZE * driving(pot, k)
        step_out[k] = moved[PAD : PAD + rows]

    layer_loop(0, nz + 4, widen)
    layer_loop(0, nz, one)


def second_step_kernel(sums, step, tangent_wide, moved_out, drive_out, field, pot):
    nz, rows, _ = drive_out.shape
    coef, _, _ = coefficient(sums)

    def move(k):
        field[k] = step[k] + coef * tangent_wide[k]

    layer_loop(0, nz + 4, move)
    potentials(field, pot, nz + 2)

    def one(k):
        drive = driving(pot, k)[PAD : PAD + rows]
        drive_out[k] = drive
        moved_out[k] = field[k + 2][PAD : PAD + rows]

    layer_loop(0, nz, one)


def second_sums_kernel(sums, far, mine, end, other_step, moved, drive, tangent_out, out):
    nz, rows, lanes = mine.shape
    coef, _, _ = coefficient(sums)

    def fields(k, r):
        o = other_step[k, r] + coef * (mine[k, r] - far[k, r])
        m, e = moved[k, r], end[k, r]
        tangent = o - e
        tangent_out[k, r] = tangent
        return o - m, m - e, tangent, drive[k, r]

    write_sums(out, sums_of(0, nz, rows, fields, no_sums(lanes)))


def last_kernel(cells, sums, moved, drive, tangent, base, out, par_out, buf, sems):
    del base
    nz = moved.shape[0]
    at = lax.axis_index("image")
    which = 1 - at
    coef, par, safe = coefficient(sums)
    copies = []
    for k in range(nz):
        buf[k] = moved[k] + STEP_SIZE * drive[k] + coef * tangent[k]
        if k % 4 == 3:
            where = pl.ds(k - 3, 4)
            copies.append(
                pltpu.make_async_copy(buf.at[where], out.at[which, where], sems.at[k // 4])
            )
            copies[-1].start()
    value = (par / jnp.sqrt(safe * cells))[0, 0]
    sign = jnp.where(at == 0, 1.0, -1.0).astype(jnp.float32)
    par_out[which] = value * sign
    par_out[1 - which] = jnp.float32(0.0)
    for c in copies:
        c.wait()


ANY = pl.BlockSpec(memory_space=pl.ANY)
VMEM = pl.BlockSpec(memory_space=pltpu.VMEM)
SMEM = pl.BlockSpec(memory_space=pltpu.SMEM)
DMA = pltpu.SemaphoreType.DMA
SWAP = [(0, 1), (1, 0)]


def copy_kernel(src, dst, sem):
    c = pltpu.make_async_copy(src, dst, sem)
    c.start()
    c.wait()


def from_z(up, down):
    count = lax.axis_size("space")
    low = lax.ppermute(up, "space", [(i, (i + 1) % count) for i in range(count)])
    high = lax.ppermute(down, "space", [((i + 1) % count, i) for i in range(count)])
    return low, high


def y_sides(*pieces):
    rows = pieces[0].shape[1]
    ends = [jnp.concatenate([p[:, :PAD], p[:, rows - PAD :]], 1) for p in pieces]
    return lax.ppermute(jnp.concatenate(ends, 0), "yslab", SWAP)


def summed(sums):
    sums = sums + lax.ppermute(sums, "yslab", SWAP)
    count, stride = lax.axis_size("space"), 1
    while stride < count:
        sums = sums + lax.ppermute(sums, "space", [(i, i ^ stride) for i in range(count)])
        stride *= 2
    return sums


def body_pair(images):
    _, nz, ny, nx = images.shape
    wide = ny + 2 * PAD
    cells = float(nz * lax.axis_size("space") * ny * lax.axis_size("yslab") * nx)
    block, outer = shape(nz, ny, nx), shape(nz + 4, wide, nx)
    table = shape(8, 128)

    def room(layers):
        return pltpu.VMEM((layers, wide, nx), jnp.float32)

    mine, end, edges, middle, up, down = call(
        split_kernel,
        [block, block, shape(4, ny, nx), shape(nz - 4, ny, nx), shape(4, ny, nx), shape(4, ny, nx)],
        [DMA((7,))],
        "split",
        in_specs=[ANY],
        out_specs=[ANY] * 6,
    )(images)

    o_edges = lax.ppermute(edges, "image", SWAP)
    o_middle = lax.ppermute(middle, "image", SWAP)

    low, high = from_z(up, down)
    sides = y_sides(low, mine, high)
    step, drive = call(first_step_kernel, [outer, block], [room(nz + 8), room(nz + 6)], "first_step")(
        mine, low, high, sides
    )

    end_later, drive = lax.optimization_barrier((end, drive))
    far = lax.ppermute(end_later, "image", SWAP)

    o_low, o_high = from_z(
        jnp.concatenate([o_edges[2:], end[nz - 2 :]]), jnp.concatenate([o_edges[:2], end[:2]])
    )
    o_sides = y_sides(o_low[:2], o_edges[:2], o_middle, o_edges[2:], o_high[:2], o_low[2:], end, o_high[2:])

    base = call(
        copy_kernel,
        jax.ShapeDtypeStruct(images.shape, images.dtype),
        [DMA],
        "base",
        in_specs=[ANY],
        out_specs=ANY,
    )(images)

    sums = summed(call(first_sums_kernel, table, name="first_sums")(o_edges, o_middle, mine, end, drive))
    other_step, tangent_wide = call(
        other_step_kernel, [block, outer], [room(nz + 4), room(nz + 2)], "other_step"
    )(o_edges, o_middle, end, o_low, o_high, o_sides)

    moved, drive2 = call(
        second_step_kernel, [block, block], [room(nz + 4), room(nz + 2)], "second_step"
    )(sums, step, tangent_wide)

    o_sums = lax.ppermute(sums, "image", SWAP)
    tangent, sums = call(second_sums_kernel, [block, table], name="second_sums")(
        o_sums, far, mine, end, other_step, moved, drive2
    )

    return call(
        functools.partial(last_kernel, cells),
        [jax.ShapeDtypeStruct(images.shape, images.dtype), shape(2)],
        [pltpu.VMEM(block.shape, jnp.float32), DMA((nz // 4,))],
        "last",
        in_specs=[VMEM] * 4 + [ANY],
        out_specs=[ANY, SMEM],
        input_output_aliases={4: 0},
    )(summed(sums), moved, drive2, tangent, base)


def body(images):
    layers = lax.axis_size("space")
    pair = lax.axis_size("image") == 2 and lax.axis_size("yslab") == 2 and images.shape[0] == 2
    pair = pair and layers & (layers - 1) == 0
    return body_pair(images) if pair else body_any(images)


def solution(mesh):
    in_specs = (P(("groups", "image"), "space", "yslab", None),)
    out_specs = (P(("groups", "image"), "space", "yslab", None), P(("groups", "image")))
    return jax.shard_map(body, mesh=mesh, in_specs=in_specs, out_specs=out_specs, check_vma=False)
```

```python
import functools
import math

import jax
import jax.numpy as jnp
from jax import lax
from jax.experimental import pallas as pl
from jax.experimental.pallas import tpu as pltpu
from jax.sharding import PartitionSpec as P

ITERS = 2


GRADIENT_COEF = 1.0
MOBILITY = 0.004
SPRING_K = 1.0
STEP_SIZE = 0.5
EPSILON = 1e-06

PAD = 8
VMEM_ROOM = 2 * 2**20
UNROLL = 4


def passed_along(array, axis, by):
    peers = lax.axis_size(axis)
    pairs = [(i, i + by) for i in range(peers) if 0 <= i + by < peers]
    return lax.ppermute(array, axis, pairs)


def extended(cells, sides, width):
    for axis, dim in sides:
        count = lax.axis_size(axis)
        head = lax.slice_in_dim(cells, 0, width, axis=dim)
        tail = lax.slice_in_dim(cells, cells.shape[dim] - width, cells.shape[dim], axis=dim)
        cells = jnp.concatenate(
            [
                lax.ppermute(tail, axis, [(i, (i + 1) % count) for i in range(count)]),
                cells,
                lax.ppermute(head, axis, [((i + 1) % count, i) for i in range(count)]),
            ],
            axis=dim,
        )
    return cells


def stencil(padded):
    middle = padded[:, 1:-1, 1:-1]
    neighbours = padded[:, 2:, 1:-1] + padded[:, :-2, 1:-1]
    neighbours = neighbours + padded[:, 1:-1, 2:] + padded[:, 1:-1, :-2]
    neighbours = neighbours + jnp.roll(middle, -1, 3) + jnp.roll(middle, 1, 3)
    return neighbours - 6.0 * middle


def sum_cells(field):
    return jnp.sum(field, axis=(1, 2, 3))


def body_any(images):
    current = images
    per_device = current.shape[0]
    total_images = per_device * lax.axis_size("image")
    cell_total = float(
        current.shape[1]
        * lax.axis_size("space")
        * current.shape[2]
        * lax.axis_size("yslab")
        * current.shape[3]
    )
    image_ids = lax.axis_index("image") * per_device + jnp.arange(per_device, dtype=jnp.int32)
    interior = (image_ids > 0) & (image_ids < total_images - 1)
    parallel = jnp.zeros((per_device,), jnp.float32)
    for iteration in range(ITERS):
        next_first = passed_along(current[0], "image", -1)
        prev_last = passed_along(current[-1], "image", 1)
        ahead = jnp.concatenate([current[1:], next_first[None]], 0)
        behind = jnp.concatenate([prev_last[None], current[:-1]], 0)
        forward = ahead - current
        backward = current - behind
        tangent = forward + backward
        plus_sq, minus_sq, tangent_sq = lax.psum(
            (
                sum_cells(forward * forward),
                sum_cells(backward * backward),
                sum_cells(tangent * tangent),
            ),
            ("space", "yslab"),
        )
        wide_pad = extended(current, (("space", 1), ("yslab", 2)), 2)
        inner_field = wide_pad[:, 1:-1, 1:-1]
        potential = (
            inner_field * inner_field * inner_field
            - inner_field
            - GRADIENT_COEF * stencil(wide_pad)
        )
        driving = MOBILITY * stencil(potential)
        parallel_sum = lax.psum(sum_cells(driving * tangent), ("space", "yslab"))
        project_coef = parallel_sum / (tangent_sq + EPSILON)
        spring = (
            SPRING_K * (jnp.sqrt(plus_sq) - jnp.sqrt(minus_sq)) / jnp.sqrt(tangent_sq + EPSILON)
        )
        update = (
            driving
            - project_coef[:, None, None, None] * tangent
            + spring[:, None, None, None] * tangent
        )
        current = jnp.where(interior[:, None, None, None], current + STEP_SIZE * update, current)
        parallel = jnp.where(
            interior, parallel_sum / jnp.sqrt((tangent_sq + EPSILON) * cell_total), jnp.float32(0.0)
        )
    return (current, parallel)


def call(kernel, out_shape, scratch=(), name=None, **kw):
    return pl.pallas_call(
        kernel,
        out_shape=out_shape,
        scratch_shapes=list(scratch),
        name=name,
        compiler_params=pltpu.CompilerParams(
            vmem_limit_bytes=VMEM_ROOM + sum(4 * math.prod(s.shape) for s in scratch if s is not DMA)
        ),
        **kw,
    )


def shape(*dims):
    return jax.ShapeDtypeStruct(dims, jnp.float32)


def lap(below, here, above):
    rows, lanes = here.shape
    ys = pltpu.roll(here, 1, 0) + pltpu.roll(here, rows - 1, 0)
    xs = pltpu.roll(here, 1, 1) + pltpu.roll(here, lanes - 1, 1)
    return (below + above) + ys + xs - 6.0 * here


def layer_loop(start, stop, body):
    def step(k, carry):
        body(k)
        return carry

    lax.fori_loop(start, stop, step, 0, unroll=min(UNROLL, stop - start))


def potentials(field, pot, count):
    def one(k):
        here = field[k + 1]
        pot[k] = here * here * here - here - GRADIENT_COEF * lap(field[k], here, field[k + 2])

    layer_loop(0, count, one)


def driving(pot, k):
    return MOBILITY * lap(pot[k], pot[k + 1], pot[k + 2])


def rows_sum(field):
    rows, lanes = field.shape
    return jnp.sum(field.reshape(rows // 8, 8, lanes), axis=0)


def lane_row(total):
    lanes = total.shape[1]
    folded = jnp.sum(total.reshape(8, lanes // 128, 128), axis=1)
    return jnp.sum(folded, axis=0, keepdims=True)


def fill_padded(dst, pieces, sides, sides_at):
    at = 0
    for piece in pieces:
        layers, rows, _ = piece.shape
        dst[at : at + layers, PAD : PAD + rows] = piece[...]
        at += layers
    dst[:, 0:PAD] = sides[sides_at : sides_at + at, PAD : 2 * PAD]
    dst[:, PAD + rows : 2 * PAD + rows] = sides[sides_at : sides_at + at, 0:PAD]


def split_kernel(images, mine, end, edges, middle, sems):
    which = 1 - lax.axis_index("image")
    nz = mine.shape[0]
    copies = [
        pltpu.make_async_copy(src, dst, sems.at[i])
        for i, (src, dst) in enumerate(
            [
                (images.at[which, pl.ds(0, 2)], edges.at[pl.ds(0, 2)]),
                (images.at[which, pl.ds(nz - 2, 2)], edges.at[pl.ds(2, 2)]),
                (images.at[which, pl.ds(2, nz - 4)], middle),
                (images.at[which], mine),
                (images.at[1 - which], end),
            ]
        )
    ]
    for c in copies:
        c.start()
    for c in copies:
        c.wait()


def ends_kernel(mine, up, down, sems):
    layers = up.shape[0]
    last = pltpu.make_async_copy(mine.at[pl.ds(mine.shape[0] - layers, layers)], up, sems.at[0])
    first = pltpu.make_async_copy(mine.at[pl.ds(0, layers)], down, sems.at[1])
    last.start()
    first.start()
    last.wait()
    first.wait()


def first_step_kernel(mine, low, high, sides, step_out, drive_out, field, pot):
    nz, rows, _ = mine.shape
    fill_padded(field, (low, mine, high), sides, 0)
    potentials(field, pot, nz + 6)

    def edge(k):
        step_out[k] = field[k + 2] + STEP_SIZE * driving(pot, k)

    def inner(k):
        drive = driving(pot, k)
        step_out[k] = field[k + 2] + STEP_SIZE * drive
        drive_out[k - 2] = drive[PAD : PAD + rows]

    layer_loop(0, 2, edge)
    layer_loop(2, nz + 2, inner)
    layer_loop(nz + 2, nz + 4, edge)


CHUNK = 16


def sums_of(start, stop, rows, fields, totals):
    def one(k, totals):
        for r in range(0, rows, CHUNK):
            plus, minus, tangent, drive = fields(k, pl.ds(r, CHUNK))
            terms = (plus * plus, minus * minus, tangent * tangent, drive * tangent)
            totals = tuple(t + rows_sum(v) for t, v in zip(totals, terms))
        return totals

    return lax.fori_loop(start, stop, one, totals, unroll=min(UNROLL, stop - start))


def no_sums(lanes):
    return (jnp.zeros((8, lanes), jnp.float32),) * 4


def write_sums(out, totals):
    out[...] = jnp.concatenate(
        [lane_row(t) for t in totals] + [jnp.zeros((4, 128), jnp.float32)], 0
    )


def first_sums_kernel(edges, middle, mine, end, drive, out):
    nz, rows, lanes = mine.shape

    def fields_from(other, shift):
        def fields(k, r):
            m, o, e = mine[k, r], other[k + shift, r], end[k, r]
            return o - m, m - e, o - e, drive[k, r]

        return fields

    totals = sums_of(0, 2, rows, fields_from(edges, 0), no_sums(lanes))
    totals = sums_of(2, nz - 2, rows, fields_from(middle, -2), totals)
    totals = sums_of(nz - 2, nz, rows, fields_from(edges, 4 - nz), totals)
    write_sums(out, totals)


def coefficient(sums):
    total = jnp.sum(sums[...], axis=1, keepdims=True)
    plus_sq, minus_sq, tangent_sq, par = (total[i : i + 1] for i in range(4))
    safe = tangent_sq + EPSILON
    spring = SPRING_K * (jnp.sqrt(plus_sq) - jnp.sqrt(minus_sq)) / jnp.sqrt(safe)
    return STEP_SIZE * (spring - par / safe), par, safe


def other_step_kernel(edges, middle, end, low, high, sides, step_out, tangent_out, field, pot):
    nz, rows, _ = end.shape
    first, last = edges.at[0:2], edges.at[2:4]
    fill_padded(field, (low.at[0:2], first, middle, last, high.at[0:2]), sides, 0)
    fill_padded(tangent_out, (low.at[2:4], end, high.at[2:4]), sides, nz + 4)
    potentials(field, pot, nz + 2)

    def widen(k):
        tangent_out[k] = field[k] - tangent_out[k]

    def one(k):
        moved = field[k + 2] + STEP_SIZE * driving(pot, k)
        step_out[k] = moved[PAD : PAD + rows]

    layer_loop(0, nz + 4, widen)
    layer_loop(0, nz, one)


def second_step_kernel(sums, step, tangent_wide, moved_out, drive_out, field, pot):
    nz, rows, _ = drive_out.shape
    coef, _, _ = coefficient(sums)

    def move(k):
        field[k] = step[k] + coef * tangent_wide[k]

    layer_loop(0, nz + 4, move)
    potentials(field, pot, nz + 2)

    def one(k):
        drive = driving(pot, k)[PAD : PAD + rows]
        drive_out[k] = drive
        moved_out[k] = field[k + 2][PAD : PAD + rows]

    layer_loop(0, nz, one)


def second_sums_kernel(sums, far, mine, end, other_step, moved, drive, out):
    nz, rows, lanes = mine.shape
    coef, _, _ = coefficient(sums)

    def fields(k, r):
        o = other_step[k, r] + coef * (mine[k, r] - far[k, r])
        m, e = moved[k, r], end[k, r]
        return o - m, m - e, o - e, drive[k, r]

    write_sums(out, sums_of(0, nz, rows, fields, no_sums(lanes)))


def last_kernel(
    cells, sums, o_sums, far, mine, end, other_step, moved, drive, base, out, par_out, buf, sems
):
    del base
    nz = moved.shape[0]
    at = lax.axis_index("image")
    which = 1 - at
    coef, par, safe = coefficient(sums)
    o_coef, _, _ = coefficient(o_sums)
    copies = []
    for k in range(nz):
        tangent = other_step[k] + o_coef * (mine[k] - far[k]) - end[k]
        buf[k] = moved[k] + STEP_SIZE * drive[k] + coef * tangent
        if k % 4 == 3:
            where = pl.ds(k - 3, 4)
            copies.append(
                pltpu.make_async_copy(buf.at[where], out.at[which, where], sems.at[k // 4])
            )
            copies[-1].start()
    value = (par / jnp.sqrt(safe * cells))[0, 0]
    sign = jnp.where(at == 0, 1.0, -1.0).astype(jnp.float32)
    par_out[which] = value * sign
    par_out[1 - which] = jnp.float32(0.0)
    for c in copies:
        c.wait()


ANY = pl.BlockSpec(memory_space=pl.ANY)
VMEM = pl.BlockSpec(memory_space=pltpu.VMEM)
SMEM = pl.BlockSpec(memory_space=pltpu.SMEM)
DMA = pltpu.SemaphoreType.DMA
SWAP = [(0, 1), (1, 0)]


def copy_kernel(src, dst, sem):
    c = pltpu.make_async_copy(src, dst, sem)
    c.start()
    c.wait()


def from_z(up, down):
    count = lax.axis_size("space")
    low = lax.ppermute(up, "space", [(i, (i + 1) % count) for i in range(count)])
    high = lax.ppermute(down, "space", [((i + 1) % count, i) for i in range(count)])
    return low, high


def y_sides(*pieces):
    rows = pieces[0].shape[1]
    ends = [jnp.concatenate([p[:, :PAD], p[:, rows - PAD :]], 1) for p in pieces]
    return lax.ppermute(jnp.concatenate(ends, 0), "yslab", SWAP)


def summed(sums):
    sums = sums + lax.ppermute(sums, "yslab", SWAP)
    count, stride = lax.axis_size("space"), 1
    while stride < count:
        sums = sums + lax.ppermute(sums, "space", [(i, i ^ stride) for i in range(count)])
        stride *= 2
    return sums


def body_pair(images):
    _, nz, ny, nx = images.shape
    wide = ny + 2 * PAD
    cells = float(nz * lax.axis_size("space") * ny * lax.axis_size("yslab") * nx)
    block, outer = shape(nz, ny, nx), shape(nz + 4, wide, nx)
    table = shape(8, 128)

    def room(layers):
        return pltpu.VMEM((layers, wide, nx), jnp.float32)

    mine, end, edges, middle = call(
        split_kernel,
        [block, block, shape(4, ny, nx), shape(nz - 4, ny, nx)],
        [DMA((5,))],
        "split",
        in_specs=[ANY],
        out_specs=[ANY] * 4,
    )(pltpu.with_memory_space_constraint(images, pltpu.HBM))

    o_edges = lax.ppermute(edges, "image", SWAP)
    o_middle = lax.ppermute(middle, "image", SWAP)

    thin = shape(4, ny, nx)
    up, down = call(
        ends_kernel,
        [thin, thin],
        [DMA((2,))],
        "ends",
        in_specs=[ANY],
        out_specs=[ANY] * 2,
        cost_estimate=pl.CostEstimate(flops=0, bytes_accessed=2**24, transcendentals=0),
    )(mine)
    low, high = from_z(up, down)
    sides = y_sides(low, mine, high)
    step, drive = call(first_step_kernel, [outer, block], [room(nz + 8), room(nz + 6)], "first_step")(
        mine, low, high, sides
    )
    end_later, drive = lax.optimization_barrier((end, drive))
    far = lax.ppermute(end_later, "image", SWAP)

    o_low, o_high = from_z(
        jnp.concatenate([o_edges[2:], end[nz - 2 :]]), jnp.concatenate([o_edges[:2], end[:2]])
    )
    o_low, o_high, o_middle = lax.optimization_barrier((o_low, o_high, o_middle))
    o_sides = y_sides(o_low[:2], o_edges[:2], o_middle, o_edges[2:], o_high[:2], o_low[2:], end, o_high[2:])

    base = call(
        copy_kernel,
        jax.ShapeDtypeStruct(images.shape, images.dtype),
        [DMA],
        "base",
        in_specs=[ANY],
        out_specs=ANY,
    )(images)

    sums = summed(call(first_sums_kernel, table, name="first_sums")(o_edges, o_middle, mine, end, drive))
    other_step, tangent_wide = call(
        other_step_kernel, [block, outer], [room(nz + 4), room(nz + 2)], "other_step"
    )(o_edges, o_middle, end, o_low, o_high, o_sides)

    moved, drive2 = call(
        second_step_kernel, [block, block], [room(nz + 4), room(nz + 2)], "second_step"
    )(sums, step, tangent_wide)

    o_sums = lax.ppermute(sums, "image", SWAP)
    known = (o_sums, far, mine, end, other_step, moved, drive2)
    sums = summed(call(second_sums_kernel, table, name="second_sums")(*known))

    return call(
        functools.partial(last_kernel, cells),
        [jax.ShapeDtypeStruct(images.shape, images.dtype), shape(2)],
        [pltpu.VMEM(block.shape, jnp.float32), DMA((nz // 4,))],
        "last",
        in_specs=[VMEM] * 8 + [ANY],
        out_specs=[ANY, SMEM],
        input_output_aliases={8: 0},
    )(sums, *known, base)


def body(images):
    layers = lax.axis_size("space")
    pair = lax.axis_size("image") == 2 and lax.axis_size("yslab") == 2 and images.shape[0] == 2
    pair = pair and layers & (layers - 1) == 0
    return body_pair(images) if pair else body_any(images)


def solution(mesh):
    in_specs = (P(("groups", "image"), "space", "yslab", None),)
    out_specs = (P(("groups", "image"), "space", "yslab", None), P(("groups", "image")))
    return jax.shard_map(body, mesh=mesh, in_specs=in_specs, out_specs=out_specs, check_vma=False)
```

```python
import functools
import math

import jax
import jax.numpy as jnp
from jax import lax
from jax.experimental import pallas as pl
from jax.experimental.pallas import tpu as pltpu
from jax.sharding import PartitionSpec as P

ITERS = 2


GRADIENT_COEF = 1.0
MOBILITY = 0.004
SPRING_K = 1.0
STEP_SIZE = 0.5
EPSILON = 1e-06

PAD = 8
VMEM_ROOM = 2 * 2**20
UNROLL = 4


def passed_along(array, axis, by):
    peers = lax.axis_size(axis)
    pairs = [(i, i + by) for i in range(peers) if 0 <= i + by < peers]
    return lax.ppermute(array, axis, pairs)


def extended(cells, sides, width):
    for axis, dim in sides:
        count = lax.axis_size(axis)
        head = lax.slice_in_dim(cells, 0, width, axis=dim)
        tail = lax.slice_in_dim(cells, cells.shape[dim] - width, cells.shape[dim], axis=dim)
        cells = jnp.concatenate(
            [
                lax.ppermute(tail, axis, [(i, (i + 1) % count) for i in range(count)]),
                cells,
                lax.ppermute(head, axis, [((i + 1) % count, i) for i in range(count)]),
            ],
            axis=dim,
        )
    return cells


def stencil(padded):
    middle = padded[:, 1:-1, 1:-1]
    neighbours = padded[:, 2:, 1:-1] + padded[:, :-2, 1:-1]
    neighbours = neighbours + padded[:, 1:-1, 2:] + padded[:, 1:-1, :-2]
    neighbours = neighbours + jnp.roll(middle, -1, 3) + jnp.roll(middle, 1, 3)
    return neighbours - 6.0 * middle


def sum_cells(field):
    return jnp.sum(field, axis=(1, 2, 3))


def body_any(images):
    current = images
    per_device = current.shape[0]
    total_images = per_device * lax.axis_size("image")
    cell_total = float(
        current.shape[1]
        * lax.axis_size("space")
        * current.shape[2]
        * lax.axis_size("yslab")
        * current.shape[3]
    )
    image_ids = lax.axis_index("image") * per_device + jnp.arange(per_device, dtype=jnp.int32)
    interior = (image_ids > 0) & (image_ids < total_images - 1)
    parallel = jnp.zeros((per_device,), jnp.float32)
    for iteration in range(ITERS):
        next_first = passed_along(current[0], "image", -1)
        prev_last = passed_along(current[-1], "image", 1)
        ahead = jnp.concatenate([current[1:], next_first[None]], 0)
        behind = jnp.concatenate([prev_last[None], current[:-1]], 0)
        forward = ahead - current
        backward = current - behind
        tangent = forward + backward
        plus_sq, minus_sq, tangent_sq = lax.psum(
            (
                sum_cells(forward * forward),
                sum_cells(backward * backward),
                sum_cells(tangent * tangent),
            ),
            ("space", "yslab"),
        )
        wide_pad = extended(current, (("space", 1), ("yslab", 2)), 2)
        inner_field = wide_pad[:, 1:-1, 1:-1]
        potential = (
            inner_field * inner_field * inner_field
            - inner_field
            - GRADIENT_COEF * stencil(wide_pad)
        )
        driving = MOBILITY * stencil(potential)
        parallel_sum = lax.psum(sum_cells(driving * tangent), ("space", "yslab"))
        project_coef = parallel_sum / (tangent_sq + EPSILON)
        spring = (
            SPRING_K * (jnp.sqrt(plus_sq) - jnp.sqrt(minus_sq)) / jnp.sqrt(tangent_sq + EPSILON)
        )
        update = (
            driving
            - project_coef[:, None, None, None] * tangent
            + spring[:, None, None, None] * tangent
        )
        current = jnp.where(interior[:, None, None, None], current + STEP_SIZE * update, current)
        parallel = jnp.where(
            interior, parallel_sum / jnp.sqrt((tangent_sq + EPSILON) * cell_total), jnp.float32(0.0)
        )
    return (current, parallel)


def call(kernel, out_shape, scratch=(), name=None, **kw):
    return pl.pallas_call(
        kernel,
        out_shape=out_shape,
        scratch_shapes=list(scratch),
        name=name,
        compiler_params=pltpu.CompilerParams(
            vmem_limit_bytes=VMEM_ROOM + sum(4 * math.prod(s.shape) for s in scratch if s is not DMA)
        ),
        **kw,
    )


def shape(*dims):
    return jax.ShapeDtypeStruct(dims, jnp.float32)


def lap(below, here, above):
    rows, lanes = here.shape
    ys = pltpu.roll(here, 1, 0) + pltpu.roll(here, rows - 1, 0)
    xs = pltpu.roll(here, 1, 1) + pltpu.roll(here, lanes - 1, 1)
    return (below + above) + ys + xs - 6.0 * here


def layer_loop(start, stop, body):
    def step(k, carry):
        body(k)
        return carry

    lax.fori_loop(start, stop, step, 0, unroll=min(UNROLL, stop - start))


def potentials(field, pot, count):
    def one(k):
        here = field[k + 1]
        pot[k] = here * here * here - here - GRADIENT_COEF * lap(field[k], here, field[k + 2])

    layer_loop(0, count, one)


def driving(pot, k):
    return MOBILITY * lap(pot[k], pot[k + 1], pot[k + 2])


def rows_sum(field):
    rows, lanes = field.shape
    return jnp.sum(field.reshape(rows // 8, 8, lanes), axis=0)


def lane_row(total):
    lanes = total.shape[1]
    folded = jnp.sum(total.reshape(8, lanes // 128, 128), axis=1)
    return jnp.sum(folded, axis=0, keepdims=True)


def fill_padded(dst, pieces, sides, sides_at):
    at = 0
    for piece in pieces:
        layers, rows, _ = piece.shape
        dst[at : at + layers, PAD : PAD + rows] = piece[...]
        at += layers
    dst[:, 0:PAD] = sides[sides_at : sides_at + at, PAD : 2 * PAD]
    dst[:, PAD + rows : 2 * PAD + rows] = sides[sides_at : sides_at + at, 0:PAD]


def all_copied(pairs, sems):
    copies = [pltpu.make_async_copy(src, dst, sems.at[i]) for i, (src, dst) in enumerate(pairs)]
    for c in copies:
        c.start()
    for c in copies:
        c.wait()


def send_kernel(images, edges, middle, sems):
    which = 1 - lax.axis_index("image")
    nz = images.shape[1]
    pairs = [
        (images.at[which, pl.ds(0, 2)], edges.at[pl.ds(0, 2)]),
        (images.at[which, pl.ds(nz - 2, 2)], edges.at[pl.ds(2, 2)]),
        (images.at[which, pl.ds(2, nz - 4)], middle),
    ]
    all_copied(pairs, sems)


def keep_kernel(images, mine, end, up, down, sems):
    which = 1 - lax.axis_index("image")
    nz, layers = mine.shape[0], up.shape[0]
    pairs = [
        (images.at[which, pl.ds(nz - layers, layers)], up),
        (images.at[which, pl.ds(0, layers)], down),
        (images.at[which], mine),
        (images.at[1 - which], end),
    ]
    all_copied(pairs, sems)


def first_step_kernel(mine, low, high, sides, step_out, drive_out, field, pot):
    nz, rows, _ = mine.shape
    fill_padded(field, (low, mine, high), sides, 0)
    potentials(field, pot, nz + 6)

    def edge(k):
        step_out[k] = field[k + 2] + STEP_SIZE * driving(pot, k)

    def inner(k):
        drive = driving(pot, k)
        step_out[k] = field[k + 2] + STEP_SIZE * drive
        drive_out[k - 2] = drive[PAD : PAD + rows]

    layer_loop(0, 2, edge)
    layer_loop(2, nz + 2, inner)
    layer_loop(nz + 2, nz + 4, edge)


CHUNK = 16


def sums_of(start, stop, rows, terms, totals):
    def one(k, totals):
        for r in range(0, rows, CHUNK):
            totals = tuple(t + rows_sum(v) for t, v in zip(totals, terms(k, pl.ds(r, CHUNK))))
        return totals

    return lax.fori_loop(start, stop, one, totals, unroll=min(UNROLL, stop - start))


def no_sums(count, lanes):
    return (jnp.zeros((8, lanes), jnp.float32),) * count


def table_of(*rows):
    return jnp.concatenate(rows + (jnp.zeros((8 - len(rows), 128), jnp.float32),), 0)


def first_sums_kernel(edges, middle, mine, end, drive, out):
    nz, rows, lanes = mine.shape

    def terms_from(other, shift):
        def terms(k, r):
            m, o, e = mine[k, r], other[k + shift, r], end[k, r]
            plus, minus, tangent = o - m, m - e, o - e
            return plus * plus, minus * minus, tangent * tangent, drive[k, r] * tangent

        return terms

    totals = sums_of(0, 2, rows, terms_from(edges, 0), no_sums(4, lanes))
    totals = sums_of(2, nz - 2, rows, terms_from(middle, -2), totals)
    totals = sums_of(nz - 2, nz, rows, terms_from(edges, 4 - nz), totals)
    out[...] = table_of(*(lane_row(t) for t in totals))


def coefficient(sums):
    total = jnp.sum(sums[...], axis=1, keepdims=True)
    plus_sq, minus_sq, tangent_sq, par = (total[i : i + 1] for i in range(4))
    safe = tangent_sq + EPSILON
    spring = SPRING_K * (jnp.sqrt(plus_sq) - jnp.sqrt(minus_sq)) / jnp.sqrt(safe)
    return STEP_SIZE * (spring - par / safe), par, safe


def other_step_kernel(edges, middle, end, low, high, sides, step_out, tangent_out, field, pot):
    nz, rows, _ = end.shape
    first, last = edges.at[0:2], edges.at[2:4]
    fill_padded(field, (low.at[0:2], first, middle, last, high.at[0:2]), sides, 0)
    fill_padded(tangent_out, (low.at[2:4], end, high.at[2:4]), sides, nz + 4)
    potentials(field, pot, nz + 2)

    def widen(k):
        tangent_out[k] = field[k] - tangent_out[k]

    def one(k):
        moved = field[k + 2] + STEP_SIZE * driving(pot, k)
        step_out[k] = moved[PAD : PAD + rows]

    layer_loop(0, nz + 4, widen)
    layer_loop(0, nz, one)


def second_step_kernel(sums, step, tangent_wide, end, moved_out, drive_out, minus_out, field, pot):
    nz, rows, _ = end.shape
    coef, _, _ = coefficient(sums)

    def move(k):
        field[k] = step[k] + coef * tangent_wide[k]

    layer_loop(0, nz + 4, move)
    potentials(field, pot, nz + 2)

    def one(k):
        drive = driving(pot, k)[PAD : PAD + rows]
        here = field[k + 2][PAD : PAD + rows]
        drive_out[k] = drive
        minus_out[k] = here - end[k]
        moved_out[k] = here + STEP_SIZE * drive

    layer_loop(0, nz, one)


def prepare_kernel(o_sums, other_step, mine, end, minus, near_out, known_out):
    nz, rows, lanes = mine.shape
    coef, _, _ = coefficient(o_sums)

    def near(k):
        near_out[k] = other_step[k] + coef * mine[k] - end[k]

    def terms(k, r):
        m = minus[k, r]
        return (m * m,)

    layer_loop(0, nz, near)
    (total,) = sums_of(0, nz, rows, terms, no_sums(1, lanes))
    known_out[...] = table_of(jnp.broadcast_to(coef, (1, 128)), lane_row(total))


def second_sums_kernel(known, far, near, minus, drive, out):
    nz, rows, lanes = far.shape
    coef = known[0:1, 0:1]

    def terms(k, r):
        tangent = near[k, r] - coef * far[k, r]
        plus = tangent - minus[k, r]
        return plus * plus, tangent * tangent, drive[k, r] * tangent

    plus, tangent, par = sums_of(0, nz, rows, terms, no_sums(3, lanes))
    out[...] = table_of(lane_row(plus), known[1:2], lane_row(tangent), lane_row(par))


def last_kernel(cells, sums, known, far, near, moved, base, out, par_out, buf, sems):
    del base
    nz = moved.shape[0]
    at = lax.axis_index("image")
    which = 1 - at
    coef, par, safe = coefficient(sums)
    o_coef = known[0:1, 0:1]
    copies = []
    for k in range(nz):
        buf[k] = moved[k] + coef * (near[k] - o_coef * far[k])
        if k % 4 == 3:
            where = pl.ds(k - 3, 4)
            copies.append(
                pltpu.make_async_copy(buf.at[where], out.at[which, where], sems.at[k // 4])
            )
            copies[-1].start()
    value = (par / jnp.sqrt(safe * cells))[0, 0]
    sign = jnp.where(at == 0, 1.0, -1.0).astype(jnp.float32)
    par_out[which] = value * sign
    par_out[1 - which] = jnp.float32(0.0)
    for c in copies:
        c.wait()


ANY = pl.BlockSpec(memory_space=pl.ANY)
VMEM = pl.BlockSpec(memory_space=pltpu.VMEM)
SMEM = pl.BlockSpec(memory_space=pltpu.SMEM)
DMA = pltpu.SemaphoreType.DMA
SWAP = [(0, 1), (1, 0)]


def copy_kernel(src, dst, sem):
    c = pltpu.make_async_copy(src, dst, sem)
    c.start()
    c.wait()


def from_z(up, down):
    count = lax.axis_size("space")
    low = lax.ppermute(up, "space", [(i, (i + 1) % count) for i in range(count)])
    high = lax.ppermute(down, "space", [((i + 1) % count, i) for i in range(count)])
    return low, high


def y_sides(*pieces):
    rows = pieces[0].shape[1]
    ends = [jnp.concatenate([p[:, :PAD], p[:, rows - PAD :]], 1) for p in pieces]
    return lax.ppermute(jnp.concatenate(ends, 0), "yslab", SWAP)


def summed(sums):
    sums = sums + lax.ppermute(sums, "yslab", SWAP)
    count, stride = lax.axis_size("space"), 1
    while stride < count:
        sums = sums + lax.ppermute(sums, "space", [(i, i ^ stride) for i in range(count)])
        stride *= 2
    return sums


def body_pair(images):
    _, nz, ny, nx = images.shape
    wide = ny + 2 * PAD
    cells = float(nz * lax.axis_size("space") * ny * lax.axis_size("yslab") * nx)
    block, outer = shape(nz, ny, nx), shape(nz + 4, wide, nx)
    table = shape(8, 128)

    def room(layers):
        return pltpu.VMEM((layers, wide, nx), jnp.float32)

    thin = shape(4, ny, nx)
    source = pltpu.with_memory_space_constraint(images, pltpu.HBM)
    edges, middle = call(
        send_kernel,
        [thin, shape(nz - 4, ny, nx)],
        [DMA((3,))],
        "send",
        in_specs=[ANY],
        out_specs=[ANY] * 2,
    )(source)
    mine, end, up, down = call(
        keep_kernel,
        [block, block, thin, thin],
        [DMA((4,))],
        "keep",
        in_specs=[ANY],
        out_specs=[ANY] * 4,
    )(source)

    o_edges = lax.ppermute(edges, "image", SWAP)
    o_middle = lax.ppermute(middle, "image", SWAP)

    low, high = from_z(up, down)
    sides = y_sides(low, mine, high)
    step, drive = call(first_step_kernel, [outer, block], [room(nz + 8), room(nz + 6)], "first_step")(
        mine, low, high, sides
    )
    end_later, drive = lax.optimization_barrier((end, drive))
    far = lax.ppermute(end_later, "image", SWAP)

    o_low, o_high = from_z(
        jnp.concatenate([o_edges[2:], end[nz - 2 :]]), jnp.concatenate([o_edges[:2], end[:2]])
    )
    o_low, o_high, o_middle = lax.optimization_barrier((o_low, o_high, o_middle))
    o_sides = y_sides(o_low[:2], o_edges[:2], o_middle, o_edges[2:], o_high[:2], o_low[2:], end, o_high[2:])

    base = call(
        copy_kernel,
        jax.ShapeDtypeStruct(images.shape, images.dtype),
        [DMA],
        "base",
        in_specs=[ANY],
        out_specs=ANY,
    )(images)

    sums = summed(call(first_sums_kernel, table, name="first_sums")(o_edges, o_middle, mine, end, drive))
    other_step, tangent_wide = call(
        other_step_kernel, [block, outer], [room(nz + 4), room(nz + 2)], "other_step"
    )(o_edges, o_middle, end, o_low, o_high, o_sides)

    moved, drive2, minus = call(
        second_step_kernel, [block] * 3, [room(nz + 4), room(nz + 2)], "second_step"
    )(sums, step, tangent_wide, end)

    o_sums = lax.ppermute(sums, "image", SWAP)
    near, known = call(prepare_kernel, [block, table], name="prepare")(
        o_sums, other_step, mine, end, minus
    )
    sums = summed(
        call(second_sums_kernel, table, name="second_sums")(known, far, near, minus, drive2)
    )

    return call(
        functools.partial(last_kernel, cells),
        [jax.ShapeDtypeStruct(images.shape, images.dtype), shape(2)],
        [pltpu.VMEM(block.shape, jnp.float32), DMA((nz // 4,))],
        "last",
        in_specs=[VMEM] * 5 + [ANY],
        out_specs=[ANY, SMEM],
        input_output_aliases={5: 0},
    )(sums, known, far, near, moved, base)


def body(images):
    layers = lax.axis_size("space")
    pair = lax.axis_size("image") == 2 and lax.axis_size("yslab") == 2 and images.shape[0] == 2
    pair = pair and layers & (layers - 1) == 0
    return body_pair(images) if pair else body_any(images)


def solution(mesh):
    in_specs = (P(("groups", "image"), "space", "yslab", None),)
    out_specs = (P(("groups", "image"), "space", "yslab", None), P(("groups", "image")))
    return jax.shard_map(body, mesh=mesh, in_specs=in_specs, out_specs=out_specs, check_vma=False)
```

```python
import functools
import math

import jax
import jax.numpy as jnp
from jax import lax
from jax.experimental import pallas as pl
from jax.experimental.pallas import tpu as pltpu
from jax.sharding import PartitionSpec as P

ITERS = 2


GRADIENT_COEF = 1.0
MOBILITY = 0.004
SPRING_K = 1.0
STEP_SIZE = 0.5
EPSILON = 1e-06

PAD = 8
VMEM_ROOM = 2 * 2**20
UNROLL = 4
AHEAD = 4


def passed_along(array, axis, by):
    peers = lax.axis_size(axis)
    pairs = [(i, i + by) for i in range(peers) if 0 <= i + by < peers]
    return lax.ppermute(array, axis, pairs)


def extended(cells, sides, width):
    for axis, dim in sides:
        count = lax.axis_size(axis)
        head = lax.slice_in_dim(cells, 0, width, axis=dim)
        tail = lax.slice_in_dim(cells, cells.shape[dim] - width, cells.shape[dim], axis=dim)
        cells = jnp.concatenate(
            [
                lax.ppermute(tail, axis, [(i, (i + 1) % count) for i in range(count)]),
                cells,
                lax.ppermute(head, axis, [((i + 1) % count, i) for i in range(count)]),
            ],
            axis=dim,
        )
    return cells


def stencil(padded):
    middle = padded[:, 1:-1, 1:-1]
    neighbours = padded[:, 2:, 1:-1] + padded[:, :-2, 1:-1]
    neighbours = neighbours + padded[:, 1:-1, 2:] + padded[:, 1:-1, :-2]
    neighbours = neighbours + jnp.roll(middle, -1, 3) + jnp.roll(middle, 1, 3)
    return neighbours - 6.0 * middle


def sum_cells(field):
    return jnp.sum(field, axis=(1, 2, 3))


def body_any(images):
    current = images
    per_device = current.shape[0]
    total_images = per_device * lax.axis_size("image")
    cell_total = float(
        current.shape[1]
        * lax.axis_size("space")
        * current.shape[2]
        * lax.axis_size("yslab")
        * current.shape[3]
    )
    image_ids = lax.axis_index("image") * per_device + jnp.arange(per_device, dtype=jnp.int32)
    interior = (image_ids > 0) & (image_ids < total_images - 1)
    parallel = jnp.zeros((per_device,), jnp.float32)
    for iteration in range(ITERS):
        next_first = passed_along(current[0], "image", -1)
        prev_last = passed_along(current[-1], "image", 1)
        ahead = jnp.concatenate([current[1:], next_first[None]], 0)
        behind = jnp.concatenate([prev_last[None], current[:-1]], 0)
        forward = ahead - current
        backward = current - behind
        tangent = forward + backward
        plus_sq, minus_sq, tangent_sq = lax.psum(
            (
                sum_cells(forward * forward),
                sum_cells(backward * backward),
                sum_cells(tangent * tangent),
            ),
            ("space", "yslab"),
        )
        wide_pad = extended(current, (("space", 1), ("yslab", 2)), 2)
        inner_field = wide_pad[:, 1:-1, 1:-1]
        potential = (
            inner_field * inner_field * inner_field
            - inner_field
            - GRADIENT_COEF * stencil(wide_pad)
        )
        driving = MOBILITY * stencil(potential)
        parallel_sum = lax.psum(sum_cells(driving * tangent), ("space", "yslab"))
        project_coef = parallel_sum / (tangent_sq + EPSILON)
        spring = (
            SPRING_K * (jnp.sqrt(plus_sq) - jnp.sqrt(minus_sq)) / jnp.sqrt(tangent_sq + EPSILON)
        )
        update = (
            driving
            - project_coef[:, None, None, None] * tangent
            + spring[:, None, None, None] * tangent
        )
        current = jnp.where(interior[:, None, None, None], current + STEP_SIZE * update, current)
        parallel = jnp.where(
            interior, parallel_sum / jnp.sqrt((tangent_sq + EPSILON) * cell_total), jnp.float32(0.0)
        )
    return (current, parallel)


def call(kernel, out_shape, scratch=(), name=None, **kw):
    return pl.pallas_call(
        kernel,
        out_shape=out_shape,
        scratch_shapes=list(scratch),
        name=name,
        compiler_params=pltpu.CompilerParams(
            vmem_limit_bytes=VMEM_ROOM + sum(4 * math.prod(s.shape) for s in scratch if s is not DMA)
        ),
        **kw,
    )


def shape(*dims):
    return jax.ShapeDtypeStruct(dims, jnp.float32)


def lap(below, here, above):
    rows, lanes = here.shape
    ys = pltpu.roll(here, 1, 0) + pltpu.roll(here, rows - 1, 0)
    xs = pltpu.roll(here, 1, 1) + pltpu.roll(here, lanes - 1, 1)
    return (below + above) + ys + xs - 6.0 * here


def layer_loop(start, stop, body):
    def step(k, carry):
        body(k)
        return carry

    lax.fori_loop(start, stop, step, 0, unroll=min(UNROLL, stop - start))


def potentials(field, pot, count):
    def one(k):
        here = field[k + 1]
        pot[k] = here * here * here - here - GRADIENT_COEF * lap(field[k], here, field[k + 2])

    layer_loop(0, count, one)


def driving(pot, k):
    return MOBILITY * lap(pot[k], pot[k + 1], pot[k + 2])


def rows_sum(field):
    rows, lanes = field.shape
    return jnp.sum(field.reshape(rows // 8, 8, lanes), axis=0)


def lane_row(total):
    lanes = total.shape[1]
    folded = jnp.sum(total.reshape(8, lanes // 128, 128), axis=1)
    return jnp.sum(folded, axis=0, keepdims=True)


def fill_padded(dst, pieces, sides, sides_at):
    at = 0
    for piece in pieces:
        layers, rows, _ = piece.shape
        dst[at : at + layers, PAD : PAD + rows] = piece[...]
        at += layers
    dst[:, 0:PAD] = sides[sides_at : sides_at + at, PAD : 2 * PAD]
    dst[:, PAD + rows : 2 * PAD + rows] = sides[sides_at : sides_at + at, 0:PAD]


def all_copied(pairs, sems):
    copies = [pltpu.make_async_copy(src, dst, sems.at[i]) for i, (src, dst) in enumerate(pairs)]
    for c in copies:
        c.start()
    for c in copies:
        c.wait()


def send_kernel(images, edges, middle, sems):
    which = 1 - lax.axis_index("image")
    nz = images.shape[1]
    pairs = [
        (images.at[which, pl.ds(0, AHEAD)], edges.at[pl.ds(0, AHEAD)]),
        (images.at[which, pl.ds(nz - AHEAD, AHEAD)], edges.at[pl.ds(AHEAD, AHEAD)]),
        (images.at[which, pl.ds(AHEAD, nz - 2 * AHEAD)], middle),
    ]
    all_copied(pairs, sems)


def keep_kernel(images, mine, end, up, down, sems):
    which = 1 - lax.axis_index("image")
    nz, layers = mine.shape[0], up.shape[0]
    pairs = [
        (images.at[which, pl.ds(nz - layers, layers)], up),
        (images.at[which, pl.ds(0, layers)], down),
        (images.at[which], mine),
        (images.at[1 - which], end),
    ]
    all_copied(pairs, sems)


def first_step_kernel(mine, low, high, sides, step_out, drive_out, field, pot):
    nz, rows, _ = mine.shape
    fill_padded(field, (low, mine, high), sides, 0)
    potentials(field, pot, nz + 6)

    def edge(k):
        step_out[k] = field[k + 2] + STEP_SIZE * driving(pot, k)

    def inner(k):
        drive = driving(pot, k)
        step_out[k] = field[k + 2] + STEP_SIZE * drive
        drive_out[k - 2] = drive[PAD : PAD + rows]

    layer_loop(0, 2, edge)
    layer_loop(2, nz + 2, inner)
    layer_loop(nz + 2, nz + 4, edge)


CHUNK = 16


def sums_of(start, stop, rows, terms, totals):
    def one(k, totals):
        for r in range(0, rows, CHUNK):
            totals = tuple(t + rows_sum(v) for t, v in zip(totals, terms(k, pl.ds(r, CHUNK))))
        return totals

    return lax.fori_loop(start, stop, one, totals, unroll=min(UNROLL, stop - start))


def no_sums(count, lanes):
    return (jnp.zeros((8, lanes), jnp.float32),) * count


def table_of(*rows):
    return jnp.concatenate(rows + (jnp.zeros((8 - len(rows), 128), jnp.float32),), 0)


def first_sums_kernel(edges, middle, mine, end, drive, out):
    nz, rows, lanes = mine.shape

    def terms_from(other, shift):
        def terms(k, r):
            m, o, e = mine[k, r], other[k + shift, r], end[k, r]
            plus, minus, tangent = o - m, m - e, o - e
            return plus * plus, minus * minus, tangent * tangent, drive[k, r] * tangent

        return terms

    last = nz - AHEAD
    totals = sums_of(0, AHEAD, rows, terms_from(edges, 0), no_sums(4, lanes))
    totals = sums_of(AHEAD, last, rows, terms_from(middle, -AHEAD), totals)
    totals = sums_of(last, nz, rows, terms_from(edges, AHEAD - last), totals)
    out[...] = table_of(*(lane_row(t) for t in totals))


def coefficient(sums):
    total = jnp.sum(sums[...], axis=1, keepdims=True)
    plus_sq, minus_sq, tangent_sq, par = (total[i : i + 1] for i in range(4))
    safe = tangent_sq + EPSILON
    spring = SPRING_K * (jnp.sqrt(plus_sq) - jnp.sqrt(minus_sq)) / jnp.sqrt(safe)
    return STEP_SIZE * (spring - par / safe), par, safe


def other_step_kernel(edges, middle, end, low, high, sides, near_out, tangent_out, field, pot):
    nz, rows, _ = end.shape
    first, last = edges.at[0:AHEAD], edges.at[AHEAD : 2 * AHEAD]
    fill_padded(field, (low.at[0:2], first, middle, last, high.at[0:2]), sides, 0)
    fill_padded(tangent_out, (low.at[2:4], end, high.at[2:4]), sides, nz + 4)
    potentials(field, pot, nz + 2)

    def widen(k):
        tangent_out[k] = field[k] - tangent_out[k]

    def one(k):
        moved = field[k + 2] + STEP_SIZE * driving(pot, k)
        near_out[k] = moved[PAD : PAD + rows] - end[k]

    layer_loop(0, nz + 4, widen)
    layer_loop(0, nz, one)


def second_step_kernel(sums, step, tangent_wide, end, moved_out, drive_out, minus_out, field, pot):
    nz, rows, _ = end.shape
    coef, _, _ = coefficient(sums)

    def move(k):
        field[k] = step[k] + coef * tangent_wide[k]

    layer_loop(0, nz + 4, move)
    potentials(field, pot, nz + 2)

    def one(k):
        drive = driving(pot, k)[PAD : PAD + rows]
        here = field[k + 2][PAD : PAD + rows]
        drive_out[k] = drive
        minus_out[k] = here - end[k]
        moved_out[k] = here + STEP_SIZE * drive

    layer_loop(0, nz, one)


def second_sums_kernel(o_sums, far, mine, near, minus, drive, out):
    nz, rows, lanes = far.shape
    coef, _, _ = coefficient(o_sums)

    def terms(k, r):
        tangent = near[k, r] + coef * (mine[k, r] - far[k, r])
        m = minus[k, r]
        plus = tangent - m
        return plus * plus, m * m, tangent * tangent, drive[k, r] * tangent

    out[...] = table_of(*(lane_row(t) for t in sums_of(0, nz, rows, terms, no_sums(4, lanes))))


def last_kernel(cells, sums, o_sums, far, mine, near, moved, base, out, par_out, buf, sems):
    del base
    nz = moved.shape[0]
    at = lax.axis_index("image")
    which = 1 - at
    coef, par, safe = coefficient(sums)
    o_coef, _, _ = coefficient(o_sums)
    copies = []
    for k in range(nz):
        buf[k] = moved[k] + coef * (near[k] + o_coef * (mine[k] - far[k]))
        if k % 4 == 3:
            where = pl.ds(k - 3, 4)
            copies.append(
                pltpu.make_async_copy(buf.at[where], out.at[which, where], sems.at[k // 4])
            )
            copies[-1].start()
    value = (par / jnp.sqrt(safe * cells))[0, 0]
    sign = jnp.where(at == 0, 1.0, -1.0).astype(jnp.float32)
    par_out[which] = value * sign
    par_out[1 - which] = jnp.float32(0.0)
    for c in copies:
        c.wait()


ANY = pl.BlockSpec(memory_space=pl.ANY)
VMEM = pl.BlockSpec(memory_space=pltpu.VMEM)
SMEM = pl.BlockSpec(memory_space=pltpu.SMEM)
DMA = pltpu.SemaphoreType.DMA
SWAP = [(0, 1), (1, 0)]


def copy_kernel(src, dst, sem):
    c = pltpu.make_async_copy(src, dst, sem)
    c.start()
    c.wait()


def from_z(up, down):
    count = lax.axis_size("space")
    low = lax.ppermute(up, "space", [(i, (i + 1) % count) for i in range(count)])
    high = lax.ppermute(down, "space", [((i + 1) % count, i) for i in range(count)])
    return low, high


def y_sides(*pieces):
    rows = pieces[0].shape[1]
    ends = [jnp.concatenate([p[:, :PAD], p[:, rows - PAD :]], 1) for p in pieces]
    return lax.ppermute(jnp.concatenate(ends, 0), "yslab", SWAP)


def summed(sums):
    sums = sums + lax.ppermute(sums, "yslab", SWAP)
    count, stride = lax.axis_size("space"), 1
    while stride < count:
        sums = sums + lax.ppermute(sums, "space", [(i, i ^ stride) for i in range(count)])
        stride *= 2
    return sums


def body_pair(images):
    _, nz, ny, nx = images.shape
    wide = ny + 2 * PAD
    cells = float(nz * lax.axis_size("space") * ny * lax.axis_size("yslab") * nx)
    block, outer = shape(nz, ny, nx), shape(nz + 4, wide, nx)
    table = shape(8, 128)

    def room(layers):
        return pltpu.VMEM((layers, wide, nx), jnp.float32)

    thin = shape(4, ny, nx)
    source = pltpu.with_memory_space_constraint(images, pltpu.HBM)
    edges, middle = call(
        send_kernel,
        [shape(2 * AHEAD, ny, nx), shape(nz - 2 * AHEAD, ny, nx)],
        [DMA((3,))],
        "send",
        in_specs=[ANY],
        out_specs=[ANY] * 2,
    )(source)
    mine, end, up, down = call(
        keep_kernel,
        [block, block, thin, thin],
        [DMA((4,))],
        "keep",
        in_specs=[ANY],
        out_specs=[ANY] * 4,
    )(source)

    o_edges = lax.ppermute(edges, "image", SWAP)
    o_middle = lax.ppermute(middle, "image", SWAP)

    low, high = from_z(up, down)
    sides = y_sides(low, mine, high)
    step, drive = call(first_step_kernel, [outer, block], [room(nz + 8), room(nz + 6)], "first_step")(
        mine, low, high, sides
    )
    end_later, drive = lax.optimization_barrier((end, drive))
    far = lax.ppermute(end_later, "image", SWAP)

    o_low, o_high = from_z(
        jnp.concatenate([o_edges[2 * AHEAD - 2 :], end[nz - 2 :]]),
        jnp.concatenate([o_edges[:2], end[:2]]),
    )
    o_low, o_high, o_middle = lax.optimization_barrier((o_low, o_high, o_middle))
    o_sides = y_sides(
        o_low[:2], o_edges[:AHEAD], o_middle, o_edges[AHEAD:], o_high[:2], o_low[2:], end, o_high[2:]
    )

    base = call(
        copy_kernel,
        jax.ShapeDtypeStruct(images.shape, images.dtype),
        [DMA],
        "base",
        in_specs=[ANY],
        out_specs=ANY,
    )(images)

    sums = summed(call(first_sums_kernel, table, name="first_sums")(o_edges, o_middle, mine, end, drive))
    near, tangent_wide = call(
        other_step_kernel, [block, outer], [room(nz + 4), room(nz + 2)], "other_step"
    )(o_edges, o_middle, end, o_low, o_high, o_sides)

    moved, drive2, minus = call(
        second_step_kernel, [block] * 3, [room(nz + 4), room(nz + 2)], "second_step"
    )(sums, step, tangent_wide, end)

    o_sums = lax.ppermute(sums, "image", SWAP)
    sums = call(second_sums_kernel, table, name="second_sums")(
        o_sums, far, mine, near, minus, drive2
    )

    return call(
        functools.partial(last_kernel, cells),
        [jax.ShapeDtypeStruct(images.shape, images.dtype), shape(2)],
        [pltpu.VMEM(block.shape, jnp.float32), DMA((nz // 4,))],
        "last",
        in_specs=[VMEM] * 6 + [ANY],
        out_specs=[ANY, SMEM],
        input_output_aliases={6: 0},
    )(summed(sums), o_sums, far, mine, near, moved, base)


def body(images):
    layers = lax.axis_size("space")
    pair = lax.axis_size("image") == 2 and lax.axis_size("yslab") == 2 and images.shape[0] == 2
    pair = pair and layers & (layers - 1) == 0 and images.shape[1] % 4 == 0
    pair = pair and images.shape[1] > 2 * AHEAD and images.shape[2] % CHUNK == 0
    return body_pair(images) if pair else body_any(images)


def solution(mesh):
    in_specs = (P(("groups", "image"), "space", "yslab", None),)
    out_specs = (P(("groups", "image"), "space", "yslab", None), P(("groups", "image")))
    return jax.shard_map(body, mesh=mesh, in_specs=in_specs, out_specs=out_specs, check_vma=False)
```

```python
import functools
import math

import jax
import jax.numpy as jnp
from jax import lax
from jax.experimental import pallas as pl
from jax.experimental.pallas import tpu as pltpu
from jax.sharding import PartitionSpec as P

ITERS = 2


GRADIENT_COEF = 1.0
MOBILITY = 0.004
SPRING_K = 1.0
STEP_SIZE = 0.5
EPSILON = 1e-06

PAD = 8
VMEM_ROOM = 2 * 2**20
UNROLL = 4
AHEAD = 2


def passed_along(array, axis, by):
    peers = lax.axis_size(axis)
    pairs = [(i, i + by) for i in range(peers) if 0 <= i + by < peers]
    return lax.ppermute(array, axis, pairs)


def extended(cells, sides, width):
    for axis, dim in sides:
        count = lax.axis_size(axis)
        head = lax.slice_in_dim(cells, 0, width, axis=dim)
        tail = lax.slice_in_dim(cells, cells.shape[dim] - width, cells.shape[dim], axis=dim)
        cells = jnp.concatenate(
            [
                lax.ppermute(tail, axis, [(i, (i + 1) % count) for i in range(count)]),
                cells,
                lax.ppermute(head, axis, [((i + 1) % count, i) for i in range(count)]),
            ],
            axis=dim,
        )
    return cells


def stencil(padded):
    middle = padded[:, 1:-1, 1:-1]
    neighbours = padded[:, 2:, 1:-1] + padded[:, :-2, 1:-1]
    neighbours = neighbours + padded[:, 1:-1, 2:] + padded[:, 1:-1, :-2]
    neighbours = neighbours + jnp.roll(middle, -1, 3) + jnp.roll(middle, 1, 3)
    return neighbours - 6.0 * middle


def sum_cells(field):
    return jnp.sum(field, axis=(1, 2, 3))


def body_any(images):
    current = images
    per_device = current.shape[0]
    total_images = per_device * lax.axis_size("image")
    cell_total = float(
        current.shape[1]
        * lax.axis_size("space")
        * current.shape[2]
        * lax.axis_size("yslab")
        * current.shape[3]
    )
    image_ids = lax.axis_index("image") * per_device + jnp.arange(per_device, dtype=jnp.int32)
    interior = (image_ids > 0) & (image_ids < total_images - 1)
    parallel = jnp.zeros((per_device,), jnp.float32)
    for iteration in range(ITERS):
        next_first = passed_along(current[0], "image", -1)
        prev_last = passed_along(current[-1], "image", 1)
        ahead = jnp.concatenate([current[1:], next_first[None]], 0)
        behind = jnp.concatenate([prev_last[None], current[:-1]], 0)
        forward = ahead - current
        backward = current - behind
        tangent = forward + backward
        plus_sq, minus_sq, tangent_sq = lax.psum(
            (
                sum_cells(forward * forward),
                sum_cells(backward * backward),
                sum_cells(tangent * tangent),
            ),
            ("space", "yslab"),
        )
        wide_pad = extended(current, (("space", 1), ("yslab", 2)), 2)
        inner_field = wide_pad[:, 1:-1, 1:-1]
        potential = (
            inner_field * inner_field * inner_field
            - inner_field
            - GRADIENT_COEF * stencil(wide_pad)
        )
        driving = MOBILITY * stencil(potential)
        parallel_sum = lax.psum(sum_cells(driving * tangent), ("space", "yslab"))
        project_coef = parallel_sum / (tangent_sq + EPSILON)
        spring = (
            SPRING_K * (jnp.sqrt(plus_sq) - jnp.sqrt(minus_sq)) / jnp.sqrt(tangent_sq + EPSILON)
        )
        update = (
            driving
            - project_coef[:, None, None, None] * tangent
            + spring[:, None, None, None] * tangent
        )
        current = jnp.where(interior[:, None, None, None], current + STEP_SIZE * update, current)
        parallel = jnp.where(
            interior, parallel_sum / jnp.sqrt((tangent_sq + EPSILON) * cell_total), jnp.float32(0.0)
        )
    return (current, parallel)


def call(kernel, out_shape, scratch=(), name=None, **kw):
    return pl.pallas_call(
        kernel,
        out_shape=out_shape,
        scratch_shapes=list(scratch),
        name=name,
        compiler_params=pltpu.CompilerParams(
            vmem_limit_bytes=VMEM_ROOM + sum(4 * math.prod(s.shape) for s in scratch if s is not DMA)
        ),
        **kw,
    )


def shape(*dims):
    return jax.ShapeDtypeStruct(dims, jnp.float32)


def lap(below, here, above):
    rows, lanes = here.shape
    ys = pltpu.roll(here, 1, 0) + pltpu.roll(here, rows - 1, 0)
    xs = pltpu.roll(here, 1, 1) + pltpu.roll(here, lanes - 1, 1)
    return (below + above) + ys + xs - 6.0 * here


def layer_loop(start, stop, body):
    def step(k, carry):
        body(k)
        return carry

    lax.fori_loop(start, stop, step, 0, unroll=min(UNROLL, stop - start))


def potentials(field, pot, count):
    def one(k):
        here = field[k + 1]
        pot[k] = here * here * here - here - GRADIENT_COEF * lap(field[k], here, field[k + 2])

    layer_loop(0, count, one)


def driving(pot, k):
    return MOBILITY * lap(pot[k], pot[k + 1], pot[k + 2])


def rows_sum(field):
    rows, lanes = field.shape
    return jnp.sum(field.reshape(rows // 8, 8, lanes), axis=0)


def lane_row(total):
    lanes = total.shape[1]
    folded = jnp.sum(total.reshape(8, lanes // 128, 128), axis=1)
    return jnp.sum(folded, axis=0, keepdims=True)


def fill_padded(dst, pieces, sides, sides_at):
    at = 0
    for piece in pieces:
        layers, rows, _ = piece.shape
        dst[at : at + layers, PAD : PAD + rows] = piece[...]
        at += layers
    dst[:, 0:PAD] = sides[sides_at : sides_at + at, PAD : 2 * PAD]
    dst[:, PAD + rows : 2 * PAD + rows] = sides[sides_at : sides_at + at, 0:PAD]


def all_copied(pairs, sems):
    copies = [pltpu.make_async_copy(src, dst, sems.at[i]) for i, (src, dst) in enumerate(pairs)]
    for c in copies:
        c.start()
    for c in copies:
        c.wait()


def send_kernel(images, edges, middle, sems):
    which = 1 - lax.axis_index("image")
    nz = images.shape[1]
    pairs = [
        (images.at[which, pl.ds(0, AHEAD)], edges.at[pl.ds(0, AHEAD)]),
        (images.at[which, pl.ds(nz - AHEAD, AHEAD)], edges.at[pl.ds(AHEAD, AHEAD)]),
        (images.at[which, pl.ds(AHEAD, nz - 2 * AHEAD)], middle),
    ]
    all_copied(pairs, sems)


def keep_kernel(images, mine, end, up, down, sems):
    which = 1 - lax.axis_index("image")
    nz, layers = mine.shape[0], up.shape[0]
    pairs = [
        (images.at[which, pl.ds(nz - layers, layers)], up),
        (images.at[which, pl.ds(0, layers)], down),
        (images.at[which], mine),
        (images.at[1 - which], end),
    ]
    all_copied(pairs, sems)


def first_step_kernel(mine, low, high, sides, step_out, drive_out, field, pot):
    nz, rows, _ = mine.shape
    fill_padded(field, (low, mine, high), sides, 0)
    potentials(field, pot, nz + 6)

    def edge(k):
        step_out[k] = field[k + 2] + STEP_SIZE * driving(pot, k)

    def inner(k):
        drive = driving(pot, k)
        step_out[k] = field[k + 2] + STEP_SIZE * drive
        drive_out[k - 2] = drive[PAD : PAD + rows]

    layer_loop(0, 2, edge)
    layer_loop(2, nz + 2, inner)
    layer_loop(nz + 2, nz + 4, edge)


CHUNK = 16


def sums_of(start, stop, rows, terms, totals):
    def one(k, totals):
        for r in range(0, rows, CHUNK):
            totals = tuple(t + rows_sum(v) for t, v in zip(totals, terms(k, pl.ds(r, CHUNK))))
        return totals

    return lax.fori_loop(start, stop, one, totals, unroll=min(UNROLL, stop - start))


def no_sums(count, lanes):
    return (jnp.zeros((8, lanes), jnp.float32),) * count


def table_of(*rows):
    return jnp.concatenate(rows + (jnp.zeros((8 - len(rows), 128), jnp.float32),), 0)


def first_sums_kernel(edges, middle, mine, end, drive, out):
    nz, rows, lanes = mine.shape

    def terms_from(other, shift):
        def terms(k, r):
            m, o, e = mine[k, r], other[k + shift, r], end[k, r]
            plus, minus, tangent = o - m, m - e, o - e
            return plus * plus, minus * minus, tangent * tangent, drive[k, r] * tangent

        return terms

    last = nz - AHEAD
    totals = sums_of(0, AHEAD, rows, terms_from(edges, 0), no_sums(4, lanes))
    totals = sums_of(AHEAD, last, rows, terms_from(middle, -AHEAD), totals)
    totals = sums_of(last, nz, rows, terms_from(edges, AHEAD - last), totals)
    out[...] = table_of(*(lane_row(t) for t in totals))


def coefficient(sums):
    total = jnp.sum(sums[...], axis=1, keepdims=True)
    plus_sq, minus_sq, tangent_sq, par = (total[i : i + 1] for i in range(4))
    safe = tangent_sq + EPSILON
    spring = SPRING_K * (jnp.sqrt(plus_sq) - jnp.sqrt(minus_sq)) / jnp.sqrt(safe)
    return STEP_SIZE * (spring - par / safe), par, safe


def other_step_kernel(edges, middle, end, low, high, sides, near_out, tangent_out, field, pot):
    nz, rows, _ = end.shape
    first, last = edges.at[0:AHEAD], edges.at[AHEAD : 2 * AHEAD]
    fill_padded(field, (low.at[0:2], first, middle, last, high.at[0:2]), sides, 0)
    fill_padded(tangent_out, (low.at[2:4], end, high.at[2:4]), sides, nz + 4)
    potentials(field, pot, nz + 2)

    def widen(k):
        tangent_out[k] = field[k] - tangent_out[k]

    def one(k):
        moved = field[k + 2] + STEP_SIZE * driving(pot, k)
        near_out[k] = moved[PAD : PAD + rows] - end[k]

    layer_loop(0, nz + 4, widen)
    layer_loop(0, nz, one)


def second_step_kernel(sums, step, tangent_wide, end, moved_out, drive_out, minus_out, field, pot):
    nz, rows, _ = end.shape
    coef, _, _ = coefficient(sums)

    def move(k):
        field[k] = step[k] + coef * tangent_wide[k]

    layer_loop(0, nz + 4, move)
    potentials(field, pot, nz + 2)

    def one(k):
        drive = driving(pot, k)[PAD : PAD + rows]
        here = field[k + 2][PAD : PAD + rows]
        drive_out[k] = drive
        minus_out[k] = here - end[k]
        moved_out[k] = here + STEP_SIZE * drive

    layer_loop(0, nz, one)


def second_sums_kernel(o_sums, far, mine, near, minus, drive, out):
    nz, rows, lanes = far.shape
    coef, _, _ = coefficient(o_sums)

    def terms(k, r):
        tangent = near[k, r] + coef * (mine[k, r] - far[k, r])
        m = minus[k, r]
        plus = tangent - m
        return plus * plus, m * m, tangent * tangent, drive[k, r] * tangent

    out[...] = table_of(*(lane_row(t) for t in sums_of(0, nz, rows, terms, no_sums(4, lanes))))


def last_kernel(cells, sums, o_sums, far, mine, near, moved, base, out, par_out, buf, sems):
    del base
    nz = moved.shape[0]
    at = lax.axis_index("image")
    which = 1 - at
    coef, par, safe = coefficient(sums)
    o_coef, _, _ = coefficient(o_sums)
    copies = []
    for k in range(nz):
        buf[k] = moved[k] + coef * (near[k] + o_coef * (mine[k] - far[k]))
        if k % 4 == 3:
            where = pl.ds(k - 3, 4)
            copies.append(
                pltpu.make_async_copy(buf.at[where], out.at[which, where], sems.at[k // 4])
            )
            copies[-1].start()
    value = (par / jnp.sqrt(safe * cells))[0, 0]
    sign = jnp.where(at == 0, 1.0, -1.0).astype(jnp.float32)
    par_out[which] = value * sign
    par_out[1 - which] = jnp.float32(0.0)
    for c in copies:
        c.wait()


ANY = pl.BlockSpec(memory_space=pl.ANY)
VMEM = pl.BlockSpec(memory_space=pltpu.VMEM)
SMEM = pl.BlockSpec(memory_space=pltpu.SMEM)
DMA = pltpu.SemaphoreType.DMA
SWAP = [(0, 1), (1, 0)]


def copy_kernel(src, dst, sem):
    c = pltpu.make_async_copy(src, dst, sem)
    c.start()
    c.wait()


def from_z(up, down):
    count = lax.axis_size("space")
    low = lax.ppermute(up, "space", [(i, (i + 1) % count) for i in range(count)])
    high = lax.ppermute(down, "space", [((i + 1) % count, i) for i in range(count)])
    return low, high


def y_sides(*pieces):
    rows = pieces[0].shape[1]
    ends = [jnp.concatenate([p[:, :PAD], p[:, rows - PAD :]], 1) for p in pieces]
    return lax.ppermute(jnp.concatenate(ends, 0), "yslab", SWAP)


def summed(sums):
    sums = sums + lax.ppermute(sums, "yslab", SWAP)
    count, stride = lax.axis_size("space"), 1
    while stride < count:
        sums = sums + lax.ppermute(sums, "space", [(i, i ^ stride) for i in range(count)])
        stride *= 2
    return sums


def body_pair(images):
    _, nz, ny, nx = images.shape
    wide = ny + 2 * PAD
    cells = float(nz * lax.axis_size("space") * ny * lax.axis_size("yslab") * nx)
    block, outer = shape(nz, ny, nx), shape(nz + 4, wide, nx)
    table = shape(8, 128)

    def room(layers):
        return pltpu.VMEM((layers, wide, nx), jnp.float32)

    thin = shape(4, ny, nx)
    source = pltpu.with_memory_space_constraint(images, pltpu.HBM)
    edges, middle = call(
        send_kernel,
        [shape(2 * AHEAD, ny, nx), shape(nz - 2 * AHEAD, ny, nx)],
        [DMA((3,))],
        "send",
        in_specs=[ANY],
        out_specs=[ANY] * 2,
    )(source)
    mine, end, up, down = call(
        keep_kernel,
        [block, block, thin, thin],
        [DMA((4,))],
        "keep",
        in_specs=[ANY],
        out_specs=[ANY] * 4,
    )(source)

    o_first = lax.ppermute(edges[:AHEAD], "image", SWAP)
    o_last = lax.ppermute(edges[AHEAD:], "image", SWAP)
    o_middle = lax.ppermute(middle, "image", SWAP)
    far = lax.ppermute(end, "image", SWAP)

    up, down, o_first = lax.optimization_barrier((up, down, o_first))
    o_edges = jnp.concatenate([o_first, o_last])
    low, high = from_z(up, down)
    sides = y_sides(low, mine, high)
    step, drive = call(first_step_kernel, [outer, block], [room(nz + 8), room(nz + 6)], "first_step")(
        mine, low, high, sides
    )

    o_low, o_high = from_z(
        jnp.concatenate([o_edges[2 * AHEAD - 2 :], end[nz - 2 :]]),
        jnp.concatenate([o_edges[:2], end[:2]]),
    )
    base = call(
        copy_kernel,
        jax.ShapeDtypeStruct(images.shape, images.dtype),
        [DMA],
        "base",
        in_specs=[ANY],
        out_specs=ANY,
    )(images)

    sums = summed(
        call(first_sums_kernel, table, name="first_sums")(o_edges, o_middle, mine, end, drive)
    )
    o_low, o_high, sums = lax.optimization_barrier((o_low, o_high, sums))
    o_sides = y_sides(
        o_low[:2], o_edges[:AHEAD], o_middle, o_edges[AHEAD:], o_high[:2], o_low[2:], end, o_high[2:]
    )
    near, tangent_wide = call(
        other_step_kernel, [block, outer], [room(nz + 4), room(nz + 2)], "other_step"
    )(o_edges, o_middle, end, o_low, o_high, o_sides)

    moved, drive2, minus = call(
        second_step_kernel, [block] * 3, [room(nz + 4), room(nz + 2)], "second_step"
    )(sums, step, tangent_wide, end)

    o_sums = lax.ppermute(sums, "image", SWAP)
    sums = call(second_sums_kernel, table, name="second_sums")(
        o_sums, far, mine, near, minus, drive2
    )

    return call(
        functools.partial(last_kernel, cells),
        [jax.ShapeDtypeStruct(images.shape, images.dtype), shape(2)],
        [pltpu.VMEM(block.shape, jnp.float32), DMA((nz // 4,))],
        "last",
        in_specs=[VMEM] * 6 + [ANY],
        out_specs=[ANY, SMEM],
        input_output_aliases={6: 0},
    )(summed(sums), o_sums, far, mine, near, moved, base)


def body(images):
    layers = lax.axis_size("space")
    pair = lax.axis_size("image") == 2 and lax.axis_size("yslab") == 2 and images.shape[0] == 2
    pair = pair and layers & (layers - 1) == 0 and images.shape[1] % 4 == 0
    pair = pair and images.shape[1] > 2 * AHEAD and images.shape[2] % CHUNK == 0
    return body_pair(images) if pair else body_any(images)


def solution(mesh):
    in_specs = (P(("groups", "image"), "space", "yslab", None),)
    out_specs = (P(("groups", "image"), "space", "yslab", None), P(("groups", "image")))
    return jax.shard_map(body, mesh=mesh, in_specs=in_specs, out_specs=out_specs, check_vma=False)
```

```python
import functools
import math

import jax
import jax.numpy as jnp
from jax import lax
from jax.experimental import pallas as pl
from jax.experimental.pallas import tpu as pltpu
from jax.sharding import PartitionSpec as P

ITERS = 2


GRADIENT_COEF = 1.0
MOBILITY = 0.004
SPRING_K = 1.0
STEP_SIZE = 0.5
EPSILON = 1e-06

PAD = 8
VMEM_ROOM = 2 * 2**20
UNROLL = 4
AHEAD = 2


def passed_along(array, axis, by):
    peers = lax.axis_size(axis)
    pairs = [(i, i + by) for i in range(peers) if 0 <= i + by < peers]
    return lax.ppermute(array, axis, pairs)


def extended(cells, sides, width):
    for axis, dim in sides:
        count = lax.axis_size(axis)
        head = lax.slice_in_dim(cells, 0, width, axis=dim)
        tail = lax.slice_in_dim(cells, cells.shape[dim] - width, cells.shape[dim], axis=dim)
        cells = jnp.concatenate(
            [
                lax.ppermute(tail, axis, [(i, (i + 1) % count) for i in range(count)]),
                cells,
                lax.ppermute(head, axis, [((i + 1) % count, i) for i in range(count)]),
            ],
            axis=dim,
        )
    return cells


def stencil(padded):
    middle = padded[:, 1:-1, 1:-1]
    neighbours = padded[:, 2:, 1:-1] + padded[:, :-2, 1:-1]
    neighbours = neighbours + padded[:, 1:-1, 2:] + padded[:, 1:-1, :-2]
    neighbours = neighbours + jnp.roll(middle, -1, 3) + jnp.roll(middle, 1, 3)
    return neighbours - 6.0 * middle


def sum_cells(field):
    return jnp.sum(field, axis=(1, 2, 3))


def body_any(images):
    current = images
    per_device = current.shape[0]
    total_images = per_device * lax.axis_size("image")
    cell_total = float(
        current.shape[1]
        * lax.axis_size("space")
        * current.shape[2]
        * lax.axis_size("yslab")
        * current.shape[3]
    )
    image_ids = lax.axis_index("image") * per_device + jnp.arange(per_device, dtype=jnp.int32)
    interior = (image_ids > 0) & (image_ids < total_images - 1)
    parallel = jnp.zeros((per_device,), jnp.float32)
    for iteration in range(ITERS):
        next_first = passed_along(current[0], "image", -1)
        prev_last = passed_along(current[-1], "image", 1)
        ahead = jnp.concatenate([current[1:], next_first[None]], 0)
        behind = jnp.concatenate([prev_last[None], current[:-1]], 0)
        forward = ahead - current
        backward = current - behind
        tangent = forward + backward
        plus_sq, minus_sq, tangent_sq = lax.psum(
            (
                sum_cells(forward * forward),
                sum_cells(backward * backward),
                sum_cells(tangent * tangent),
            ),
            ("space", "yslab"),
        )
        wide_pad = extended(current, (("space", 1), ("yslab", 2)), 2)
        inner_field = wide_pad[:, 1:-1, 1:-1]
        potential = (
            inner_field * inner_field * inner_field
            - inner_field
            - GRADIENT_COEF * stencil(wide_pad)
        )
        driving = MOBILITY * stencil(potential)
        parallel_sum = lax.psum(sum_cells(driving * tangent), ("space", "yslab"))
        project_coef = parallel_sum / (tangent_sq + EPSILON)
        spring = (
            SPRING_K * (jnp.sqrt(plus_sq) - jnp.sqrt(minus_sq)) / jnp.sqrt(tangent_sq + EPSILON)
        )
        update = (
            driving
            - project_coef[:, None, None, None] * tangent
            + spring[:, None, None, None] * tangent
        )
        current = jnp.where(interior[:, None, None, None], current + STEP_SIZE * update, current)
        parallel = jnp.where(
            interior, parallel_sum / jnp.sqrt((tangent_sq + EPSILON) * cell_total), jnp.float32(0.0)
        )
    return (current, parallel)


def call(kernel, out_shape, scratch=(), name=None, **kw):
    return pl.pallas_call(
        kernel,
        out_shape=out_shape,
        scratch_shapes=list(scratch),
        name=name,
        compiler_params=pltpu.CompilerParams(
            vmem_limit_bytes=VMEM_ROOM + sum(4 * math.prod(s.shape) for s in scratch if s is not DMA)
        ),
        **kw,
    )


def shape(*dims):
    return jax.ShapeDtypeStruct(dims, jnp.float32)


def lap(below, here, above):
    rows, lanes = here.shape
    ys = pltpu.roll(here, 1, 0) + pltpu.roll(here, rows - 1, 0)
    xs = pltpu.roll(here, 1, 1) + pltpu.roll(here, lanes - 1, 1)
    return (below + above) + ys + xs - 6.0 * here


def layer_loop(start, stop, body):
    def step(k, carry):
        body(k)
        return carry

    lax.fori_loop(start, stop, step, 0, unroll=min(UNROLL, stop - start))


def potentials(field, pot, count):
    def one(k):
        here = field[k + 1]
        pot[k] = here * here * here - here - GRADIENT_COEF * lap(field[k], here, field[k + 2])

    layer_loop(0, count, one)


def driving(pot, k):
    return MOBILITY * lap(pot[k], pot[k + 1], pot[k + 2])


def rows_sum(field):
    rows, lanes = field.shape
    return jnp.sum(field.reshape(rows // 8, 8, lanes), axis=0)


def lane_row(total):
    lanes = total.shape[1]
    folded = jnp.sum(total.reshape(8, lanes // 128, 128), axis=1)
    return jnp.sum(folded, axis=0, keepdims=True)


def fill_padded(dst, pieces, sides, sides_at):
    at = 0
    for piece in pieces:
        layers, rows, _ = piece.shape
        dst[at : at + layers, PAD : PAD + rows] = piece[...]
        at += layers
    dst[:, 0:PAD] = sides[sides_at : sides_at + at, PAD : 2 * PAD]
    dst[:, PAD + rows : 2 * PAD + rows] = sides[sides_at : sides_at + at, 0:PAD]


def all_copied(pairs, sems):
    copies = [pltpu.make_async_copy(src, dst, sems.at[i]) for i, (src, dst) in enumerate(pairs)]
    for c in copies:
        c.start()
    for c in copies:
        c.wait()


def send_kernel(images, edges, middle, sems):
    which = 1 - lax.axis_index("image")
    nz = images.shape[1]
    pairs = [
        (images.at[which, pl.ds(0, AHEAD)], edges.at[pl.ds(0, AHEAD)]),
        (images.at[which, pl.ds(nz - AHEAD, AHEAD)], edges.at[pl.ds(AHEAD, AHEAD)]),
        (images.at[which, pl.ds(AHEAD, nz - 2 * AHEAD)], middle),
    ]
    all_copied(pairs, sems)


def keep_kernel(images, mine, end, up, down, sems):
    which = 1 - lax.axis_index("image")
    nz, layers = mine.shape[0], up.shape[0]
    pairs = [
        (images.at[which, pl.ds(nz - layers, layers)], up),
        (images.at[which, pl.ds(0, layers)], down),
        (images.at[which], mine),
        (images.at[1 - which], end),
    ]
    all_copied(pairs, sems)


def first_step_kernel(mine, low, high, sides, step_out, drive_out, field, pot):
    nz, rows, _ = mine.shape
    fill_padded(field, (low, mine, high), sides, 0)
    potentials(field, pot, nz + 6)

    def edge(k):
        step_out[k] = field[k + 2] + STEP_SIZE * driving(pot, k)

    def inner(k):
        drive = driving(pot, k)
        step_out[k] = field[k + 2] + STEP_SIZE * drive
        drive_out[k - 2] = drive[PAD : PAD + rows]

    layer_loop(0, 2, edge)
    layer_loop(2, nz + 2, inner)
    layer_loop(nz + 2, nz + 4, edge)


CHUNK = 16


def sums_of(start, stop, rows, terms, totals):
    def one(k, totals):
        for r in range(0, rows, CHUNK):
            totals = tuple(t + rows_sum(v) for t, v in zip(totals, terms(k, pl.ds(r, CHUNK))))
        return totals

    return lax.fori_loop(start, stop, one, totals, unroll=min(UNROLL, stop - start))


def no_sums(count, lanes):
    return (jnp.zeros((8, lanes), jnp.float32),) * count


def table_of(*rows):
    return jnp.concatenate(rows + (jnp.zeros((8 - len(rows), 128), jnp.float32),), 0)


def first_sums_kernel(edges, middle, mine, end, drive, out):
    nz, rows, lanes = mine.shape

    def terms_from(other, shift):
        def terms(k, r):
            m, o, e = mine[k, r], other[k + shift, r], end[k, r]
            plus, minus, tangent = o - m, m - e, o - e
            return plus * plus, minus * minus, tangent * tangent, drive[k, r] * tangent

        return terms

    last = nz - AHEAD
    totals = sums_of(0, AHEAD, rows, terms_from(edges, 0), no_sums(4, lanes))
    totals = sums_of(AHEAD, last, rows, terms_from(middle, -AHEAD), totals)
    totals = sums_of(last, nz, rows, terms_from(edges, AHEAD - last), totals)
    out[...] = table_of(*(lane_row(t) for t in totals))


def coefficient(sums):
    total = jnp.sum(sums[...], axis=1, keepdims=True)
    plus_sq, minus_sq, tangent_sq, par = (total[i : i + 1] for i in range(4))
    safe = tangent_sq + EPSILON
    spring = SPRING_K * (jnp.sqrt(plus_sq) - jnp.sqrt(minus_sq)) / jnp.sqrt(safe)
    return STEP_SIZE * (spring - par / safe), par, safe


def other_step_kernel(edges, middle, end, low, high, sides, near_out, tangent_out, field, pot):
    nz, rows, _ = end.shape
    first, last = edges.at[0:AHEAD], edges.at[AHEAD : 2 * AHEAD]
    fill_padded(field, (low.at[0:2], first, middle, last, high.at[0:2]), sides, 0)
    fill_padded(tangent_out, (low.at[2:4], end, high.at[2:4]), sides, nz + 4)
    potentials(field, pot, nz + 2)

    def widen(k):
        tangent_out[k] = field[k] - tangent_out[k]

    def one(k):
        moved = field[k + 2] + STEP_SIZE * driving(pot, k)
        near_out[k] = moved[PAD : PAD + rows] - end[k]

    layer_loop(0, nz + 4, widen)
    layer_loop(0, nz, one)


def second_step_kernel(
    sums, step, tangent_wide, end, images, moved_out, drive_out, minus_out, base, field, pot, sem
):
    nz, rows, _ = end.shape
    still = lax.axis_index("image")
    copy = pltpu.make_async_copy(images.at[still], base.at[still], sem)
    copy.start()
    coef, _, _ = coefficient(sums)

    def move(k):
        field[k] = step[k] + coef * tangent_wide[k]

    layer_loop(0, nz + 4, move)
    potentials(field, pot, nz + 2)

    def one(k):
        drive = driving(pot, k)[PAD : PAD + rows]
        here = field[k + 2][PAD : PAD + rows]
        drive_out[k] = drive
        minus_out[k] = here - end[k]
        moved_out[k] = here + STEP_SIZE * drive

    layer_loop(0, nz, one)
    copy.wait()


def second_sums_kernel(o_sums, far, mine, near, minus, drive, out):
    nz, rows, lanes = far.shape
    coef, _, _ = coefficient(o_sums)

    def terms(k, r):
        tangent = near[k, r] + coef * (mine[k, r] - far[k, r])
        m = minus[k, r]
        plus = tangent - m
        return plus * plus, m * m, tangent * tangent, drive[k, r] * tangent

    out[...] = table_of(*(lane_row(t) for t in sums_of(0, nz, rows, terms, no_sums(4, lanes))))


def last_kernel(cells, sums, o_sums, far, mine, near, moved, base, out, par_out, buf, sems):
    del base
    nz = moved.shape[0]
    at = lax.axis_index("image")
    which = 1 - at
    coef, par, safe = coefficient(sums)
    o_coef, _, _ = coefficient(o_sums)
    copies = []
    for k in range(nz):
        buf[k] = moved[k] + coef * (near[k] + o_coef * (mine[k] - far[k]))
        if k % 4 == 3:
            where = pl.ds(k - 3, 4)
            copies.append(
                pltpu.make_async_copy(buf.at[where], out.at[which, where], sems.at[k // 4])
            )
            copies[-1].start()
    value = (par / jnp.sqrt(safe * cells))[0, 0]
    sign = jnp.where(at == 0, 1.0, -1.0).astype(jnp.float32)
    par_out[which] = value * sign
    par_out[1 - which] = jnp.float32(0.0)
    for c in copies:
        c.wait()


ANY = pl.BlockSpec(memory_space=pl.ANY)
VMEM = pl.BlockSpec(memory_space=pltpu.VMEM)
SMEM = pl.BlockSpec(memory_space=pltpu.SMEM)
DMA = pltpu.SemaphoreType.DMA
SWAP = [(0, 1), (1, 0)]


def from_z(up, down):
    count = lax.axis_size("space")
    low = lax.ppermute(up, "space", [(i, (i + 1) % count) for i in range(count)])
    high = lax.ppermute(down, "space", [((i + 1) % count, i) for i in range(count)])
    return low, high


def y_sides(*pieces):
    rows = pieces[0].shape[1]
    ends = [jnp.concatenate([p[:, :PAD], p[:, rows - PAD :]], 1) for p in pieces]
    return lax.ppermute(jnp.concatenate(ends, 0), "yslab", SWAP)


def summed(sums):
    sums = sums + lax.ppermute(sums, "yslab", SWAP)
    count, stride = lax.axis_size("space"), 1
    while stride < count:
        sums = sums + lax.ppermute(sums, "space", [(i, i ^ stride) for i in range(count)])
        stride *= 2
    return sums


def body_pair(images):
    _, nz, ny, nx = images.shape
    wide = ny + 2 * PAD
    cells = float(nz * lax.axis_size("space") * ny * lax.axis_size("yslab") * nx)
    block, outer = shape(nz, ny, nx), shape(nz + 4, wide, nx)
    table = shape(8, 128)

    def room(layers):
        return pltpu.VMEM((layers, wide, nx), jnp.float32)

    thin = shape(4, ny, nx)
    source = pltpu.with_memory_space_constraint(images, pltpu.HBM)
    edges, middle = call(
        send_kernel,
        [shape(2 * AHEAD, ny, nx), shape(nz - 2 * AHEAD, ny, nx)],
        [DMA((3,))],
        "send",
        in_specs=[ANY],
        out_specs=[ANY] * 2,
    )(source)
    mine, end, up, down = call(
        keep_kernel,
        [block, block, thin, thin],
        [DMA((4,))],
        "keep",
        in_specs=[ANY],
        out_specs=[ANY] * 4,
    )(source)

    o_first = lax.ppermute(edges[:AHEAD], "image", SWAP)
    o_last = lax.ppermute(edges[AHEAD:], "image", SWAP)
    o_middle = lax.ppermute(middle, "image", SWAP)
    far = lax.ppermute(end, "image", SWAP)

    up, down, o_first = lax.optimization_barrier((up, down, o_first))
    o_edges = jnp.concatenate([o_first, o_last])
    low, high = from_z(up, down)
    sides = y_sides(low, mine, high)
    step, drive = call(first_step_kernel, [outer, block], [room(nz + 8), room(nz + 6)], "first_step")(
        mine, low, high, sides
    )

    o_low, o_high = from_z(
        jnp.concatenate([o_edges[2 * AHEAD - 2 :], end[nz - 2 :]]),
        jnp.concatenate([o_edges[:2], end[:2]]),
    )
    sums = summed(
        call(first_sums_kernel, table, name="first_sums")(o_edges, o_middle, mine, end, drive)
    )
    o_low, o_high, sums = lax.optimization_barrier((o_low, o_high, sums))
    o_sides = y_sides(
        o_low[:2], o_edges[:AHEAD], o_middle, o_edges[AHEAD:], o_high[:2], o_low[2:], end, o_high[2:]
    )
    near, tangent_wide = call(
        other_step_kernel, [block, outer], [room(nz + 4), room(nz + 2)], "other_step"
    )(o_edges, o_middle, end, o_low, o_high, o_sides)

    whole = jax.ShapeDtypeStruct(images.shape, images.dtype)
    moved, drive2, minus, base = call(
        second_step_kernel,
        [block] * 3 + [whole],
        [room(nz + 4), room(nz + 2), DMA],
        "second_step",
        in_specs=[VMEM] * 4 + [ANY],
        out_specs=[VMEM] * 3 + [ANY],
    )(sums, step, tangent_wide, end, source)

    o_sums = lax.ppermute(sums, "image", SWAP)
    sums = call(second_sums_kernel, table, name="second_sums")(
        o_sums, far, mine, near, minus, drive2
    )

    return call(
        functools.partial(last_kernel, cells),
        [whole, shape(2)],
        [pltpu.VMEM(block.shape, jnp.float32), DMA((nz // 4,))],
        "last",
        in_specs=[VMEM] * 6 + [ANY],
        out_specs=[ANY, SMEM],
        input_output_aliases={6: 0},
    )(summed(sums), o_sums, far, mine, near, moved, base)


def body(images):
    layers = lax.axis_size("space")
    pair = lax.axis_size("image") == 2 and lax.axis_size("yslab") == 2 and images.shape[0] == 2
    pair = pair and layers & (layers - 1) == 0 and images.shape[1] % 4 == 0
    pair = pair and images.shape[1] > 2 * AHEAD and images.shape[2] % CHUNK == 0
    return body_pair(images) if pair else body_any(images)


def solution(mesh):
    in_specs = (P(("groups", "image"), "space", "yslab", None),)
    out_specs = (P(("groups", "image"), "space", "yslab", None), P(("groups", "image")))
    return jax.shard_map(body, mesh=mesh, in_specs=in_specs, out_specs=out_specs, check_vma=False)
```

```python
import functools
import math

import jax
import jax.numpy as jnp
from jax import lax
from jax.experimental import pallas as pl
from jax.experimental.pallas import tpu as pltpu
from jax.sharding import PartitionSpec as P

ITERS = 2


GRADIENT_COEF = 1.0
MOBILITY = 0.004
SPRING_K = 1.0
STEP_SIZE = 0.5
EPSILON = 1e-06

PAD = 8
VMEM_ROOM = 2 * 2**20
UNROLL = 4
AHEAD = 2


def passed_along(array, axis, by):
    peers = lax.axis_size(axis)
    pairs = [(i, i + by) for i in range(peers) if 0 <= i + by < peers]
    return lax.ppermute(array, axis, pairs)


def extended(cells, sides, width):
    for axis, dim in sides:
        count = lax.axis_size(axis)
        head = lax.slice_in_dim(cells, 0, width, axis=dim)
        tail = lax.slice_in_dim(cells, cells.shape[dim] - width, cells.shape[dim], axis=dim)
        cells = jnp.concatenate(
            [
                lax.ppermute(tail, axis, [(i, (i + 1) % count) for i in range(count)]),
                cells,
                lax.ppermute(head, axis, [((i + 1) % count, i) for i in range(count)]),
            ],
            axis=dim,
        )
    return cells


def stencil(padded):
    middle = padded[:, 1:-1, 1:-1]
    neighbours = padded[:, 2:, 1:-1] + padded[:, :-2, 1:-1]
    neighbours = neighbours + padded[:, 1:-1, 2:] + padded[:, 1:-1, :-2]
    neighbours = neighbours + jnp.roll(middle, -1, 3) + jnp.roll(middle, 1, 3)
    return neighbours - 6.0 * middle


def sum_cells(field):
    return jnp.sum(field, axis=(1, 2, 3))


def body_any(images):
    current = images
    per_device = current.shape[0]
    total_images = per_device * lax.axis_size("image")
    cell_total = float(
        current.shape[1]
        * lax.axis_size("space")
        * current.shape[2]
        * lax.axis_size("yslab")
        * current.shape[3]
    )
    image_ids = lax.axis_index("image") * per_device + jnp.arange(per_device, dtype=jnp.int32)
    interior = (image_ids > 0) & (image_ids < total_images - 1)
    parallel = jnp.zeros((per_device,), jnp.float32)
    for iteration in range(ITERS):
        next_first = passed_along(current[0], "image", -1)
        prev_last = passed_along(current[-1], "image", 1)
        ahead = jnp.concatenate([current[1:], next_first[None]], 0)
        behind = jnp.concatenate([prev_last[None], current[:-1]], 0)
        forward = ahead - current
        backward = current - behind
        tangent = forward + backward
        plus_sq, minus_sq, tangent_sq = lax.psum(
            (
                sum_cells(forward * forward),
                sum_cells(backward * backward),
                sum_cells(tangent * tangent),
            ),
            ("space", "yslab"),
        )
        wide_pad = extended(current, (("space", 1), ("yslab", 2)), 2)
        inner_field = wide_pad[:, 1:-1, 1:-1]
        potential = (
            inner_field * inner_field * inner_field
            - inner_field
            - GRADIENT_COEF * stencil(wide_pad)
        )
        driving = MOBILITY * stencil(potential)
        parallel_sum = lax.psum(sum_cells(driving * tangent), ("space", "yslab"))
        project_coef = parallel_sum / (tangent_sq + EPSILON)
        spring = (
            SPRING_K * (jnp.sqrt(plus_sq) - jnp.sqrt(minus_sq)) / jnp.sqrt(tangent_sq + EPSILON)
        )
        update = (
            driving
            - project_coef[:, None, None, None] * tangent
            + spring[:, None, None, None] * tangent
        )
        current = jnp.where(interior[:, None, None, None], current + STEP_SIZE * update, current)
        parallel = jnp.where(
            interior, parallel_sum / jnp.sqrt((tangent_sq + EPSILON) * cell_total), jnp.float32(0.0)
        )
    return (current, parallel)


def call(kernel, out_shape, scratch=(), name=None, **kw):
    return pl.pallas_call(
        kernel,
        out_shape=out_shape,
        scratch_shapes=list(scratch),
        name=name,
        compiler_params=pltpu.CompilerParams(
            vmem_limit_bytes=VMEM_ROOM + sum(4 * math.prod(s.shape) for s in scratch if s is not DMA)
        ),
        **kw,
    )


def shape(*dims):
    return jax.ShapeDtypeStruct(dims, jnp.float32)


def lap(below, here, above):
    rows, lanes = here.shape
    ys = pltpu.roll(here, 1, 0) + pltpu.roll(here, rows - 1, 0)
    xs = pltpu.roll(here, 1, 1) + pltpu.roll(here, lanes - 1, 1)
    return (below + above) + ys + xs - 6.0 * here


def layer_loop(start, stop, body):
    def step(k, carry):
        body(k)
        return carry

    lax.fori_loop(start, stop, step, 0, unroll=min(UNROLL, stop - start))


def potentials(field, pot, count):
    def one(k):
        here = field[k + 1]
        pot[k] = here * here * here - here - GRADIENT_COEF * lap(field[k], here, field[k + 2])

    layer_loop(0, count, one)


def driving(pot, k):
    return MOBILITY * lap(pot[k], pot[k + 1], pot[k + 2])


def rows_sum(field):
    rows, lanes = field.shape
    return jnp.sum(field.reshape(rows // 8, 8, lanes), axis=0)


def lane_row(total):
    lanes = total.shape[1]
    folded = jnp.sum(total.reshape(8, lanes // 128, 128), axis=1)
    return jnp.sum(folded, axis=0, keepdims=True)


def fill_padded(dst, pieces, sides, sides_at):
    at = 0
    for piece in pieces:
        layers, rows, _ = piece.shape
        dst[at : at + layers, PAD : PAD + rows] = piece[...]
        at += layers
    dst[:, 0:PAD] = sides[sides_at : sides_at + at, PAD : 2 * PAD]
    dst[:, PAD + rows : 2 * PAD + rows] = sides[sides_at : sides_at + at, 0:PAD]


def all_copied(pairs, sems):
    copies = [pltpu.make_async_copy(src, dst, sems.at[i]) for i, (src, dst) in enumerate(pairs)]
    for c in copies:
        c.start()
    for c in copies:
        c.wait()


def send_kernel(images, edges, middle, sems):
    which = 1 - lax.axis_index("image")
    nz = images.shape[1]
    pairs = [
        (images.at[which, pl.ds(0, AHEAD)], edges.at[pl.ds(0, AHEAD)]),
        (images.at[which, pl.ds(nz - AHEAD, AHEAD)], edges.at[pl.ds(AHEAD, AHEAD)]),
        (images.at[which, pl.ds(AHEAD, nz - 2 * AHEAD)], middle),
    ]
    all_copied(pairs, sems)


def keep_kernel(images, mine, end, up, down, sems):
    which = 1 - lax.axis_index("image")
    nz, layers = mine.shape[0], up.shape[0]
    pairs = [
        (images.at[which, pl.ds(nz - layers, layers)], up),
        (images.at[which, pl.ds(0, layers)], down),
        (images.at[which], mine),
        (images.at[1 - which], end),
    ]
    all_copied(pairs, sems)


def first_step_kernel(mine, low, high, sides, step_out, drive_out, field, pot):
    nz, rows, _ = mine.shape
    fill_padded(field, (low, mine, high), sides, 0)
    potentials(field, pot, nz + 6)

    def edge(k):
        step_out[k] = field[k + 2] + STEP_SIZE * driving(pot, k)

    def inner(k):
        drive = driving(pot, k)
        step_out[k] = field[k + 2] + STEP_SIZE * drive
        drive_out[k - 2] = drive[PAD : PAD + rows]

    layer_loop(0, 2, edge)
    layer_loop(2, nz + 2, inner)
    layer_loop(nz + 2, nz + 4, edge)


CHUNK = 16


def sums_of(start, stop, rows, terms, totals):
    def one(k, totals):
        for r in range(0, rows, CHUNK):
            totals = tuple(t + rows_sum(v) for t, v in zip(totals, terms(k, pl.ds(r, CHUNK))))
        return totals

    return lax.fori_loop(start, stop, one, totals, unroll=True)


def no_sums(count, lanes):
    return (jnp.zeros((8, lanes), jnp.float32),) * count


def table_of(*rows):
    return jnp.concatenate(rows + (jnp.zeros((8 - len(rows), 128), jnp.float32),), 0)


def first_sums_kernel(edges, middle, mine, end, drive, out):
    nz, rows, lanes = mine.shape

    def terms_from(other, shift):
        def terms(k, r):
            m, o, e = mine[k, r], other[k + shift, r], end[k, r]
            plus, minus, tangent = o - m, m - e, o - e
            return plus * plus, minus * minus, tangent * tangent, drive[k, r] * tangent

        return terms

    last = nz - AHEAD
    totals = sums_of(0, AHEAD, rows, terms_from(edges, 0), no_sums(4, lanes))
    totals = sums_of(AHEAD, last, rows, terms_from(middle, -AHEAD), totals)
    totals = sums_of(last, nz, rows, terms_from(edges, AHEAD - last), totals)
    out[...] = table_of(*(lane_row(t) for t in totals))


def coefficient(sums):
    total = jnp.sum(sums[...], axis=1, keepdims=True)
    plus_sq, minus_sq, tangent_sq, par = (total[i : i + 1] for i in range(4))
    safe = tangent_sq + EPSILON
    spring = SPRING_K * (jnp.sqrt(plus_sq) - jnp.sqrt(minus_sq)) / jnp.sqrt(safe)
    return STEP_SIZE * (spring - par / safe), par, safe


def other_step_kernel(edges, middle, end, low, high, sides, near_out, tangent_out, field, pot):
    nz, rows, _ = end.shape
    first, last = edges.at[0:AHEAD], edges.at[AHEAD : 2 * AHEAD]
    fill_padded(field, (low.at[0:2], first, middle, last, high.at[0:2]), sides, 0)
    fill_padded(tangent_out, (low.at[2:4], end, high.at[2:4]), sides, nz + 4)
    potentials(field, pot, nz + 2)

    def widen(k):
        tangent_out[k] = field[k] - tangent_out[k]

    def one(k):
        moved = field[k + 2] + STEP_SIZE * driving(pot, k)
        near_out[k] = moved[PAD : PAD + rows] - end[k]

    layer_loop(0, nz + 4, widen)
    layer_loop(0, nz, one)


def second_step_kernel(
    sums, step, tangent_wide, end, moved_out, drive_out, minus_out, base, field, pot, sem
):
    nz, rows, _ = end.shape
    still = lax.axis_index("image")
    copy = pltpu.make_async_copy(end, base.at[still], sem)
    copy.start()
    coef, _, _ = coefficient(sums)

    def move(k):
        field[k] = step[k] + coef * tangent_wide[k]

    layer_loop(0, nz + 4, move)
    potentials(field, pot, nz + 2)

    def one(k):
        drive = driving(pot, k)[PAD : PAD + rows]
        here = field[k + 2][PAD : PAD + rows]
        drive_out[k] = drive
        minus_out[k] = here - end[k]
        moved_out[k] = here + STEP_SIZE * drive

    layer_loop(0, nz, one)
    copy.wait()


def second_sums_kernel(o_sums, far, mine, near, minus, drive, out):
    nz, rows, lanes = far.shape
    coef, _, _ = coefficient(o_sums)

    def terms(k, r):
        tangent = near[k, r] + coef * (mine[k, r] - far[k, r])
        m = minus[k, r]
        plus = tangent - m
        return plus * plus, m * m, tangent * tangent, drive[k, r] * tangent

    out[...] = table_of(*(lane_row(t) for t in sums_of(0, nz, rows, terms, no_sums(4, lanes))))


def last_kernel(cells, sums, o_sums, far, mine, near, moved, base, out, par_out, buf, sems):
    del base
    nz = moved.shape[0]
    at = lax.axis_index("image")
    which = 1 - at
    coef, par, safe = coefficient(sums)
    o_coef, _, _ = coefficient(o_sums)
    copies = []
    for k in range(nz):
        buf[k] = moved[k] + coef * (near[k] + o_coef * (mine[k] - far[k]))
        if k % 4 == 3:
            where = pl.ds(k - 3, 4)
            copies.append(
                pltpu.make_async_copy(buf.at[where], out.at[which, where], sems.at[k // 4])
            )
            copies[-1].start()
    value = (par / jnp.sqrt(safe * cells))[0, 0]
    sign = jnp.where(at == 0, 1.0, -1.0).astype(jnp.float32)
    par_out[which] = value * sign
    par_out[1 - which] = jnp.float32(0.0)
    for c in copies:
        c.wait()


ANY = pl.BlockSpec(memory_space=pl.ANY)
VMEM = pl.BlockSpec(memory_space=pltpu.VMEM)
SMEM = pl.BlockSpec(memory_space=pltpu.SMEM)
DMA = pltpu.SemaphoreType.DMA
SWAP = [(0, 1), (1, 0)]


def from_z(up, down):
    count = lax.axis_size("space")
    low = lax.ppermute(up, "space", [(i, (i + 1) % count) for i in range(count)])
    high = lax.ppermute(down, "space", [((i + 1) % count, i) for i in range(count)])
    return low, high


def y_sides(*pieces):
    rows = pieces[0].shape[1]
    ends = [jnp.concatenate([p[:, :PAD], p[:, rows - PAD :]], 1) for p in pieces]
    return lax.ppermute(jnp.concatenate(ends, 0), "yslab", SWAP)


def summed(sums):
    sums = sums + lax.ppermute(sums, "yslab", SWAP)
    count, stride = lax.axis_size("space"), 1
    while stride < count:
        sums = sums + lax.ppermute(sums, "space", [(i, i ^ stride) for i in range(count)])
        stride *= 2
    return sums


def body_pair(images):
    _, nz, ny, nx = images.shape
    wide = ny + 2 * PAD
    cells = float(nz * lax.axis_size("space") * ny * lax.axis_size("yslab") * nx)
    block, outer = shape(nz, ny, nx), shape(nz + 4, wide, nx)
    table = shape(8, 128)

    def room(layers):
        return pltpu.VMEM((layers, wide, nx), jnp.float32)

    thin = shape(4, ny, nx)
    source = pltpu.with_memory_space_constraint(images, pltpu.HBM)
    edges, middle = call(
        send_kernel,
        [shape(2 * AHEAD, ny, nx), shape(nz - 2 * AHEAD, ny, nx)],
        [DMA((3,))],
        "send",
        in_specs=[ANY],
        out_specs=[ANY] * 2,
    )(source)
    mine, end, up, down = call(
        keep_kernel,
        [block, block, thin, thin],
        [DMA((4,))],
        "keep",
        in_specs=[ANY],
        out_specs=[ANY] * 4,
    )(source)

    o_first = lax.ppermute(edges[:AHEAD], "image", SWAP)
    o_last = lax.ppermute(edges[AHEAD:], "image", SWAP)
    o_middle = lax.ppermute(middle, "image", SWAP)
    far = lax.ppermute(end, "image", SWAP)

    up, down, o_first = lax.optimization_barrier((up, down, o_first))
    o_edges = jnp.concatenate([o_first, o_last])
    low, high = from_z(up, down)
    sides = y_sides(low, mine, high)
    step, drive = call(first_step_kernel, [outer, block], [room(nz + 8), room(nz + 6)], "first_step")(
        mine, low, high, sides
    )

    o_low, o_high = from_z(
        jnp.concatenate([o_edges[2 * AHEAD - 2 :], end[nz - 2 :]]),
        jnp.concatenate([o_edges[:2], end[:2]]),
    )
    sums = summed(
        call(first_sums_kernel, table, name="first_sums")(o_edges, o_middle, mine, end, drive)
    )
    o_low, o_high, sums = lax.optimization_barrier((o_low, o_high, sums))
    o_sides = y_sides(
        o_low[:2], o_edges[:AHEAD], o_middle, o_edges[AHEAD:], o_high[:2], o_low[2:], end, o_high[2:]
    )
    near, tangent_wide = call(
        other_step_kernel, [block, outer], [room(nz + 4), room(nz + 2)], "other_step"
    )(o_edges, o_middle, end, o_low, o_high, o_sides)

    whole = jax.ShapeDtypeStruct(images.shape, images.dtype)
    moved, drive2, minus, base = call(
        second_step_kernel,
        [block] * 3 + [whole],
        [room(nz + 4), room(nz + 2), DMA],
        "second_step",
        in_specs=[VMEM] * 4,
        out_specs=[VMEM] * 3 + [ANY],
    )(sums, step, tangent_wide, end)

    o_sums = lax.ppermute(sums, "image", SWAP)
    sums = call(second_sums_kernel, table, name="second_sums")(
        o_sums, far, mine, near, minus, drive2
    )

    return call(
        functools.partial(last_kernel, cells),
        [whole, shape(2)],
        [pltpu.VMEM(block.shape, jnp.float32), DMA((nz // 4,))],
        "last",
        in_specs=[VMEM] * 6 + [ANY],
        out_specs=[ANY, SMEM],
        input_output_aliases={6: 0},
    )(summed(sums), o_sums, far, mine, near, moved, base)


def body(images):
    layers = lax.axis_size("space")
    pair = lax.axis_size("image") == 2 and lax.axis_size("yslab") == 2 and images.shape[0] == 2
    pair = pair and layers & (layers - 1) == 0 and images.shape[1] % 4 == 0
    pair = pair and images.shape[1] > 2 * AHEAD and images.shape[2] % CHUNK == 0
    return body_pair(images) if pair else body_any(images)


def solution(mesh):
    in_specs = (P(("groups", "image"), "space", "yslab", None),)
    out_specs = (P(("groups", "image"), "space", "yslab", None), P(("groups", "image")))
    return jax.shard_map(body, mesh=mesh, in_specs=in_specs, out_specs=out_specs, check_vma=False)
```

```python
import functools
import math

import jax
import jax.numpy as jnp
from jax import lax
from jax.experimental import pallas as pl
from jax.experimental.pallas import tpu as pltpu
from jax.sharding import PartitionSpec as P

ITERS = 2


GRADIENT_COEF = 1.0
MOBILITY = 0.004
SPRING_K = 1.0
STEP_SIZE = 0.5
EPSILON = 1e-06

PAD = 8
VMEM_ROOM = 2 * 2**20
UNROLL = 4
AHEAD = 2


def passed_along(array, axis, by):
    peers = lax.axis_size(axis)
    pairs = [(i, i + by) for i in range(peers) if 0 <= i + by < peers]
    return lax.ppermute(array, axis, pairs)


def extended(cells, sides, width):
    for axis, dim in sides:
        count = lax.axis_size(axis)
        head = lax.slice_in_dim(cells, 0, width, axis=dim)
        tail = lax.slice_in_dim(cells, cells.shape[dim] - width, cells.shape[dim], axis=dim)
        cells = jnp.concatenate(
            [
                lax.ppermute(tail, axis, [(i, (i + 1) % count) for i in range(count)]),
                cells,
                lax.ppermute(head, axis, [((i + 1) % count, i) for i in range(count)]),
            ],
            axis=dim,
        )
    return cells


def stencil(padded):
    middle = padded[:, 1:-1, 1:-1]
    neighbours = padded[:, 2:, 1:-1] + padded[:, :-2, 1:-1]
    neighbours = neighbours + padded[:, 1:-1, 2:] + padded[:, 1:-1, :-2]
    neighbours = neighbours + jnp.roll(middle, -1, 3) + jnp.roll(middle, 1, 3)
    return neighbours - 6.0 * middle


def sum_cells(field):
    return jnp.sum(field, axis=(1, 2, 3))


def body_any(images):
    current = images
    per_device = current.shape[0]
    total_images = per_device * lax.axis_size("image")
    cell_total = float(
        current.shape[1]
        * lax.axis_size("space")
        * current.shape[2]
        * lax.axis_size("yslab")
        * current.shape[3]
    )
    image_ids = lax.axis_index("image") * per_device + jnp.arange(per_device, dtype=jnp.int32)
    interior = (image_ids > 0) & (image_ids < total_images - 1)
    parallel = jnp.zeros((per_device,), jnp.float32)
    for iteration in range(ITERS):
        next_first = passed_along(current[0], "image", -1)
        prev_last = passed_along(current[-1], "image", 1)
        ahead = jnp.concatenate([current[1:], next_first[None]], 0)
        behind = jnp.concatenate([prev_last[None], current[:-1]], 0)
        forward = ahead - current
        backward = current - behind
        tangent = forward + backward
        plus_sq, minus_sq, tangent_sq = lax.psum(
            (
                sum_cells(forward * forward),
                sum_cells(backward * backward),
                sum_cells(tangent * tangent),
            ),
            ("space", "yslab"),
        )
        wide_pad = extended(current, (("space", 1), ("yslab", 2)), 2)
        inner_field = wide_pad[:, 1:-1, 1:-1]
        potential = (
            inner_field * inner_field * inner_field
            - inner_field
            - GRADIENT_COEF * stencil(wide_pad)
        )
        driving = MOBILITY * stencil(potential)
        parallel_sum = lax.psum(sum_cells(driving * tangent), ("space", "yslab"))
        project_coef = parallel_sum / (tangent_sq + EPSILON)
        spring = (
            SPRING_K * (jnp.sqrt(plus_sq) - jnp.sqrt(minus_sq)) / jnp.sqrt(tangent_sq + EPSILON)
        )
        update = (
            driving
            - project_coef[:, None, None, None] * tangent
            + spring[:, None, None, None] * tangent
        )
        current = jnp.where(interior[:, None, None, None], current + STEP_SIZE * update, current)
        parallel = jnp.where(
            interior, parallel_sum / jnp.sqrt((tangent_sq + EPSILON) * cell_total), jnp.float32(0.0)
        )
    return (current, parallel)


def call(kernel, out_shape, scratch=(), name=None, **kw):
    return pl.pallas_call(
        kernel,
        out_shape=out_shape,
        scratch_shapes=list(scratch),
        name=name,
        compiler_params=pltpu.CompilerParams(
            vmem_limit_bytes=VMEM_ROOM + sum(4 * math.prod(s.shape) for s in scratch if s is not DMA)
        ),
        **kw,
    )


def shape(*dims):
    return jax.ShapeDtypeStruct(dims, jnp.float32)


def lap(below, here, above):
    rows, lanes = here.shape
    ys = pltpu.roll(here, 1, 0) + pltpu.roll(here, rows - 1, 0)
    xs = pltpu.roll(here, 1, 1) + pltpu.roll(here, lanes - 1, 1)
    return (below + above) + ys + xs - 6.0 * here


def layer_loop(start, stop, body):
    def step(k, carry):
        body(k)
        return carry

    lax.fori_loop(start, stop, step, 0, unroll=min(UNROLL, stop - start))


def potentials(field, pot, count):
    def one(k):
        here = field[k + 1]
        pot[k] = here * here * here - here - GRADIENT_COEF * lap(field[k], here, field[k + 2])

    layer_loop(0, count, one)


def driving(pot, k):
    return MOBILITY * lap(pot[k], pot[k + 1], pot[k + 2])


def rows_sum(field):
    rows, lanes = field.shape
    return jnp.sum(field.reshape(rows // 8, 8, lanes), axis=0)


def lane_row(total):
    lanes = total.shape[1]
    folded = jnp.sum(total.reshape(8, lanes // 128, 128), axis=1)
    return jnp.sum(folded, axis=0, keepdims=True)


def fill_padded(dst, pieces, sides, sides_at):
    at = 0
    for piece in pieces:
        layers, rows, _ = piece.shape
        dst[at : at + layers, PAD : PAD + rows] = piece[...]
        at += layers
    dst[:, 0:PAD] = sides[sides_at : sides_at + at, PAD : 2 * PAD]
    dst[:, PAD + rows : 2 * PAD + rows] = sides[sides_at : sides_at + at, 0:PAD]


def all_copied(pairs, sems):
    copies = [pltpu.make_async_copy(src, dst, sems.at[i]) for i, (src, dst) in enumerate(pairs)]
    for c in copies:
        c.start()
    for c in copies:
        c.wait()


def send_kernel(images, edges, middle, sems):
    which = 1 - lax.axis_index("image")
    nz = images.shape[1]
    pairs = [
        (images.at[which, pl.ds(0, AHEAD)], edges.at[pl.ds(0, AHEAD)]),
        (images.at[which, pl.ds(nz - AHEAD, AHEAD)], edges.at[pl.ds(AHEAD, AHEAD)]),
        (images.at[which, pl.ds(AHEAD, nz - 2 * AHEAD)], middle),
    ]
    all_copied(pairs, sems)


def keep_kernel(images, mine, end, up, down, sems):
    which = 1 - lax.axis_index("image")
    nz, layers = mine.shape[0], up.shape[0]
    pairs = [
        (images.at[which, pl.ds(nz - layers, layers)], up),
        (images.at[which, pl.ds(0, layers)], down),
        (images.at[which], mine),
        (images.at[1 - which], end),
    ]
    all_copied(pairs, sems)


def first_step_kernel(mine, low, high, sides, step_out, drive_out, field, pot):
    nz, rows, _ = mine.shape
    fill_padded(field, (low, mine, high), sides, 0)
    potentials(field, pot, nz + 6)

    def edge(k):
        step_out[k] = field[k + 2] + STEP_SIZE * driving(pot, k)

    def inner(k):
        drive = driving(pot, k)
        step_out[k] = field[k + 2] + STEP_SIZE * drive
        drive_out[k - 2] = drive[PAD : PAD + rows]

    layer_loop(0, 2, edge)
    layer_loop(2, nz + 2, inner)
    layer_loop(nz + 2, nz + 4, edge)


CHUNK = 16


def sums_of(start, stop, rows, terms, totals):
    def one(k, totals):
        for r in range(0, rows, CHUNK):
            totals = tuple(t + rows_sum(v) for t, v in zip(totals, terms(k, pl.ds(r, CHUNK))))
        return totals

    return lax.fori_loop(start, stop, one, totals, unroll=True)


def no_sums(count, lanes):
    return (jnp.zeros((8, lanes), jnp.float32),) * count


def table_of(*rows):
    return jnp.concatenate(rows + (jnp.zeros((8 - len(rows), 128), jnp.float32),), 0)


def first_sums_kernel(edges, middle, mine, end, drive, out):
    nz, rows, lanes = mine.shape

    def terms_from(other, shift):
        def terms(k, r):
            m, o, e = mine[k, r], other[k + shift, r], end[k, r]
            plus, minus, tangent = o - m, m - e, o - e
            return plus * plus, minus * minus, tangent * tangent, drive[k, r] * tangent

        return terms

    last = nz - AHEAD
    totals = sums_of(0, AHEAD, rows, terms_from(edges, 0), no_sums(4, lanes))
    totals = sums_of(AHEAD, last, rows, terms_from(middle, -AHEAD), totals)
    totals = sums_of(last, nz, rows, terms_from(edges, AHEAD - last), totals)
    out[...] = table_of(*(lane_row(t) for t in totals))


def coefficient(sums):
    total = jnp.sum(sums[...], axis=1, keepdims=True)
    plus_sq, minus_sq, tangent_sq, par = (total[i : i + 1] for i in range(4))
    safe = tangent_sq + EPSILON
    spring = SPRING_K * (jnp.sqrt(plus_sq) - jnp.sqrt(minus_sq)) / jnp.sqrt(safe)
    return STEP_SIZE * (spring - par / safe), par, safe


def other_step_kernel(edges, middle, end, low, high, sides, near_out, tangent_out, field, pot):
    nz, rows, _ = end.shape
    first, last = edges.at[0:AHEAD], edges.at[AHEAD : 2 * AHEAD]
    fill_padded(field, (low.at[0:2], first, middle, last, high.at[0:2]), sides, 0)
    fill_padded(tangent_out, (low.at[2:4], end, high.at[2:4]), sides, nz + 4)
    potentials(field, pot, nz + 2)

    def widen(k):
        tangent_out[k] = field[k] - tangent_out[k]

    def one(k):
        moved = field[k + 2] + STEP_SIZE * driving(pot, k)
        near_out[k] = moved[PAD : PAD + rows] - end[k]

    layer_loop(0, nz + 4, widen)
    layer_loop(0, nz, one)


def second_step_kernel(
    sums, step, tangent_wide, end, moved_out, drive_out, minus_out, base, field, pot, sem
):
    nz, rows, _ = end.shape
    still = lax.axis_index("image")
    copy = pltpu.make_async_copy(end, base.at[still], sem)
    copy.start()
    coef, _, _ = coefficient(sums)

    def move(k):
        field[k] = step[k] + coef * tangent_wide[k]

    layer_loop(0, nz + 4, move)
    potentials(field, pot, nz + 2)

    def one(k):
        drive = driving(pot, k)[PAD : PAD + rows]
        here = field[k + 2][PAD : PAD + rows]
        drive_out[k] = drive
        minus_out[k] = here - end[k]
        moved_out[k] = here + STEP_SIZE * drive

    layer_loop(0, nz, one)
    copy.wait()


def second_sums_kernel(o_sums, far, mine, near, minus, drive, out):
    nz, rows, lanes = far.shape
    coef, _, _ = coefficient(o_sums)

    def terms(k, r):
        tangent = near[k, r] + coef * (mine[k, r] - far[k, r])
        m = minus[k, r]
        plus = tangent - m
        return plus * plus, m * m, tangent * tangent, drive[k, r] * tangent

    out[...] = table_of(*(lane_row(t) for t in sums_of(0, nz, rows, terms, no_sums(4, lanes))))


def last_kernel(cells, sums, o_sums, far, mine, near, moved, base, out, par_out, buf, sems):
    del base
    nz = moved.shape[0]
    at = lax.axis_index("image")
    which = 1 - at
    coef, par, safe = coefficient(sums)
    o_coef, _, _ = coefficient(o_sums)
    copies = []
    for k in range(nz):
        buf[k] = moved[k] + coef * (near[k] + o_coef * (mine[k] - far[k]))
        if k % 4 == 3:
            where = pl.ds(k - 3, 4)
            copies.append(
                pltpu.make_async_copy(buf.at[where], out.at[which, where], sems.at[k // 4])
            )
            copies[-1].start()
    value = (par / jnp.sqrt(safe * cells))[0, 0]
    sign = jnp.where(at == 0, 1.0, -1.0).astype(jnp.float32)
    par_out[which] = value * sign
    par_out[1 - which] = jnp.float32(0.0)
    for c in copies:
        c.wait()


ANY = pl.BlockSpec(memory_space=pl.ANY)
VMEM = pl.BlockSpec(memory_space=pltpu.VMEM)
SMEM = pl.BlockSpec(memory_space=pltpu.SMEM)
DMA = pltpu.SemaphoreType.DMA
SWAP = [(0, 1), (1, 0)]


def from_z(up, down):
    count = lax.axis_size("space")
    low = lax.ppermute(up, "space", [(i, (i + 1) % count) for i in range(count)])
    high = lax.ppermute(down, "space", [((i + 1) % count, i) for i in range(count)])
    return low, high


def y_sides(*pieces):
    rows = pieces[0].shape[1]
    ends = [jnp.concatenate([p[:, :PAD], p[:, rows - PAD :]], 1) for p in pieces]
    return lax.ppermute(jnp.concatenate(ends, 0), "yslab", SWAP)


def sum_steps():
    count, stride = lax.axis_size("space"), 1
    steps = [("yslab", SWAP)]
    while stride < count:
        steps.append(("space", [(i, i ^ stride) for i in range(count)]))
        stride *= 2
    return steps


def summed(sums, steps):
    for axis, pairs in steps:
        sums = sums + lax.ppermute(sums, axis, pairs)
    return sums


def body_pair(images):
    _, nz, ny, nx = images.shape
    wide = ny + 2 * PAD
    cells = float(nz * lax.axis_size("space") * ny * lax.axis_size("yslab") * nx)
    block, outer = shape(nz, ny, nx), shape(nz + 4, wide, nx)
    table = shape(8, 128)

    def room(layers):
        return pltpu.VMEM((layers, wide, nx), jnp.float32)

    thin = shape(4, ny, nx)
    source = pltpu.with_memory_space_constraint(images, pltpu.HBM)
    edges, middle = call(
        send_kernel,
        [shape(2 * AHEAD, ny, nx), shape(nz - 2 * AHEAD, ny, nx)],
        [DMA((3,))],
        "send",
        in_specs=[ANY],
        out_specs=[ANY] * 2,
    )(source)
    mine, end, up, down = call(
        keep_kernel,
        [block, block, thin, thin],
        [DMA((4,))],
        "keep",
        in_specs=[ANY],
        out_specs=[ANY] * 4,
    )(source)

    o_first = lax.ppermute(edges[:AHEAD], "image", SWAP)
    o_last = lax.ppermute(edges[AHEAD:], "image", SWAP)
    o_middle = lax.ppermute(middle, "image", SWAP)
    far = lax.ppermute(end, "image", SWAP)

    up, down, o_first = lax.optimization_barrier((up, down, o_first))
    o_edges = jnp.concatenate([o_first, o_last])
    low, high = from_z(up, down)
    sides = y_sides(low, mine, high)
    step, drive = call(first_step_kernel, [outer, block], [room(nz + 8), room(nz + 6)], "first_step")(
        mine, low, high, sides
    )

    o_low, o_high = from_z(
        jnp.concatenate([o_edges[2 * AHEAD - 2 :], end[nz - 2 :]]),
        jnp.concatenate([o_edges[:2], end[:2]]),
    )
    sums = call(first_sums_kernel, table, name="first_sums")(o_edges, o_middle, mine, end, drive)
    steps = sum_steps()
    sums = summed(sums, steps[:2])
    o_low, o_high, sums = lax.optimization_barrier((o_low, o_high, sums))
    o_sides = y_sides(
        o_low[:2], o_edges[:AHEAD], o_middle, o_edges[AHEAD:], o_high[:2], o_low[2:], end, o_high[2:]
    )
    sums = summed(sums, steps[2:])
    near, tangent_wide = call(
        other_step_kernel, [block, outer], [room(nz + 4), room(nz + 2)], "other_step"
    )(o_edges, o_middle, end, o_low, o_high, o_sides)

    whole = jax.ShapeDtypeStruct(images.shape, images.dtype)
    moved, drive2, minus, base = call(
        second_step_kernel,
        [block] * 3 + [whole],
        [room(nz + 4), room(nz + 2), DMA],
        "second_step",
        in_specs=[VMEM] * 4,
        out_specs=[VMEM] * 3 + [ANY],
    )(sums, step, tangent_wide, end)

    o_sums = lax.ppermute(sums, "image", SWAP)
    sums = call(second_sums_kernel, table, name="second_sums")(
        o_sums, far, mine, near, minus, drive2
    )

    return call(
        functools.partial(last_kernel, cells),
        [whole, shape(2)],
        [pltpu.VMEM(block.shape, jnp.float32), DMA((nz // 4,))],
        "last",
        in_specs=[VMEM] * 6 + [ANY],
        out_specs=[ANY, SMEM],
        input_output_aliases={6: 0},
    )(summed(sums, sum_steps()), o_sums, far, mine, near, moved, base)


def body(images):
    layers = lax.axis_size("space")
    pair = lax.axis_size("image") == 2 and lax.axis_size("yslab") == 2 and images.shape[0] == 2
    pair = pair and layers & (layers - 1) == 0 and images.shape[1] % 4 == 0
    pair = pair and images.shape[1] > 2 * AHEAD and images.shape[2] % CHUNK == 0
    return body_pair(images) if pair else body_any(images)


def solution(mesh):
    in_specs = (P(("groups", "image"), "space", "yslab", None),)
    out_specs = (P(("groups", "image"), "space", "yslab", None), P(("groups", "image")))
    return jax.shard_map(body, mesh=mesh, in_specs=in_specs, out_specs=out_specs, check_vma=False)
```

```python
import functools
import math

import jax
import jax.numpy as jnp
from jax import lax
from jax.experimental import pallas as pl
from jax.experimental.pallas import tpu as pltpu
from jax.sharding import PartitionSpec as P

ITERS = 2


GRADIENT_COEF = 1.0
MOBILITY = 0.004
SPRING_K = 1.0
STEP_SIZE = 0.5
EPSILON = 1e-06

PAD = 8
VMEM_ROOM = 2 * 2**20
UNROLL = 4
AHEAD = 2


def passed_along(array, axis, by):
    peers = lax.axis_size(axis)
    pairs = [(i, i + by) for i in range(peers) if 0 <= i + by < peers]
    return lax.ppermute(array, axis, pairs)


def extended(cells, sides, width):
    for axis, dim in sides:
        count = lax.axis_size(axis)
        head = lax.slice_in_dim(cells, 0, width, axis=dim)
        tail = lax.slice_in_dim(cells, cells.shape[dim] - width, cells.shape[dim], axis=dim)
        cells = jnp.concatenate(
            [
                lax.ppermute(tail, axis, [(i, (i + 1) % count) for i in range(count)]),
                cells,
                lax.ppermute(head, axis, [((i + 1) % count, i) for i in range(count)]),
            ],
            axis=dim,
        )
    return cells


def stencil(padded):
    middle = padded[:, 1:-1, 1:-1]
    neighbours = padded[:, 2:, 1:-1] + padded[:, :-2, 1:-1]
    neighbours = neighbours + padded[:, 1:-1, 2:] + padded[:, 1:-1, :-2]
    neighbours = neighbours + jnp.roll(middle, -1, 3) + jnp.roll(middle, 1, 3)
    return neighbours - 6.0 * middle


def sum_cells(field):
    return jnp.sum(field, axis=(1, 2, 3))


def body_any(images):
    current = images
    per_device = current.shape[0]
    total_images = per_device * lax.axis_size("image")
    cell_total = float(
        current.shape[1]
        * lax.axis_size("space")
        * current.shape[2]
        * lax.axis_size("yslab")
        * current.shape[3]
    )
    image_ids = lax.axis_index("image") * per_device + jnp.arange(per_device, dtype=jnp.int32)
    interior = (image_ids > 0) & (image_ids < total_images - 1)
    parallel = jnp.zeros((per_device,), jnp.float32)
    for iteration in range(ITERS):
        next_first = passed_along(current[0], "image", -1)
        prev_last = passed_along(current[-1], "image", 1)
        ahead = jnp.concatenate([current[1:], next_first[None]], 0)
        behind = jnp.concatenate([prev_last[None], current[:-1]], 0)
        forward = ahead - current
        backward = current - behind
        tangent = forward + backward
        plus_sq, minus_sq, tangent_sq = lax.psum(
            (
                sum_cells(forward * forward),
                sum_cells(backward * backward),
                sum_cells(tangent * tangent),
            ),
            ("space", "yslab"),
        )
        wide_pad = extended(current, (("space", 1), ("yslab", 2)), 2)
        inner_field = wide_pad[:, 1:-1, 1:-1]
        potential = (
            inner_field * inner_field * inner_field
            - inner_field
            - GRADIENT_COEF * stencil(wide_pad)
        )
        driving = MOBILITY * stencil(potential)
        parallel_sum = lax.psum(sum_cells(driving * tangent), ("space", "yslab"))
        project_coef = parallel_sum / (tangent_sq + EPSILON)
        spring = (
            SPRING_K * (jnp.sqrt(plus_sq) - jnp.sqrt(minus_sq)) / jnp.sqrt(tangent_sq + EPSILON)
        )
        update = (
            driving
            - project_coef[:, None, None, None] * tangent
            + spring[:, None, None, None] * tangent
        )
        current = jnp.where(interior[:, None, None, None], current + STEP_SIZE * update, current)
        parallel = jnp.where(
            interior, parallel_sum / jnp.sqrt((tangent_sq + EPSILON) * cell_total), jnp.float32(0.0)
        )
    return (current, parallel)


def call(kernel, out_shape, scratch=(), name=None, **kw):
    return pl.pallas_call(
        kernel,
        out_shape=out_shape,
        scratch_shapes=list(scratch),
        name=name,
        compiler_params=pltpu.CompilerParams(
            vmem_limit_bytes=VMEM_ROOM + sum(4 * math.prod(s.shape) for s in scratch if s is not DMA)
        ),
        **kw,
    )


def shape(*dims):
    return jax.ShapeDtypeStruct(dims, jnp.float32)


def lap(below, here, above):
    rows, lanes = here.shape
    ys = pltpu.roll(here, 1, 0) + pltpu.roll(here, rows - 1, 0)
    xs = pltpu.roll(here, 1, 1) + pltpu.roll(here, lanes - 1, 1)
    return (below + above) + ys + xs - 6.0 * here


def layer_loop(start, stop, body):
    def step(k, carry):
        body(k)
        return carry

    lax.fori_loop(start, stop, step, 0, unroll=min(UNROLL, stop - start))


def potentials(field, pot, count):
    def one(k):
        here = field[k + 1]
        pot[k] = here * here * here - here - GRADIENT_COEF * lap(field[k], here, field[k + 2])

    layer_loop(0, count, one)


def driving(pot, k):
    return MOBILITY * lap(pot[k], pot[k + 1], pot[k + 2])


def rows_sum(field):
    rows, lanes = field.shape
    return jnp.sum(field.reshape(rows // 8, 8, lanes), axis=0)


def lane_row(total):
    lanes = total.shape[1]
    folded = jnp.sum(total.reshape(8, lanes // 128, 128), axis=1)
    return jnp.sum(folded, axis=0, keepdims=True)


def fill_padded(dst, pieces, sides, sides_at):
    at = 0
    for piece in pieces:
        layers, rows, _ = piece.shape
        dst[at : at + layers, PAD : PAD + rows] = piece[...]
        at += layers
    dst[:, 0:PAD] = sides[sides_at : sides_at + at, PAD : 2 * PAD]
    dst[:, PAD + rows : 2 * PAD + rows] = sides[sides_at : sides_at + at, 0:PAD]


def all_copied(pairs, sems):
    copies = [pltpu.make_async_copy(src, dst, sems.at[i]) for i, (src, dst) in enumerate(pairs)]
    for c in copies:
        c.start()
    for c in copies:
        c.wait()


def send_kernel(images, edges, middle, sems):
    which = 1 - lax.axis_index("image")
    nz = images.shape[1]
    pairs = [
        (images.at[which, pl.ds(0, AHEAD)], edges.at[pl.ds(0, AHEAD)]),
        (images.at[which, pl.ds(nz - AHEAD, AHEAD)], edges.at[pl.ds(AHEAD, AHEAD)]),
        (images.at[which, pl.ds(AHEAD, nz - 2 * AHEAD)], middle),
    ]
    all_copied(pairs, sems)


def keep_kernel(images, mine, end, up, down, sems):
    which = 1 - lax.axis_index("image")
    nz, layers = mine.shape[0], up.shape[0]
    pairs = [
        (images.at[which, pl.ds(nz - layers, layers)], up),
        (images.at[which, pl.ds(0, layers)], down),
        (images.at[which], mine),
        (images.at[1 - which], end),
    ]
    all_copied(pairs, sems)


def first_step_kernel(mine, low, high, sides, step_out, drive_out, field, pot):
    nz, rows, _ = mine.shape
    fill_padded(field, (low, mine, high), sides, 0)
    potentials(field, pot, nz + 6)

    def edge(k):
        step_out[k] = field[k + 2] + STEP_SIZE * driving(pot, k)

    def inner(k):
        drive = driving(pot, k)
        step_out[k] = field[k + 2] + STEP_SIZE * drive
        drive_out[k - 2] = drive[PAD : PAD + rows]

    layer_loop(0, 2, edge)
    layer_loop(2, nz + 2, inner)
    layer_loop(nz + 2, nz + 4, edge)


CHUNK = 16


def sums_of(start, stop, rows, terms, totals):
    def one(k, totals):
        for r in range(0, rows, CHUNK):
            totals = tuple(t + rows_sum(v) for t, v in zip(totals, terms(k, pl.ds(r, CHUNK))))
        return totals

    return lax.fori_loop(start, stop, one, totals, unroll=True)


def no_sums(count, lanes):
    return (jnp.zeros((8, lanes), jnp.float32),) * count


def table_of(*rows):
    return jnp.concatenate(rows + (jnp.zeros((8 - len(rows), 128), jnp.float32),), 0)


def first_sums_kernel(edges, middle, mine, end, drive, out):
    nz, rows, lanes = mine.shape

    def terms_from(other, shift):
        def terms(k, r):
            m, o, e = mine[k, r], other[k + shift, r], end[k, r]
            plus, minus, tangent = o - m, m - e, o - e
            return plus * plus, minus * minus, tangent * tangent, drive[k, r] * tangent

        return terms

    last = nz - AHEAD
    totals = sums_of(0, AHEAD, rows, terms_from(edges, 0), no_sums(4, lanes))
    totals = sums_of(AHEAD, last, rows, terms_from(middle, -AHEAD), totals)
    totals = sums_of(last, nz, rows, terms_from(edges, AHEAD - last), totals)
    out[...] = table_of(*(lane_row(t) for t in totals))


def coefficient(sums):
    total = jnp.sum(sums[...], axis=1, keepdims=True)
    plus_sq, minus_sq, tangent_sq, par = (total[i : i + 1] for i in range(4))
    safe = tangent_sq + EPSILON
    spring = SPRING_K * (jnp.sqrt(plus_sq) - jnp.sqrt(minus_sq)) / jnp.sqrt(safe)
    return STEP_SIZE * (spring - par / safe), par, safe


def other_step_kernel(edges, middle, end, low, high, sides, near_out, tangent_out, field, pot):
    nz, rows, _ = end.shape
    first, last = edges.at[0:AHEAD], edges.at[AHEAD : 2 * AHEAD]
    fill_padded(field, (low.at[0:2], first, middle, last, high.at[0:2]), sides, 0)
    fill_padded(tangent_out, (low.at[2:4], end, high.at[2:4]), sides, nz + 4)
    potentials(field, pot, nz + 2)

    def widen(k):
        tangent_out[k] = field[k] - tangent_out[k]

    def one(k):
        moved = field[k + 2] + STEP_SIZE * driving(pot, k)
        near_out[k] = moved[PAD : PAD + rows] - end[k]

    layer_loop(0, nz + 4, widen)
    layer_loop(0, nz, one)


def second_step_kernel(
    sums, step, tangent_wide, end, moved_out, drive_out, minus_out, base, field, pot, sem
):
    nz, rows, _ = end.shape
    still = lax.axis_index("image")
    copy = pltpu.make_async_copy(end, base.at[still], sem)
    copy.start()
    coef, _, _ = coefficient(sums)

    def move(k):
        field[k] = step[k] + coef * tangent_wide[k]

    layer_loop(0, nz + 4, move)
    potentials(field, pot, nz + 2)

    def one(k):
        drive = driving(pot, k)[PAD : PAD + rows]
        here = field[k + 2][PAD : PAD + rows]
        drive_out[k] = drive
        minus_out[k] = here - end[k]
        moved_out[k] = here + STEP_SIZE * drive

    layer_loop(0, nz, one)
    copy.wait()


def second_sums_kernel(o_sums, far, mine, near, minus, drive, out):
    nz, rows, lanes = far.shape
    coef, _, _ = coefficient(o_sums)

    def terms(k, r):
        tangent = near[k, r] + coef * (mine[k, r] - far[k, r])
        m = minus[k, r]
        plus = tangent - m
        return plus * plus, m * m, tangent * tangent, drive[k, r] * tangent

    out[...] = table_of(*(lane_row(t) for t in sums_of(0, nz, rows, terms, no_sums(4, lanes))))


def last_kernel(cells, sums, o_sums, far, mine, near, moved, base, out, par_out, buf, sems):
    del base
    nz = moved.shape[0]
    at = lax.axis_index("image")
    which = 1 - at
    coef, par, safe = coefficient(sums)
    o_coef, _, _ = coefficient(o_sums)
    copies = []
    for k in range(nz):
        buf[k] = moved[k] + coef * (near[k] + o_coef * (mine[k] - far[k]))
        if k % 4 == 3:
            where = pl.ds(k - 3, 4)
            copies.append(
                pltpu.make_async_copy(buf.at[where], out.at[which, where], sems.at[k // 4])
            )
            copies[-1].start()
    value = (par / jnp.sqrt(safe * cells))[0, 0]
    sign = jnp.where(at == 0, 1.0, -1.0).astype(jnp.float32)
    par_out[which] = value * sign
    par_out[1 - which] = jnp.float32(0.0)
    for c in copies:
        c.wait()


ANY = pl.BlockSpec(memory_space=pl.ANY)
VMEM = pl.BlockSpec(memory_space=pltpu.VMEM)
SMEM = pl.BlockSpec(memory_space=pltpu.SMEM)
DMA = pltpu.SemaphoreType.DMA
SWAP = [(0, 1), (1, 0)]


def from_z(up, down):
    count = lax.axis_size("space")
    low = lax.ppermute(up, "space", [(i, (i + 1) % count) for i in range(count)])
    high = lax.ppermute(down, "space", [((i + 1) % count, i) for i in range(count)])
    return low, high


def y_sides(*pieces):
    rows = pieces[0].shape[1]
    ends = [jnp.concatenate([p[:, :PAD], p[:, rows - PAD :]], 1) for p in pieces]
    return lax.ppermute(jnp.concatenate(ends, 0), "yslab", SWAP)


def sum_steps():
    count, stride = lax.axis_size("space"), 1
    steps = [("yslab", SWAP)]
    while stride < count:
        steps.append(("space", [(i, i ^ stride) for i in range(count)]))
        stride *= 2
    return steps


def summed(sums, steps):
    for axis, pairs in steps:
        sums = sums + lax.ppermute(sums, axis, pairs)
    return sums


def body_pair(images):
    _, nz, ny, nx = images.shape
    wide = ny + 2 * PAD
    cells = float(nz * lax.axis_size("space") * ny * lax.axis_size("yslab") * nx)
    block, outer = shape(nz, ny, nx), shape(nz + 4, wide, nx)
    table = shape(8, 128)

    def room(layers):
        return pltpu.VMEM((layers, wide, nx), jnp.float32)

    thin = shape(4, ny, nx)
    source = pltpu.with_memory_space_constraint(images, pltpu.HBM)
    edges, middle = call(
        send_kernel,
        [shape(2 * AHEAD, ny, nx), shape(nz - 2 * AHEAD, ny, nx)],
        [DMA((3,))],
        "send",
        in_specs=[ANY],
        out_specs=[ANY] * 2,
    )(source)
    mine, end, up, down = call(
        keep_kernel,
        [block, block, thin, thin],
        [DMA((4,))],
        "keep",
        in_specs=[ANY],
        out_specs=[ANY] * 4,
    )(source)

    o_first = lax.ppermute(edges[:AHEAD], "image", SWAP)
    o_last = lax.ppermute(edges[AHEAD:], "image", SWAP)
    o_middle = lax.ppermute(middle, "image", SWAP)
    far = lax.ppermute(end, "image", SWAP)

    up, down, o_first = lax.optimization_barrier((up, down, o_first))
    o_edges = jnp.concatenate([o_first, o_last])
    low, high = from_z(up, down)
    sides = y_sides(low, mine, high)
    step, drive = call(first_step_kernel, [outer, block], [room(nz + 8), room(nz + 6)], "first_step")(
        mine, low, high, sides
    )

    o_edges, low, high = lax.optimization_barrier((o_edges, low, high))
    o_low, o_high = from_z(
        jnp.concatenate([o_edges[2 * AHEAD - 2 :], end[nz - 2 :]]),
        jnp.concatenate([o_edges[:2], end[:2]]),
    )
    sums = call(first_sums_kernel, table, name="first_sums")(o_edges, o_middle, mine, end, drive)
    steps = sum_steps()
    sums = summed(sums, steps[:2])
    o_low, o_high, sums = lax.optimization_barrier((o_low, o_high, sums))
    o_sides = y_sides(
        o_low[:2], o_edges[:AHEAD], o_middle, o_edges[AHEAD:], o_high[:2], o_low[2:], end, o_high[2:]
    )
    sums = summed(sums, steps[2:])
    near, tangent_wide = call(
        other_step_kernel, [block, outer], [room(nz + 4), room(nz + 2)], "other_step"
    )(o_edges, o_middle, end, o_low, o_high, o_sides)

    whole = jax.ShapeDtypeStruct(images.shape, images.dtype)
    moved, drive2, minus, base = call(
        second_step_kernel,
        [block] * 3 + [whole],
        [room(nz + 4), room(nz + 2), DMA],
        "second_step",
        in_specs=[VMEM] * 4,
        out_specs=[VMEM] * 3 + [ANY],
    )(sums, step, tangent_wide, end)

    o_sums = lax.ppermute(sums, "image", SWAP)
    sums = call(second_sums_kernel, table, name="second_sums")(
        o_sums, far, mine, near, minus, drive2
    )

    return call(
        functools.partial(last_kernel, cells),
        [whole, shape(2)],
        [pltpu.VMEM(block.shape, jnp.float32), DMA((nz // 4,))],
        "last",
        in_specs=[VMEM] * 6 + [ANY],
        out_specs=[ANY, SMEM],
        input_output_aliases={6: 0},
    )(summed(sums, sum_steps()), o_sums, far, mine, near, moved, base)


def body(images):
    layers = lax.axis_size("space")
    pair = lax.axis_size("image") == 2 and lax.axis_size("yslab") == 2 and images.shape[0] == 2
    pair = pair and layers & (layers - 1) == 0 and images.shape[1] % 4 == 0
    pair = pair and images.shape[1] > 2 * AHEAD and images.shape[2] % CHUNK == 0
    return body_pair(images) if pair else body_any(images)


def solution(mesh):
    in_specs = (P(("groups", "image"), "space", "yslab", None),)
    out_specs = (P(("groups", "image"), "space", "yslab", None), P(("groups", "image")))
    return jax.shard_map(body, mesh=mesh, in_specs=in_specs, out_specs=out_specs, check_vma=False)
```

```python
import functools
import math

import jax
import jax.numpy as jnp
from jax import lax
from jax.experimental import pallas as pl
from jax.experimental.pallas import tpu as pltpu
from jax.sharding import PartitionSpec as P

ITERS = 2


GRADIENT_COEF = 1.0
MOBILITY = 0.004
SPRING_K = 1.0
STEP_SIZE = 0.5
EPSILON = 1e-06

PAD = 8
VMEM_ROOM = 2 * 2**20
UNROLL = 4
AHEAD = 2


def passed_along(array, axis, by):
    peers = lax.axis_size(axis)
    pairs = [(i, i + by) for i in range(peers) if 0 <= i + by < peers]
    return lax.ppermute(array, axis, pairs)


def extended(cells, sides, width):
    for axis, dim in sides:
        count = lax.axis_size(axis)
        head = lax.slice_in_dim(cells, 0, width, axis=dim)
        tail = lax.slice_in_dim(cells, cells.shape[dim] - width, cells.shape[dim], axis=dim)
        cells = jnp.concatenate(
            [
                lax.ppermute(tail, axis, [(i, (i + 1) % count) for i in range(count)]),
                cells,
                lax.ppermute(head, axis, [((i + 1) % count, i) for i in range(count)]),
            ],
            axis=dim,
        )
    return cells


def stencil(padded):
    middle = padded[:, 1:-1, 1:-1]
    neighbours = padded[:, 2:, 1:-1] + padded[:, :-2, 1:-1]
    neighbours = neighbours + padded[:, 1:-1, 2:] + padded[:, 1:-1, :-2]
    neighbours = neighbours + jnp.roll(middle, -1, 3) + jnp.roll(middle, 1, 3)
    return neighbours - 6.0 * middle


def sum_cells(field):
    return jnp.sum(field, axis=(1, 2, 3))


def body_any(images):
    current = images
    per_device = current.shape[0]
    total_images = per_device * lax.axis_size("image")
    cell_total = float(
        current.shape[1]
        * lax.axis_size("space")
        * current.shape[2]
        * lax.axis_size("yslab")
        * current.shape[3]
    )
    image_ids = lax.axis_index("image") * per_device + jnp.arange(per_device, dtype=jnp.int32)
    interior = (image_ids > 0) & (image_ids < total_images - 1)
    parallel = jnp.zeros((per_device,), jnp.float32)
    for iteration in range(ITERS):
        next_first = passed_along(current[0], "image", -1)
        prev_last = passed_along(current[-1], "image", 1)
        ahead = jnp.concatenate([current[1:], next_first[None]], 0)
        behind = jnp.concatenate([prev_last[None], current[:-1]], 0)
        forward = ahead - current
        backward = current - behind
        tangent = forward + backward
        plus_sq, minus_sq, tangent_sq = lax.psum(
            (
                sum_cells(forward * forward),
                sum_cells(backward * backward),
                sum_cells(tangent * tangent),
            ),
            ("space", "yslab"),
        )
        wide_pad = extended(current, (("space", 1), ("yslab", 2)), 2)
        inner_field = wide_pad[:, 1:-1, 1:-1]
        potential = (
            inner_field * inner_field * inner_field
            - inner_field
            - GRADIENT_COEF * stencil(wide_pad)
        )
        driving = MOBILITY * stencil(potential)
        parallel_sum = lax.psum(sum_cells(driving * tangent), ("space", "yslab"))
        project_coef = parallel_sum / (tangent_sq + EPSILON)
        spring = (
            SPRING_K * (jnp.sqrt(plus_sq) - jnp.sqrt(minus_sq)) / jnp.sqrt(tangent_sq + EPSILON)
        )
        update = (
            driving
            - project_coef[:, None, None, None] * tangent
            + spring[:, None, None, None] * tangent
        )
        current = jnp.where(interior[:, None, None, None], current + STEP_SIZE * update, current)
        parallel = jnp.where(
            interior, parallel_sum / jnp.sqrt((tangent_sq + EPSILON) * cell_total), jnp.float32(0.0)
        )
    return (current, parallel)


def call(kernel, out_shape, scratch=(), name=None, **kw):
    return pl.pallas_call(
        kernel,
        out_shape=out_shape,
        scratch_shapes=list(scratch),
        name=name,
        compiler_params=pltpu.CompilerParams(
            vmem_limit_bytes=VMEM_ROOM + sum(4 * math.prod(s.shape) for s in scratch if s is not DMA)
        ),
        **kw,
    )


def shape(*dims):
    return jax.ShapeDtypeStruct(dims, jnp.float32)


def lap(below, here, above):
    rows, lanes = here.shape
    ys = pltpu.roll(here, 1, 0) + pltpu.roll(here, rows - 1, 0)
    xs = pltpu.roll(here, 1, 1) + pltpu.roll(here, lanes - 1, 1)
    return (below + above) + ys + xs - 6.0 * here


def layer_loop(start, stop, body):
    def step(k, carry):
        body(k)
        return carry

    lax.fori_loop(start, stop, step, 0, unroll=min(UNROLL, stop - start))


def potentials(field, pot, count):
    def one(k):
        here = field[k + 1]
        pot[k] = here * here * here - here - GRADIENT_COEF * lap(field[k], here, field[k + 2])

    layer_loop(0, count, one)


def driving(pot, k):
    return MOBILITY * lap(pot[k], pot[k + 1], pot[k + 2])


def rows_sum(field):
    rows, lanes = field.shape
    return jnp.sum(field.reshape(rows // 8, 8, lanes), axis=0)


def lane_row(total):
    lanes = total.shape[1]
    folded = jnp.sum(total.reshape(8, lanes // 128, 128), axis=1)
    return jnp.sum(folded, axis=0, keepdims=True)


def fill_padded(dst, pieces, sides, sides_at):
    at = 0
    for piece in pieces:
        layers, rows, _ = piece.shape
        dst[at : at + layers, PAD : PAD + rows] = piece[...]
        at += layers
    dst[:, 0:PAD] = sides[sides_at : sides_at + at, PAD : 2 * PAD]
    dst[:, PAD + rows : 2 * PAD + rows] = sides[sides_at : sides_at + at, 0:PAD]


def all_copied(pairs, sems):
    copies = [pltpu.make_async_copy(src, dst, sems.at[i]) for i, (src, dst) in enumerate(pairs)]
    for c in copies:
        c.start()
    for c in copies:
        c.wait()


def send_first_kernel(images, first, sems):
    which = 1 - lax.axis_index("image")
    all_copied([(images.at[which, pl.ds(0, AHEAD)], first)], sems)


def send_kernel(images, last, middle, sems):
    which = 1 - lax.axis_index("image")
    nz = images.shape[1]
    pairs = [
        (images.at[which, pl.ds(nz - AHEAD, AHEAD)], last),
        (images.at[which, pl.ds(AHEAD, nz - 2 * AHEAD)], middle),
    ]
    all_copied(pairs, sems)


def keep_kernel(images, mine, end, up, down, sems):
    which = 1 - lax.axis_index("image")
    nz, layers = mine.shape[0], up.shape[0]
    pairs = [
        (images.at[which, pl.ds(nz - layers, layers)], up),
        (images.at[which, pl.ds(0, layers)], down),
        (images.at[which], mine),
        (images.at[1 - which], end),
    ]
    all_copied(pairs, sems)


def first_step_kernel(mine, low, high, sides, step_out, drive_out, field, pot):
    nz, rows, _ = mine.shape
    fill_padded(field, (low, mine, high), sides, 0)
    potentials(field, pot, nz + 6)

    def edge(k):
        step_out[k] = field[k + 2] + STEP_SIZE * driving(pot, k)

    def inner(k):
        drive = driving(pot, k)
        step_out[k] = field[k + 2] + STEP_SIZE * drive
        drive_out[k - 2] = drive[PAD : PAD + rows]

    layer_loop(0, 2, edge)
    layer_loop(2, nz + 2, inner)
    layer_loop(nz + 2, nz + 4, edge)


CHUNK = 16


def sums_of(start, stop, rows, terms, totals):
    def one(k, totals):
        for r in range(0, rows, CHUNK):
            totals = tuple(t + rows_sum(v) for t, v in zip(totals, terms(k, pl.ds(r, CHUNK))))
        return totals

    return lax.fori_loop(start, stop, one, totals, unroll=True)


def no_sums(count, lanes):
    return (jnp.zeros((8, lanes), jnp.float32),) * count


def table_of(*rows):
    return jnp.concatenate(rows + (jnp.zeros((8 - len(rows), 128), jnp.float32),), 0)


def first_sums_kernel(edges, middle, mine, end, drive, out):
    nz, rows, lanes = mine.shape

    def terms_from(other, shift):
        def terms(k, r):
            m, o, e = mine[k, r], other[k + shift, r], end[k, r]
            plus, minus, tangent = o - m, m - e, o - e
            return plus * plus, minus * minus, tangent * tangent, drive[k, r] * tangent

        return terms

    last = nz - AHEAD
    totals = sums_of(0, AHEAD, rows, terms_from(edges, 0), no_sums(4, lanes))
    totals = sums_of(AHEAD, last, rows, terms_from(middle, -AHEAD), totals)
    totals = sums_of(last, nz, rows, terms_from(edges, AHEAD - last), totals)
    out[...] = table_of(*(lane_row(t) for t in totals))


def coefficient(sums):
    total = jnp.sum(sums[...], axis=1, keepdims=True)
    plus_sq, minus_sq, tangent_sq, par = (total[i : i + 1] for i in range(4))
    safe = tangent_sq + EPSILON
    spring = SPRING_K * (jnp.sqrt(plus_sq) - jnp.sqrt(minus_sq)) / jnp.sqrt(safe)
    return STEP_SIZE * (spring - par / safe), par, safe


def other_step_kernel(edges, middle, end, low, high, sides, near_out, tangent_out, field, pot):
    nz, rows, _ = end.shape
    first, last = edges.at[0:AHEAD], edges.at[AHEAD : 2 * AHEAD]
    fill_padded(field, (low.at[0:2], first, middle, last, high.at[0:2]), sides, 0)
    fill_padded(tangent_out, (low.at[2:4], end, high.at[2:4]), sides, nz + 4)
    potentials(field, pot, nz + 2)

    def widen(k):
        tangent_out[k] = field[k] - tangent_out[k]

    def one(k):
        moved = field[k + 2] + STEP_SIZE * driving(pot, k)
        near_out[k] = moved[PAD : PAD + rows] - end[k]

    layer_loop(0, nz + 4, widen)
    layer_loop(0, nz, one)


def second_step_kernel(
    sums, step, tangent_wide, end, moved_out, drive_out, minus_out, base, field, pot, sem
):
    nz, rows, _ = end.shape
    still = lax.axis_index("image")
    copy = pltpu.make_async_copy(end, base.at[still], sem)
    copy.start()
    coef, _, _ = coefficient(sums)

    def move(k):
        field[k] = step[k] + coef * tangent_wide[k]

    layer_loop(0, nz + 4, move)
    potentials(field, pot, nz + 2)

    def one(k):
        drive = driving(pot, k)[PAD : PAD + rows]
        here = field[k + 2][PAD : PAD + rows]
        drive_out[k] = drive
        minus_out[k] = here - end[k]
        moved_out[k] = here + STEP_SIZE * drive

    layer_loop(0, nz, one)
    copy.wait()


def second_sums_kernel(o_sums, far, mine, near, minus, drive, out):
    nz, rows, lanes = far.shape
    coef, _, _ = coefficient(o_sums)

    def terms(k, r):
        tangent = near[k, r] + coef * (mine[k, r] - far[k, r])
        m = minus[k, r]
        plus = tangent - m
        return plus * plus, m * m, tangent * tangent, drive[k, r] * tangent

    out[...] = table_of(*(lane_row(t) for t in sums_of(0, nz, rows, terms, no_sums(4, lanes))))


def last_kernel(cells, sums, o_sums, far, mine, near, moved, base, out, par_out, buf, sems):
    del base
    nz = moved.shape[0]
    at = lax.axis_index("image")
    which = 1 - at
    coef, par, safe = coefficient(sums)
    o_coef, _, _ = coefficient(o_sums)
    copies = []
    for k in range(nz):
        buf[k] = moved[k] + coef * (near[k] + o_coef * (mine[k] - far[k]))
        if k % 4 == 3:
            where = pl.ds(k - 3, 4)
            copies.append(
                pltpu.make_async_copy(buf.at[where], out.at[which, where], sems.at[k // 4])
            )
            copies[-1].start()
    value = (par / jnp.sqrt(safe * cells))[0, 0]
    sign = jnp.where(at == 0, 1.0, -1.0).astype(jnp.float32)
    par_out[which] = value * sign
    par_out[1 - which] = jnp.float32(0.0)
    for c in copies:
        c.wait()


ANY = pl.BlockSpec(memory_space=pl.ANY)
VMEM = pl.BlockSpec(memory_space=pltpu.VMEM)
SMEM = pl.BlockSpec(memory_space=pltpu.SMEM)
DMA = pltpu.SemaphoreType.DMA
SWAP = [(0, 1), (1, 0)]


def from_z(up, down):
    count = lax.axis_size("space")
    low = lax.ppermute(up, "space", [(i, (i + 1) % count) for i in range(count)])
    high = lax.ppermute(down, "space", [((i + 1) % count, i) for i in range(count)])
    return low, high


def y_sides(*pieces):
    rows = pieces[0].shape[1]
    ends = [jnp.concatenate([p[:, :PAD], p[:, rows - PAD :]], 1) for p in pieces]
    return lax.ppermute(jnp.concatenate(ends, 0), "yslab", SWAP)


def sum_steps():
    count, stride = lax.axis_size("space"), 1
    steps = [("yslab", SWAP)]
    while stride < count:
        steps.append(("space", [(i, i ^ stride) for i in range(count)]))
        stride *= 2
    return steps


def summed(sums, steps):
    for axis, pairs in steps:
        sums = sums + lax.ppermute(sums, axis, pairs)
    return sums


def body_pair(images):
    _, nz, ny, nx = images.shape
    wide = ny + 2 * PAD
    cells = float(nz * lax.axis_size("space") * ny * lax.axis_size("yslab") * nx)
    block, outer = shape(nz, ny, nx), shape(nz + 4, wide, nx)
    table = shape(8, 128)

    def room(layers):
        return pltpu.VMEM((layers, wide, nx), jnp.float32)

    thin = shape(4, ny, nx)
    source = pltpu.with_memory_space_constraint(images, pltpu.HBM)
    few = shape(AHEAD, ny, nx)
    first = call(
        send_first_kernel, few, [DMA((1,))], "send_first", in_specs=[ANY], out_specs=ANY
    )(source)
    last, middle = call(
        send_kernel,
        [few, shape(nz - 2 * AHEAD, ny, nx)],
        [DMA((2,))],
        "send",
        in_specs=[ANY],
        out_specs=[ANY] * 2,
    )(source)
    mine, end, up, down = call(
        keep_kernel,
        [block, block, thin, thin],
        [DMA((4,))],
        "keep",
        in_specs=[ANY],
        out_specs=[ANY] * 4,
    )(source)

    o_first = lax.ppermute(first, "image", SWAP)
    o_last = lax.ppermute(last, "image", SWAP)
    o_middle = lax.ppermute(middle, "image", SWAP)
    far = lax.ppermute(end, "image", SWAP)

    up, down, o_first = lax.optimization_barrier((up, down, o_first))
    o_edges = jnp.concatenate([o_first, o_last])
    low, high = from_z(up, down)
    sides = y_sides(low, mine, high)
    step, drive = call(first_step_kernel, [outer, block], [room(nz + 8), room(nz + 6)], "first_step")(
        mine, low, high, sides
    )

    o_edges, low, high = lax.optimization_barrier((o_edges, low, high))
    o_low, o_high = from_z(
        jnp.concatenate([o_edges[2 * AHEAD - 2 :], end[nz - 2 :]]),
        jnp.concatenate([o_edges[:2], end[:2]]),
    )
    sums = call(first_sums_kernel, table, name="first_sums")(o_edges, o_middle, mine, end, drive)
    steps = sum_steps()
    sums = summed(sums, steps[:2])
    o_low, o_high, sums = lax.optimization_barrier((o_low, o_high, sums))
    o_sides = y_sides(
        o_low[:2], o_edges[:AHEAD], o_middle, o_edges[AHEAD:], o_high[:2], o_low[2:], end, o_high[2:]
    )
    sums = summed(sums, steps[2:])
    near, tangent_wide = call(
        other_step_kernel, [block, outer], [room(nz + 4), room(nz + 2)], "other_step"
    )(o_edges, o_middle, end, o_low, o_high, o_sides)

    whole = jax.ShapeDtypeStruct(images.shape, images.dtype)
    moved, drive2, minus, base = call(
        second_step_kernel,
        [block] * 3 + [whole],
        [room(nz + 4), room(nz + 2), DMA],
        "second_step",
        in_specs=[VMEM] * 4,
        out_specs=[VMEM] * 3 + [ANY],
    )(sums, step, tangent_wide, end)

    o_sums = lax.ppermute(sums, "image", SWAP)
    sums = call(second_sums_kernel, table, name="second_sums")(
        o_sums, far, mine, near, minus, drive2
    )

    return call(
        functools.partial(last_kernel, cells),
        [whole, shape(2)],
        [pltpu.VMEM(block.shape, jnp.float32), DMA((nz // 4,))],
        "last",
        in_specs=[VMEM] * 6 + [ANY],
        out_specs=[ANY, SMEM],
        input_output_aliases={6: 0},
    )(summed(sums, sum_steps()), o_sums, far, mine, near, moved, base)


def body(images):
    layers = lax.axis_size("space")
    pair = lax.axis_size("image") == 2 and lax.axis_size("yslab") == 2 and images.shape[0] == 2
    pair = pair and layers & (layers - 1) == 0 and images.shape[1] % 4 == 0
    pair = pair and images.shape[1] > 2 * AHEAD and images.shape[2] % CHUNK == 0
    return body_pair(images) if pair else body_any(images)


def solution(mesh):
    in_specs = (P(("groups", "image"), "space", "yslab", None),)
    out_specs = (P(("groups", "image"), "space", "yslab", None), P(("groups", "image")))
    return jax.shard_map(body, mesh=mesh, in_specs=in_specs, out_specs=out_specs, check_vma=False)
```

```python
import functools
import math

import jax
import jax.numpy as jnp
from jax import lax
from jax.experimental import pallas as pl
from jax.experimental.pallas import tpu as pltpu
from jax.sharding import PartitionSpec as P

ITERS = 2


GRADIENT_COEF = 1.0
MOBILITY = 0.004
SPRING_K = 1.0
STEP_SIZE = 0.5
EPSILON = 1e-06

PAD = 8
VMEM_ROOM = 2 * 2**20
UNROLL = 8
AHEAD = 2


def passed_along(array, axis, by):
    peers = lax.axis_size(axis)
    pairs = [(i, i + by) for i in range(peers) if 0 <= i + by < peers]
    return lax.ppermute(array, axis, pairs)


def extended(cells, sides, width):
    for axis, dim in sides:
        count = lax.axis_size(axis)
        head = lax.slice_in_dim(cells, 0, width, axis=dim)
        tail = lax.slice_in_dim(cells, cells.shape[dim] - width, cells.shape[dim], axis=dim)
        cells = jnp.concatenate(
            [
                lax.ppermute(tail, axis, [(i, (i + 1) % count) for i in range(count)]),
                cells,
                lax.ppermute(head, axis, [((i + 1) % count, i) for i in range(count)]),
            ],
            axis=dim,
        )
    return cells


def stencil(padded):
    middle = padded[:, 1:-1, 1:-1]
    neighbours = padded[:, 2:, 1:-1] + padded[:, :-2, 1:-1]
    neighbours = neighbours + padded[:, 1:-1, 2:] + padded[:, 1:-1, :-2]
    neighbours = neighbours + jnp.roll(middle, -1, 3) + jnp.roll(middle, 1, 3)
    return neighbours - 6.0 * middle


def sum_cells(field):
    return jnp.sum(field, axis=(1, 2, 3))


def body_any(images):
    current = images
    per_device = current.shape[0]
    total_images = per_device * lax.axis_size("image")
    cell_total = float(
        current.shape[1]
        * lax.axis_size("space")
        * current.shape[2]
        * lax.axis_size("yslab")
        * current.shape[3]
    )
    image_ids = lax.axis_index("image") * per_device + jnp.arange(per_device, dtype=jnp.int32)
    interior = (image_ids > 0) & (image_ids < total_images - 1)
    parallel = jnp.zeros((per_device,), jnp.float32)
    for iteration in range(ITERS):
        next_first = passed_along(current[0], "image", -1)
        prev_last = passed_along(current[-1], "image", 1)
        ahead = jnp.concatenate([current[1:], next_first[None]], 0)
        behind = jnp.concatenate([prev_last[None], current[:-1]], 0)
        forward = ahead - current
        backward = current - behind
        tangent = forward + backward
        plus_sq, minus_sq, tangent_sq = lax.psum(
            (
                sum_cells(forward * forward),
                sum_cells(backward * backward),
                sum_cells(tangent * tangent),
            ),
            ("space", "yslab"),
        )
        wide_pad = extended(current, (("space", 1), ("yslab", 2)), 2)
        inner_field = wide_pad[:, 1:-1, 1:-1]
        potential = (
            inner_field * inner_field * inner_field
            - inner_field
            - GRADIENT_COEF * stencil(wide_pad)
        )
        driving = MOBILITY * stencil(potential)
        parallel_sum = lax.psum(sum_cells(driving * tangent), ("space", "yslab"))
        project_coef = parallel_sum / (tangent_sq + EPSILON)
        spring = (
            SPRING_K * (jnp.sqrt(plus_sq) - jnp.sqrt(minus_sq)) / jnp.sqrt(tangent_sq + EPSILON)
        )
        update = (
            driving
            - project_coef[:, None, None, None] * tangent
            + spring[:, None, None, None] * tangent
        )
        current = jnp.where(interior[:, None, None, None], current + STEP_SIZE * update, current)
        parallel = jnp.where(
            interior, parallel_sum / jnp.sqrt((tangent_sq + EPSILON) * cell_total), jnp.float32(0.0)
        )
    return (current, parallel)


def call(kernel, out_shape, scratch=(), name=None, **kw):
    return pl.pallas_call(
        kernel,
        out_shape=out_shape,
        scratch_shapes=list(scratch),
        name=name,
        compiler_params=pltpu.CompilerParams(
            vmem_limit_bytes=VMEM_ROOM + sum(4 * math.prod(s.shape) for s in scratch if s is not DMA)
        ),
        **kw,
    )


def shape(*dims):
    return jax.ShapeDtypeStruct(dims, jnp.float32)


def lap(below, here, above):
    rows, lanes = here.shape
    ys = pltpu.roll(here, 1, 0) + pltpu.roll(here, rows - 1, 0)
    xs = pltpu.roll(here, 1, 1) + pltpu.roll(here, lanes - 1, 1)
    return (below + above) + ys + xs - 6.0 * here


def layer_loop(start, stop, body):
    def step(k, carry):
        body(k)
        return carry

    lax.fori_loop(start, stop, step, 0, unroll=min(UNROLL, stop - start))


def potentials(field, pot, count):
    def one(k):
        here = field[k + 1]
        pot[k] = here * here * here - here - GRADIENT_COEF * lap(field[k], here, field[k + 2])

    layer_loop(0, count, one)


def driving(pot, k):
    return MOBILITY * lap(pot[k], pot[k + 1], pot[k + 2])


def rows_sum(field):
    rows, lanes = field.shape
    return jnp.sum(field.reshape(rows // 8, 8, lanes), axis=0)


def lane_row(total):
    lanes = total.shape[1]
    folded = jnp.sum(total.reshape(8, lanes // 128, 128), axis=1)
    return jnp.sum(folded, axis=0, keepdims=True)


def fill_padded(dst, pieces, sides, sides_at):
    at = 0
    for piece in pieces:
        layers, rows, _ = piece.shape
        dst[at : at + layers, PAD : PAD + rows] = piece[...]
        at += layers
    dst[:, 0:PAD] = sides[sides_at : sides_at + at, PAD : 2 * PAD]
    dst[:, PAD + rows : 2 * PAD + rows] = sides[sides_at : sides_at + at, 0:PAD]


def all_copied(pairs, sems):
    copies = [pltpu.make_async_copy(src, dst, sems.at[i]) for i, (src, dst) in enumerate(pairs)]
    for c in copies:
        c.start()
    for c in copies:
        c.wait()


def send_kernel(images, edges, middle, sems):
    which = 1 - lax.axis_index("image")
    nz = images.shape[1]
    pairs = [
        (images.at[which, pl.ds(0, AHEAD)], edges.at[pl.ds(0, AHEAD)]),
        (images.at[which, pl.ds(nz - AHEAD, AHEAD)], edges.at[pl.ds(AHEAD, AHEAD)]),
        (images.at[which, pl.ds(AHEAD, nz - 2 * AHEAD)], middle),
    ]
    all_copied(pairs, sems)


def keep_kernel(images, mine, end, up, down, sems):
    which = 1 - lax.axis_index("image")
    nz, layers = mine.shape[0], up.shape[0]
    pairs = [
        (images.at[which, pl.ds(nz - layers, layers)], up),
        (images.at[which, pl.ds(0, layers)], down),
        (images.at[which], mine),
        (images.at[1 - which], end),
    ]
    all_copied(pairs, sems)


def first_step_kernel(mine, low, high, sides, step_out, drive_out, field, pot):
    nz, rows, _ = mine.shape
    fill_padded(field, (low, mine, high), sides, 0)
    potentials(field, pot, nz + 6)

    def edge(k):
        step_out[k] = field[k + 2] + STEP_SIZE * driving(pot, k)

    def inner(k):
        drive = driving(pot, k)
        step_out[k] = field[k + 2] + STEP_SIZE * drive
        drive_out[k - 2] = drive[PAD : PAD + rows]

    layer_loop(0, 2, edge)
    layer_loop(2, nz + 2, inner)
    layer_loop(nz + 2, nz + 4, edge)


CHUNK = 16


def sums_of(start, stop, rows, terms, totals):
    def one(k, totals):
        for r in range(0, rows, CHUNK):
            totals = tuple(t + rows_sum(v) for t, v in zip(totals, terms(k, pl.ds(r, CHUNK))))
        return totals

    return lax.fori_loop(start, stop, one, totals, unroll=True)


def no_sums(count, lanes):
    return (jnp.zeros((8, lanes), jnp.float32),) * count


def table_of(*rows):
    return jnp.concatenate(rows + (jnp.zeros((8 - len(rows), 128), jnp.float32),), 0)


def first_sums_kernel(edges, middle, mine, end, drive, out):
    nz, rows, lanes = mine.shape

    def terms_from(other, shift):
        def terms(k, r):
            m, o, e = mine[k, r], other[k + shift, r], end[k, r]
            plus, minus, tangent = o - m, m - e, o - e
            return plus * plus, minus * minus, tangent * tangent, drive[k, r] * tangent

        return terms

    last = nz - AHEAD
    totals = sums_of(0, AHEAD, rows, terms_from(edges, 0), no_sums(4, lanes))
    totals = sums_of(AHEAD, last, rows, terms_from(middle, -AHEAD), totals)
    totals = sums_of(last, nz, rows, terms_from(edges, AHEAD - last), totals)
    out[...] = table_of(*(lane_row(t) for t in totals))


def coefficient(sums):
    total = jnp.sum(sums[...], axis=1, keepdims=True)
    plus_sq, minus_sq, tangent_sq, par = (total[i : i + 1] for i in range(4))
    safe = tangent_sq + EPSILON
    spring = SPRING_K * (jnp.sqrt(plus_sq) - jnp.sqrt(minus_sq)) / jnp.sqrt(safe)
    return STEP_SIZE * (spring - par / safe), par, safe


def other_step_kernel(edges, middle, end, low, high, sides, near_out, tangent_out, field, pot):
    nz, rows, _ = end.shape
    first, last = edges.at[0:AHEAD], edges.at[AHEAD : 2 * AHEAD]
    fill_padded(field, (low.at[0:2], first, middle, last, high.at[0:2]), sides, 0)
    fill_padded(tangent_out, (low.at[2:4], end, high.at[2:4]), sides, nz + 4)
    potentials(field, pot, nz + 2)

    def widen(k):
        tangent_out[k] = field[k] - tangent_out[k]

    def one(k):
        moved = field[k + 2] + STEP_SIZE * driving(pot, k)
        near_out[k] = moved[PAD : PAD + rows] - end[k]

    layer_loop(0, nz + 4, widen)
    layer_loop(0, nz, one)


def second_step_kernel(
    sums, step, tangent_wide, end, moved_out, drive_out, minus_out, base, field, pot, sem
):
    nz, rows, _ = end.shape
    still = lax.axis_index("image")
    copy = pltpu.make_async_copy(end, base.at[still], sem)
    copy.start()
    coef, _, _ = coefficient(sums)

    def move(k):
        field[k] = step[k] + coef * tangent_wide[k]

    layer_loop(0, nz + 4, move)
    potentials(field, pot, nz + 2)

    def one(k):
        drive = driving(pot, k)[PAD : PAD + rows]
        here = field[k + 2][PAD : PAD + rows]
        drive_out[k] = drive
        minus_out[k] = here - end[k]
        moved_out[k] = here + STEP_SIZE * drive

    layer_loop(0, nz, one)
    copy.wait()


def second_sums_kernel(o_sums, far, mine, near, minus, drive, out):
    nz, rows, lanes = far.shape
    coef, _, _ = coefficient(o_sums)

    def terms(k, r):
        tangent = near[k, r] + coef * (mine[k, r] - far[k, r])
        m = minus[k, r]
        plus = tangent - m
        return plus * plus, m * m, tangent * tangent, drive[k, r] * tangent

    out[...] = table_of(*(lane_row(t) for t in sums_of(0, nz, rows, terms, no_sums(4, lanes))))


def last_kernel(cells, sums, o_sums, far, mine, near, moved, base, out, par_out, buf, sems):
    del base
    nz = moved.shape[0]
    at = lax.axis_index("image")
    which = 1 - at
    coef, par, safe = coefficient(sums)
    o_coef, _, _ = coefficient(o_sums)
    copies = []
    for k in range(nz):
        buf[k] = moved[k] + coef * (near[k] + o_coef * (mine[k] - far[k]))
        if k % 2 == 1:
            where = pl.ds(k - 1, 2)
            copies.append(
                pltpu.make_async_copy(buf.at[where], out.at[which, where], sems.at[k // 2])
            )
            copies[-1].start()
    value = (par / jnp.sqrt(safe * cells))[0, 0]
    sign = jnp.where(at == 0, 1.0, -1.0).astype(jnp.float32)
    par_out[which] = value * sign
    par_out[1 - which] = jnp.float32(0.0)
    for c in copies:
        c.wait()


ANY = pl.BlockSpec(memory_space=pl.ANY)
VMEM = pl.BlockSpec(memory_space=pltpu.VMEM)
SMEM = pl.BlockSpec(memory_space=pltpu.SMEM)
DMA = pltpu.SemaphoreType.DMA
SWAP = [(0, 1), (1, 0)]


def from_z(up, down):
    count = lax.axis_size("space")
    low = lax.ppermute(up, "space", [(i, (i + 1) % count) for i in range(count)])
    high = lax.ppermute(down, "space", [((i + 1) % count, i) for i in range(count)])
    return low, high


def y_sides(*pieces):
    rows = pieces[0].shape[1]
    ends = [jnp.concatenate([p[:, :PAD], p[:, rows - PAD :]], 1) for p in pieces]
    return lax.ppermute(jnp.concatenate(ends, 0), "yslab", SWAP)


def sum_steps():
    count, stride = lax.axis_size("space"), 1
    steps = [("yslab", SWAP)]
    while stride < count:
        steps.append(("space", [(i, i ^ stride) for i in range(count)]))
        stride *= 2
    return steps


def summed(sums, steps):
    for axis, pairs in steps:
        sums = sums + lax.ppermute(sums, axis, pairs)
    return sums


def body_pair(images):
    _, nz, ny, nx = images.shape
    wide = ny + 2 * PAD
    cells = float(nz * lax.axis_size("space") * ny * lax.axis_size("yslab") * nx)
    block, outer = shape(nz, ny, nx), shape(nz + 4, wide, nx)
    table = shape(8, 128)

    def room(layers):
        return pltpu.VMEM((layers, wide, nx), jnp.float32)

    thin = shape(4, ny, nx)
    source = pltpu.with_memory_space_constraint(images, pltpu.HBM)
    edges, middle = call(
        send_kernel,
        [shape(2 * AHEAD, ny, nx), shape(nz - 2 * AHEAD, ny, nx)],
        [DMA((3,))],
        "send",
        in_specs=[ANY],
        out_specs=[ANY] * 2,
    )(source)
    mine, end, up, down = call(
        keep_kernel,
        [block, block, thin, thin],
        [DMA((4,))],
        "keep",
        in_specs=[ANY],
        out_specs=[ANY] * 4,
    )(source)

    o_first = lax.ppermute(edges[:AHEAD], "image", SWAP)
    o_last = lax.ppermute(edges[AHEAD:], "image", SWAP)
    o_middle = lax.ppermute(middle, "image", SWAP)
    far = lax.ppermute(end, "image", SWAP)

    up, down, o_first = lax.optimization_barrier((up, down, o_first))
    o_edges = jnp.concatenate([o_first, o_last])
    low, high = from_z(up, down)
    sides = y_sides(low, mine, high)
    step, drive = call(first_step_kernel, [outer, block], [room(nz + 8), room(nz + 6)], "first_step")(
        mine, low, high, sides
    )

    o_edges, low, high = lax.optimization_barrier((o_edges, low, high))
    o_low, o_high = from_z(
        jnp.concatenate([o_edges[2 * AHEAD - 2 :], end[nz - 2 :]]),
        jnp.concatenate([o_edges[:2], end[:2]]),
    )
    sums = call(first_sums_kernel, table, name="first_sums")(o_edges, o_middle, mine, end, drive)
    steps = sum_steps()
    sums = summed(sums, steps[:2])
    o_low, o_high, sums = lax.optimization_barrier((o_low, o_high, sums))
    o_sides = y_sides(
        o_low[:2], o_edges[:AHEAD], o_middle, o_edges[AHEAD:], o_high[:2], o_low[2:], end, o_high[2:]
    )
    sums = summed(sums, steps[2:])
    near, tangent_wide = call(
        other_step_kernel, [block, outer], [room(nz + 4), room(nz + 2)], "other_step"
    )(o_edges, o_middle, end, o_low, o_high, o_sides)

    whole = jax.ShapeDtypeStruct(images.shape, images.dtype)
    moved, drive2, minus, base = call(
        second_step_kernel,
        [block] * 3 + [whole],
        [room(nz + 4), room(nz + 2), DMA],
        "second_step",
        in_specs=[VMEM] * 4,
        out_specs=[VMEM] * 3 + [ANY],
    )(sums, step, tangent_wide, end)

    o_sums = lax.ppermute(sums, "image", SWAP)
    sums = call(second_sums_kernel, table, name="second_sums")(
        o_sums, far, mine, near, minus, drive2
    )

    return call(
        functools.partial(last_kernel, cells),
        [whole, shape(2)],
        [pltpu.VMEM(block.shape, jnp.float32), DMA((nz // 2,))],
        "last",
        in_specs=[VMEM] * 6 + [ANY],
        out_specs=[ANY, SMEM],
        input_output_aliases={6: 0},
    )(summed(sums, sum_steps()), o_sums, far, mine, near, moved, base)


def body(images):
    layers = lax.axis_size("space")
    pair = lax.axis_size("image") == 2 and lax.axis_size("yslab") == 2 and images.shape[0] == 2
    pair = pair and layers & (layers - 1) == 0 and images.shape[1] % 4 == 0
    pair = pair and images.shape[1] > 2 * AHEAD and images.shape[2] % CHUNK == 0
    return body_pair(images) if pair else body_any(images)


def solution(mesh):
    in_specs = (P(("groups", "image"), "space", "yslab", None),)
    out_specs = (P(("groups", "image"), "space", "yslab", None), P(("groups", "image")))
    return jax.shard_map(body, mesh=mesh, in_specs=in_specs, out_specs=out_specs, check_vma=False)
```

```python
import functools
import math

import jax
import jax.numpy as jnp
from jax import lax
from jax.experimental import pallas as pl
from jax.experimental.pallas import tpu as pltpu
from jax.sharding import PartitionSpec as P

ITERS = 2


GRADIENT_COEF = 1.0
MOBILITY = 0.004
SPRING_K = 1.0
STEP_SIZE = 0.5
EPSILON = 1e-06

PAD = 8
VMEM_ROOM = 2 * 2**20
UNROLL = 4
AHEAD = 2


def passed_along(array, axis, by):
    peers = lax.axis_size(axis)
    pairs = [(i, i + by) for i in range(peers) if 0 <= i + by < peers]
    return lax.ppermute(array, axis, pairs)


def extended(cells, sides, width):
    for axis, dim in sides:
        count = lax.axis_size(axis)
        head = lax.slice_in_dim(cells, 0, width, axis=dim)
        tail = lax.slice_in_dim(cells, cells.shape[dim] - width, cells.shape[dim], axis=dim)
        cells = jnp.concatenate(
            [
                lax.ppermute(tail, axis, [(i, (i + 1) % count) for i in range(count)]),
                cells,
                lax.ppermute(head, axis, [((i + 1) % count, i) for i in range(count)]),
            ],
            axis=dim,
        )
    return cells


def stencil(padded):
    middle = padded[:, 1:-1, 1:-1]
    neighbours = padded[:, 2:, 1:-1] + padded[:, :-2, 1:-1]
    neighbours = neighbours + padded[:, 1:-1, 2:] + padded[:, 1:-1, :-2]
    neighbours = neighbours + jnp.roll(middle, -1, 3) + jnp.roll(middle, 1, 3)
    return neighbours - 6.0 * middle


def sum_cells(field):
    return jnp.sum(field, axis=(1, 2, 3))


def body_any(images):
    current = images
    per_device = current.shape[0]
    total_images = per_device * lax.axis_size("image")
    cell_total = float(
        current.shape[1]
        * lax.axis_size("space")
        * current.shape[2]
        * lax.axis_size("yslab")
        * current.shape[3]
    )
    image_ids = lax.axis_index("image") * per_device + jnp.arange(per_device, dtype=jnp.int32)
    interior = (image_ids > 0) & (image_ids < total_images - 1)
    parallel = jnp.zeros((per_device,), jnp.float32)
    for iteration in range(ITERS):
        next_first = passed_along(current[0], "image", -1)
        prev_last = passed_along(current[-1], "image", 1)
        ahead = jnp.concatenate([current[1:], next_first[None]], 0)
        behind = jnp.concatenate([prev_last[None], current[:-1]], 0)
        forward = ahead - current
        backward = current - behind
        tangent = forward + backward
        plus_sq, minus_sq, tangent_sq = lax.psum(
            (
                sum_cells(forward * forward),
                sum_cells(backward * backward),
                sum_cells(tangent * tangent),
            ),
            ("space", "yslab"),
        )
        wide_pad = extended(current, (("space", 1), ("yslab", 2)), 2)
        inner_field = wide_pad[:, 1:-1, 1:-1]
        potential = (
            inner_field * inner_field * inner_field
            - inner_field
            - GRADIENT_COEF * stencil(wide_pad)
        )
        driving = MOBILITY * stencil(potential)
        parallel_sum = lax.psum(sum_cells(driving * tangent), ("space", "yslab"))
        project_coef = parallel_sum / (tangent_sq + EPSILON)
        spring = (
            SPRING_K * (jnp.sqrt(plus_sq) - jnp.sqrt(minus_sq)) / jnp.sqrt(tangent_sq + EPSILON)
        )
        update = (
            driving
            - project_coef[:, None, None, None] * tangent
            + spring[:, None, None, None] * tangent
        )
        current = jnp.where(interior[:, None, None, None], current + STEP_SIZE * update, current)
        parallel = jnp.where(
            interior, parallel_sum / jnp.sqrt((tangent_sq + EPSILON) * cell_total), jnp.float32(0.0)
        )
    return (current, parallel)


def call(kernel, out_shape, scratch=(), name=None, **kw):
    return pl.pallas_call(
        kernel,
        out_shape=out_shape,
        scratch_shapes=list(scratch),
        name=name,
        compiler_params=pltpu.CompilerParams(
            vmem_limit_bytes=VMEM_ROOM + sum(4 * math.prod(s.shape) for s in scratch if s is not DMA)
        ),
        **kw,
    )


def shape(*dims):
    return jax.ShapeDtypeStruct(dims, jnp.float32)


def lap(below, here, above):
    rows, lanes = here.shape
    ys = pltpu.roll(here, 1, 0) + pltpu.roll(here, rows - 1, 0)
    xs = pltpu.roll(here, 1, 1) + pltpu.roll(here, lanes - 1, 1)
    return (below + above) + ys + xs - 6.0 * here


def layer_loop(start, stop, body):
    def step(k, carry):
        body(k)
        return carry

    lax.fori_loop(start, stop, step, 0, unroll=min(UNROLL, stop - start))


def potentials(field, pot, count):
    def one(k):
        here = field[k + 1]
        pot[k] = here * here * here - here - GRADIENT_COEF * lap(field[k], here, field[k + 2])

    layer_loop(0, count, one)


def driving(pot, k):
    return MOBILITY * lap(pot[k], pot[k + 1], pot[k + 2])


def rows_sum(field):
    rows, lanes = field.shape
    return jnp.sum(field.reshape(rows // 8, 8, lanes), axis=0)


def lane_row(total):
    lanes = total.shape[1]
    folded = jnp.sum(total.reshape(8, lanes // 128, 128), axis=1)
    return jnp.sum(folded, axis=0, keepdims=True)


def fill_padded(dst, pieces, sides, sides_at):
    at = 0
    for piece in pieces:
        layers, rows, _ = piece.shape
        dst[at : at + layers, PAD : PAD + rows] = piece[...]
        at += layers
    dst[:, 0:PAD] = sides[sides_at : sides_at + at, PAD : 2 * PAD]
    dst[:, PAD + rows : 2 * PAD + rows] = sides[sides_at : sides_at + at, 0:PAD]


def all_copied(pairs, sems):
    copies = [pltpu.make_async_copy(src, dst, sems.at[i]) for i, (src, dst) in enumerate(pairs)]
    for c in copies:
        c.start()
    for c in copies:
        c.wait()


def send_kernel(images, edges, middle, sems):
    which = 1 - lax.axis_index("image")
    nz = images.shape[1]
    pairs = [
        (images.at[which, pl.ds(0, AHEAD)], edges.at[pl.ds(0, AHEAD)]),
        (images.at[which, pl.ds(nz - AHEAD, AHEAD)], edges.at[pl.ds(AHEAD, AHEAD)]),
        (images.at[which, pl.ds(AHEAD, nz - 2 * AHEAD)], middle),
    ]
    all_copied(pairs, sems)


def keep_kernel(images, mine, end, up, down, sems):
    which = 1 - lax.axis_index("image")
    nz, layers = mine.shape[0], up.shape[0]
    pairs = [
        (images.at[which, pl.ds(nz - layers, layers)], up),
        (images.at[which, pl.ds(0, layers)], down),
        (images.at[which], mine),
        (images.at[1 - which], end),
    ]
    all_copied(pairs, sems)


def first_step_kernel(mine, low, high, sides, step_out, drive_out, field, pot):
    nz, rows, _ = mine.shape
    fill_padded(field, (low, mine, high), sides, 0)
    potentials(field, pot, nz + 6)

    def edge(k):
        step_out[k] = field[k + 2] + STEP_SIZE * driving(pot, k)

    def inner(k):
        drive = driving(pot, k)
        step_out[k] = field[k + 2] + STEP_SIZE * drive
        drive_out[k - 2] = drive[PAD : PAD + rows]

    layer_loop(0, 2, edge)
    layer_loop(2, nz + 2, inner)
    layer_loop(nz + 2, nz + 4, edge)


CHUNK = 16


def sums_of(start, stop, rows, terms, totals):
    def one(k, totals):
        for r in range(0, rows, CHUNK):
            totals = tuple(t + rows_sum(v) for t, v in zip(totals, terms(k, pl.ds(r, CHUNK))))
        return totals

    return lax.fori_loop(start, stop, one, totals, unroll=True)


def no_sums(count, lanes):
    return (jnp.zeros((8, lanes), jnp.float32),) * count


def table_of(*rows):
    return jnp.concatenate(rows + (jnp.zeros((8 - len(rows), 128), jnp.float32),), 0)


def first_sums_kernel(edges, middle, mine, end, drive, out):
    nz, rows, lanes = mine.shape

    def terms_from(other, shift):
        def terms(k, r):
            m, o, e = mine[k, r], other[k + shift, r], end[k, r]
            plus, minus, tangent = o - m, m - e, o - e
            return plus * plus, minus * minus, tangent * tangent, drive[k, r] * tangent

        return terms

    last = nz - AHEAD
    totals = sums_of(0, AHEAD, rows, terms_from(edges, 0), no_sums(4, lanes))
    totals = sums_of(AHEAD, last, rows, terms_from(middle, -AHEAD), totals)
    totals = sums_of(last, nz, rows, terms_from(edges, AHEAD - last), totals)
    out[...] = table_of(*(lane_row(t) for t in totals))


def coefficient(sums):
    total = jnp.sum(sums[...], axis=1, keepdims=True)
    plus_sq, minus_sq, tangent_sq, par = (total[i : i + 1] for i in range(4))
    safe = tangent_sq + EPSILON
    spring = SPRING_K * (jnp.sqrt(plus_sq) - jnp.sqrt(minus_sq)) / jnp.sqrt(safe)
    return STEP_SIZE * (spring - par / safe), par, safe


def other_step_kernel(edges, middle, end, low, high, sides, near_out, tangent_out, field, pot):
    nz, rows, _ = end.shape
    first, last = edges.at[0:AHEAD], edges.at[AHEAD : 2 * AHEAD]
    fill_padded(field, (low.at[0:2], first, middle, last, high.at[0:2]), sides, 0)
    fill_padded(tangent_out, (low.at[2:4], end, high.at[2:4]), sides, nz + 4)
    potentials(field, pot, nz + 2)

    def widen(k):
        tangent_out[k] = field[k] - tangent_out[k]

    def one(k):
        moved = field[k + 2] + STEP_SIZE * driving(pot, k)
        near_out[k] = moved[PAD : PAD + rows] - end[k]

    layer_loop(0, nz + 4, widen)
    layer_loop(0, nz, one)


def second_step_kernel(
    sums, step, tangent_wide, end, moved_out, drive_out, minus_out, base, field, pot, sem
):
    nz, rows, _ = end.shape
    still = lax.axis_index("image")
    copy = pltpu.make_async_copy(end, base.at[still], sem)
    copy.start()
    coef, _, _ = coefficient(sums)

    def move(k):
        field[k] = step[k] + coef * tangent_wide[k]

    layer_loop(0, nz + 4, move)
    potentials(field, pot, nz + 2)

    def one(k):
        drive = driving(pot, k)[PAD : PAD + rows]
        here = field[k + 2][PAD : PAD + rows]
        drive_out[k] = drive
        minus_out[k] = here - end[k]
        moved_out[k] = here + STEP_SIZE * drive

    layer_loop(0, nz, one)
    copy.wait()


def second_sums_kernel(o_sums, far, mine, near, minus, drive, out):
    nz, rows, lanes = far.shape
    coef, _, _ = coefficient(o_sums)

    def terms(k, r):
        tangent = near[k, r] + coef * (mine[k, r] - far[k, r])
        m = minus[k, r]
        plus = tangent - m
        return plus * plus, m * m, tangent * tangent, drive[k, r] * tangent

    out[...] = table_of(*(lane_row(t) for t in sums_of(0, nz, rows, terms, no_sums(4, lanes))))


def last_kernel(cells, sums, o_sums, far, mine, near, moved, base, out, par_out, buf, sems):
    del base
    nz = moved.shape[0]
    at = lax.axis_index("image")
    which = 1 - at
    coef, par, safe = coefficient(sums)
    o_coef, _, _ = coefficient(o_sums)
    copies = []
    for k in range(nz):
        buf[k] = moved[k] + coef * (near[k] + o_coef * (mine[k] - far[k]))
        if k % 4 == 3:
            where = pl.ds(k - 3, 4)
            copies.append(
                pltpu.make_async_copy(buf.at[where], out.at[which, where], sems.at[k // 4])
            )
            copies[-1].start()
    value = (par / jnp.sqrt(safe * cells))[0, 0]
    sign = jnp.where(at == 0, 1.0, -1.0).astype(jnp.float32)
    par_out[which] = value * sign
    par_out[1 - which] = jnp.float32(0.0)
    for c in copies:
        c.wait()


ANY = pl.BlockSpec(memory_space=pl.ANY)
VMEM = pl.BlockSpec(memory_space=pltpu.VMEM)
SMEM = pl.BlockSpec(memory_space=pltpu.SMEM)
DMA = pltpu.SemaphoreType.DMA
SWAP = [(0, 1), (1, 0)]


def from_z(up, down):
    count = lax.axis_size("space")
    low = lax.ppermute(up, "space", [(i, (i + 1) % count) for i in range(count)])
    high = lax.ppermute(down, "space", [((i + 1) % count, i) for i in range(count)])
    return low, high


def y_sides(*pieces):
    rows = pieces[0].shape[1]
    ends = [jnp.concatenate([p[:, :PAD], p[:, rows - PAD :]], 1) for p in pieces]
    return lax.ppermute(jnp.concatenate(ends, 0), "yslab", SWAP)


def sum_steps():
    count = lax.axis_size("space")
    stride = count // 2
    steps = [("yslab", SWAP)]
    while stride:
        steps.append(("space", [(i, i ^ stride) for i in range(count)]))
        stride //= 2
    return steps


def summed(sums, steps):
    for axis, pairs in steps:
        sums = sums + lax.ppermute(sums, axis, pairs)
    return sums


def body_pair(images):
    _, nz, ny, nx = images.shape
    wide = ny + 2 * PAD
    cells = float(nz * lax.axis_size("space") * ny * lax.axis_size("yslab") * nx)
    block, outer = shape(nz, ny, nx), shape(nz + 4, wide, nx)
    table = shape(8, 128)

    def room(layers):
        return pltpu.VMEM((layers, wide, nx), jnp.float32)

    thin = shape(4, ny, nx)
    source = pltpu.with_memory_space_constraint(images, pltpu.HBM)
    edges, middle = call(
        send_kernel,
        [shape(2 * AHEAD, ny, nx), shape(nz - 2 * AHEAD, ny, nx)],
        [DMA((3,))],
        "send",
        in_specs=[ANY],
        out_specs=[ANY] * 2,
    )(source)
    mine, end, up, down = call(
        keep_kernel,
        [block, block, thin, thin],
        [DMA((4,))],
        "keep",
        in_specs=[ANY],
        out_specs=[ANY] * 4,
    )(source)

    o_first = lax.ppermute(edges[:AHEAD], "image", SWAP)
    o_last = lax.ppermute(edges[AHEAD:], "image", SWAP)
    o_middle = lax.ppermute(middle, "image", SWAP)
    far = lax.ppermute(end, "image", SWAP)

    up, down, o_first = lax.optimization_barrier((up, down, o_first))
    o_edges = jnp.concatenate([o_first, o_last])
    low, high = from_z(up, down)
    sides = y_sides(low, mine, high)
    step, drive = call(first_step_kernel, [outer, block], [room(nz + 8), room(nz + 6)], "first_step")(
        mine, low, high, sides
    )

    o_edges, low, high = lax.optimization_barrier((o_edges, low, high))
    o_low, o_high = from_z(
        jnp.concatenate([o_edges[2 * AHEAD - 2 :], end[nz - 2 :]]),
        jnp.concatenate([o_edges[:2], end[:2]]),
    )
    sums = call(first_sums_kernel, table, name="first_sums")(o_edges, o_middle, mine, end, drive)
    steps = sum_steps()
    sums = summed(sums, steps[:2])
    o_low, o_high, sums = lax.optimization_barrier((o_low, o_high, sums))
    o_sides = y_sides(
        o_low[:2], o_edges[:AHEAD], o_middle, o_edges[AHEAD:], o_high[:2], o_low[2:], end, o_high[2:]
    )
    sums = summed(sums, steps[2:])
    near, tangent_wide = call(
        other_step_kernel, [block, outer], [room(nz + 4), room(nz + 2)], "other_step"
    )(o_edges, o_middle, end, o_low, o_high, o_sides)

    whole = jax.ShapeDtypeStruct(images.shape, images.dtype)
    moved, drive2, minus, base = call(
        second_step_kernel,
        [block] * 3 + [whole],
        [room(nz + 4), room(nz + 2), DMA],
        "second_step",
        in_specs=[VMEM] * 4,
        out_specs=[VMEM] * 3 + [ANY],
    )(sums, step, tangent_wide, end)

    o_sums = lax.ppermute(sums, "image", SWAP)
    sums = call(second_sums_kernel, table, name="second_sums")(
        o_sums, far, mine, near, minus, drive2
    )

    return call(
        functools.partial(last_kernel, cells),
        [whole, shape(2)],
        [pltpu.VMEM(block.shape, jnp.float32), DMA((nz // 4,))],
        "last",
        in_specs=[VMEM] * 6 + [ANY],
        out_specs=[ANY, SMEM],
        input_output_aliases={6: 0},
    )(summed(sums, sum_steps()), o_sums, far, mine, near, moved, base)


def body(images):
    layers = lax.axis_size("space")
    pair = lax.axis_size("image") == 2 and lax.axis_size("yslab") == 2 and images.shape[0] == 2
    pair = pair and layers & (layers - 1) == 0 and images.shape[1] % 4 == 0
    pair = pair and images.shape[1] > 2 * AHEAD and images.shape[2] % CHUNK == 0
    return body_pair(images) if pair else body_any(images)


def solution(mesh):
    in_specs = (P(("groups", "image"), "space", "yslab", None),)
    out_specs = (P(("groups", "image"), "space", "yslab", None), P(("groups", "image")))
    return jax.shard_map(body, mesh=mesh, in_specs=in_specs, out_specs=out_specs, check_vma=False)
```

```python
import functools
import math

import jax
import jax.numpy as jnp
from jax import lax
from jax.experimental import pallas as pl
from jax.experimental.pallas import tpu as pltpu
from jax.sharding import PartitionSpec as P

ITERS = 2


GRADIENT_COEF = 1.0
MOBILITY = 0.004
SPRING_K = 1.0
STEP_SIZE = 0.5
EPSILON = 1e-06

PAD = 8
VMEM_ROOM = 2 * 2**20
UNROLL = 8
AHEAD = 2


def passed_along(array, axis, by):
    peers = lax.axis_size(axis)
    pairs = [(i, i + by) for i in range(peers) if 0 <= i + by < peers]
    return lax.ppermute(array, axis, pairs)


def extended(cells, sides, width):
    for axis, dim in sides:
        count = lax.axis_size(axis)
        head = lax.slice_in_dim(cells, 0, width, axis=dim)
        tail = lax.slice_in_dim(cells, cells.shape[dim] - width, cells.shape[dim], axis=dim)
        cells = jnp.concatenate(
            [
                lax.ppermute(tail, axis, [(i, (i + 1) % count) for i in range(count)]),
                cells,
                lax.ppermute(head, axis, [((i + 1) % count, i) for i in range(count)]),
            ],
            axis=dim,
        )
    return cells


def stencil(padded):
    middle = padded[:, 1:-1, 1:-1]
    neighbours = padded[:, 2:, 1:-1] + padded[:, :-2, 1:-1]
    neighbours = neighbours + padded[:, 1:-1, 2:] + padded[:, 1:-1, :-2]
    neighbours = neighbours + jnp.roll(middle, -1, 3) + jnp.roll(middle, 1, 3)
    return neighbours - 6.0 * middle


def sum_cells(field):
    return jnp.sum(field, axis=(1, 2, 3))


def body_any(images):
    current = images
    per_device = current.shape[0]
    total_images = per_device * lax.axis_size("image")
    cell_total = float(
        current.shape[1]
        * lax.axis_size("space")
        * current.shape[2]
        * lax.axis_size("yslab")
        * current.shape[3]
    )
    image_ids = lax.axis_index("image") * per_device + jnp.arange(per_device, dtype=jnp.int32)
    interior = (image_ids > 0) & (image_ids < total_images - 1)
    parallel = jnp.zeros((per_device,), jnp.float32)
    for iteration in range(ITERS):
        next_first = passed_along(current[0], "image", -1)
        prev_last = passed_along(current[-1], "image", 1)
        ahead = jnp.concatenate([current[1:], next_first[None]], 0)
        behind = jnp.concatenate([prev_last[None], current[:-1]], 0)
        forward = ahead - current
        backward = current - behind
        tangent = forward + backward
        plus_sq, minus_sq, tangent_sq = lax.psum(
            (
                sum_cells(forward * forward),
                sum_cells(backward * backward),
                sum_cells(tangent * tangent),
            ),
            ("space", "yslab"),
        )
        wide_pad = extended(current, (("space", 1), ("yslab", 2)), 2)
        inner_field = wide_pad[:, 1:-1, 1:-1]
        potential = (
            inner_field * inner_field * inner_field
            - inner_field
            - GRADIENT_COEF * stencil(wide_pad)
        )
        driving = MOBILITY * stencil(potential)
        parallel_sum = lax.psum(sum_cells(driving * tangent), ("space", "yslab"))
        project_coef = parallel_sum / (tangent_sq + EPSILON)
        spring = (
            SPRING_K * (jnp.sqrt(plus_sq) - jnp.sqrt(minus_sq)) / jnp.sqrt(tangent_sq + EPSILON)
        )
        update = (
            driving
            - project_coef[:, None, None, None] * tangent
            + spring[:, None, None, None] * tangent
        )
        current = jnp.where(interior[:, None, None, None], current + STEP_SIZE * update, current)
        parallel = jnp.where(
            interior, parallel_sum / jnp.sqrt((tangent_sq + EPSILON) * cell_total), jnp.float32(0.0)
        )
    return (current, parallel)


def call(kernel, out_shape, scratch=(), name=None, **kw):
    return pl.pallas_call(
        kernel,
        out_shape=out_shape,
        scratch_shapes=list(scratch),
        name=name,
        compiler_params=pltpu.CompilerParams(
            vmem_limit_bytes=VMEM_ROOM + sum(4 * math.prod(s.shape) for s in scratch if s is not DMA)
        ),
        **kw,
    )


def shape(*dims):
    return jax.ShapeDtypeStruct(dims, jnp.float32)


def lap(below, here, above):
    rows, lanes = here.shape
    ys = pltpu.roll(here, 1, 0) + pltpu.roll(here, rows - 1, 0)
    xs = pltpu.roll(here, 1, 1) + pltpu.roll(here, lanes - 1, 1)
    return (below + above) + ys + xs - 6.0 * here


def layer_loop(start, stop, body):
    def step(k, carry):
        body(k)
        return carry

    lax.fori_loop(start, stop, step, 0, unroll=min(UNROLL, stop - start))


def potentials(field, pot, count):
    def one(k):
        here = field[k + 1]
        pot[k] = here * here * here - here - GRADIENT_COEF * lap(field[k], here, field[k + 2])

    layer_loop(0, count, one)


def driving(pot, k):
    return MOBILITY * lap(pot[k], pot[k + 1], pot[k + 2])


def rows_sum(field):
    rows, lanes = field.shape
    return jnp.sum(field.reshape(rows // 8, 8, lanes), axis=0)


def lane_row(total):
    lanes = total.shape[1]
    folded = jnp.sum(total.reshape(8, lanes // 128, 128), axis=1)
    return jnp.sum(folded, axis=0, keepdims=True)


def fill_padded(dst, pieces, sides, sides_at):
    at = 0
    for piece in pieces:
        layers, rows, _ = piece.shape
        dst[at : at + layers, PAD : PAD + rows] = piece[...]
        at += layers
    dst[:, 0:PAD] = sides[sides_at : sides_at + at, PAD : 2 * PAD]
    dst[:, PAD + rows : 2 * PAD + rows] = sides[sides_at : sides_at + at, 0:PAD]


def all_copied(pairs, sems):
    copies = [pltpu.make_async_copy(src, dst, sems.at[i]) for i, (src, dst) in enumerate(pairs)]
    for c in copies:
        c.start()
    for c in copies:
        c.wait()


def send_kernel(images, edges, middle, sems):
    which = 1 - lax.axis_index("image")
    nz = images.shape[1]
    pairs = [
        (images.at[which, pl.ds(0, AHEAD)], edges.at[pl.ds(0, AHEAD)]),
        (images.at[which, pl.ds(nz - AHEAD, AHEAD)], edges.at[pl.ds(AHEAD, AHEAD)]),
        (images.at[which, pl.ds(AHEAD, nz - 2 * AHEAD)], middle),
    ]
    all_copied(pairs, sems)


def keep_kernel(images, mine, end, up, down, sems):
    which = 1 - lax.axis_index("image")
    nz, layers = mine.shape[0], up.shape[0]
    pairs = [
        (images.at[which, pl.ds(nz - layers, layers)], up),
        (images.at[which, pl.ds(0, layers)], down),
        (images.at[which], mine),
        (images.at[1 - which], end),
    ]
    all_copied(pairs, sems)


def first_step_kernel(mine, low, high, sides, step_out, drive_out, field, pot):
    nz, rows, _ = mine.shape
    fill_padded(field, (low, mine, high), sides, 0)
    potentials(field, pot, nz + 6)

    def edge(k):
        step_out[k] = field[k + 2] + STEP_SIZE * driving(pot, k)

    def inner(k):
        drive = driving(pot, k)
        step_out[k] = field[k + 2] + STEP_SIZE * drive
        drive_out[k - 2] = drive[PAD : PAD + rows]

    layer_loop(0, 2, edge)
    layer_loop(2, nz + 2, inner)
    layer_loop(nz + 2, nz + 4, edge)


CHUNK = 16


def sums_of(start, stop, rows, terms, totals):
    def one(k, totals):
        for r in range(0, rows, CHUNK):
            totals = tuple(t + rows_sum(v) for t, v in zip(totals, terms(k, pl.ds(r, CHUNK))))
        return totals

    return lax.fori_loop(start, stop, one, totals, unroll=True)


def no_sums(count, lanes):
    return (jnp.zeros((8, lanes), jnp.float32),) * count


def table_of(*rows):
    return jnp.concatenate(rows + (jnp.zeros((8 - len(rows), 128), jnp.float32),), 0)


def first_sums_kernel(edges, middle, mine, end, drive, out):
    nz, rows, lanes = mine.shape

    def terms_from(other, shift):
        def terms(k, r):
            m, o, e = mine[k, r], other[k + shift, r], end[k, r]
            plus, minus, tangent = o - m, m - e, o - e
            return plus * plus, minus * minus, tangent * tangent, drive[k, r] * tangent

        return terms

    last = nz - AHEAD
    totals = sums_of(0, AHEAD, rows, terms_from(edges, 0), no_sums(4, lanes))
    totals = sums_of(AHEAD, last, rows, terms_from(middle, -AHEAD), totals)
    totals = sums_of(last, nz, rows, terms_from(edges, AHEAD - last), totals)
    out[...] = table_of(*(lane_row(t) for t in totals))


def coefficient(sums):
    total = jnp.sum(sums[...], axis=1, keepdims=True)
    plus_sq, minus_sq, tangent_sq, par = (total[i : i + 1] for i in range(4))
    safe = tangent_sq + EPSILON
    spring = SPRING_K * (jnp.sqrt(plus_sq) - jnp.sqrt(minus_sq)) / jnp.sqrt(safe)
    return STEP_SIZE * (spring - par / safe), par, safe


def other_step_kernel(edges, middle, end, low, high, sides, near_out, tangent_out, field, pot):
    nz, rows, _ = end.shape
    first, last = edges.at[0:AHEAD], edges.at[AHEAD : 2 * AHEAD]
    fill_padded(field, (low.at[0:2], first, middle, last, high.at[0:2]), sides, 0)
    fill_padded(tangent_out, (low.at[2:4], end, high.at[2:4]), sides, nz + 4)
    potentials(field, pot, nz + 2)

    def widen(k):
        tangent_out[k] = field[k] - tangent_out[k]

    def one(k):
        moved = field[k + 2] + STEP_SIZE * driving(pot, k)
        near_out[k] = moved[PAD : PAD + rows] - end[k]

    layer_loop(0, nz + 4, widen)
    layer_loop(0, nz, one)


def second_step_kernel(
    sums, step, tangent_wide, end, moved_out, drive_out, minus_out, base, field, pot, sem
):
    nz, rows, _ = end.shape
    still = lax.axis_index("image")
    copy = pltpu.make_async_copy(end, base.at[still], sem)
    copy.start()
    coef, _, _ = coefficient(sums)

    def move(k):
        field[k] = step[k] + coef * tangent_wide[k]

    layer_loop(0, nz + 4, move)
    potentials(field, pot, nz + 2)

    def one(k):
        drive = driving(pot, k)[PAD : PAD + rows]
        here = field[k + 2][PAD : PAD + rows]
        drive_out[k] = drive
        minus_out[k] = here - end[k]
        moved_out[k] = here + STEP_SIZE * drive

    layer_loop(0, nz, one)
    copy.wait()


def second_sums_kernel(o_sums, far, mine, near, minus, drive, out):
    nz, rows, lanes = far.shape
    coef, _, _ = coefficient(o_sums)

    def terms(k, r):
        tangent = near[k, r] + coef * (mine[k, r] - far[k, r])
        m = minus[k, r]
        plus = tangent - m
        return plus * plus, m * m, tangent * tangent, drive[k, r] * tangent

    out[...] = table_of(*(lane_row(t) for t in sums_of(0, nz, rows, terms, no_sums(4, lanes))))


def last_kernel(cells, sums, o_sums, far, mine, near, moved, base, out, par_out, buf, sems):
    del base
    nz = moved.shape[0]
    at = lax.axis_index("image")
    which = 1 - at
    coef, par, safe = coefficient(sums)
    o_coef, _, _ = coefficient(o_sums)
    copies = []
    for k in range(nz):
        buf[k] = moved[k] + coef * (near[k] + o_coef * (mine[k] - far[k]))
        if k % 2 == 1:
            where = pl.ds(k - 1, 2)
            copies.append(
                pltpu.make_async_copy(buf.at[where], out.at[which, where], sems.at[k // 2])
            )
            copies[-1].start()
    value = (par / jnp.sqrt(safe * cells))[0, 0]
    sign = jnp.where(at == 0, 1.0, -1.0).astype(jnp.float32)
    par_out[which] = value * sign
    par_out[1 - which] = jnp.float32(0.0)
    for c in copies:
        c.wait()


ANY = pl.BlockSpec(memory_space=pl.ANY)
VMEM = pl.BlockSpec(memory_space=pltpu.VMEM)
SMEM = pl.BlockSpec(memory_space=pltpu.SMEM)
DMA = pltpu.SemaphoreType.DMA
SWAP = [(0, 1), (1, 0)]


def from_z(up, down):
    count = lax.axis_size("space")
    low = lax.ppermute(up, "space", [(i, (i + 1) % count) for i in range(count)])
    high = lax.ppermute(down, "space", [((i + 1) % count, i) for i in range(count)])
    return low, high


def y_sides(*pieces):
    rows = pieces[0].shape[1]
    ends = [jnp.concatenate([p[:, :PAD], p[:, rows - PAD :]], 1) for p in pieces]
    return lax.ppermute(jnp.concatenate(ends, 0), "yslab", SWAP)


def sum_steps():
    count = lax.axis_size("space")
    stride = count // 2
    steps = [("yslab", SWAP)]
    while stride:
        steps.append(("space", [(i, i ^ stride) for i in range(count)]))
        stride //= 2
    return steps


def summed(sums, steps):
    for axis, pairs in steps:
        sums = sums + lax.ppermute(sums, axis, pairs)
    return sums


def body_pair(images):
    _, nz, ny, nx = images.shape
    wide = ny + 2 * PAD
    cells = float(nz * lax.axis_size("space") * ny * lax.axis_size("yslab") * nx)
    block, outer = shape(nz, ny, nx), shape(nz + 4, wide, nx)
    table = shape(8, 128)

    def room(layers):
        return pltpu.VMEM((layers, wide, nx), jnp.float32)

    thin = shape(4, ny, nx)
    source = pltpu.with_memory_space_constraint(images, pltpu.HBM)
    edges, middle = call(
        send_kernel,
        [shape(2 * AHEAD, ny, nx), shape(nz - 2 * AHEAD, ny, nx)],
        [DMA((3,))],
        "send",
        in_specs=[ANY],
        out_specs=[ANY] * 2,
    )(source)
    mine, end, up, down = call(
        keep_kernel,
        [block, block, thin, thin],
        [DMA((4,))],
        "keep",
        in_specs=[ANY],
        out_specs=[ANY] * 4,
    )(source)

    o_first = lax.ppermute(edges[:AHEAD], "image", SWAP)
    o_last = lax.ppermute(edges[AHEAD:], "image", SWAP)
    o_middle = lax.ppermute(middle, "image", SWAP)
    far = lax.ppermute(end, "image", SWAP)

    up, down, o_first = lax.optimization_barrier((up, down, o_first))
    o_edges = jnp.concatenate([o_first, o_last])
    low, high = from_z(up, down)
    sides = y_sides(low, mine, high)
    step, drive = call(first_step_kernel, [outer, block], [room(nz + 8), room(nz + 6)], "first_step")(
        mine, low, high, sides
    )

    o_edges, low, high = lax.optimization_barrier((o_edges, low, high))
    o_low, o_high = from_z(
        jnp.concatenate([o_edges[2 * AHEAD - 2 :], end[nz - 2 :]]),
        jnp.concatenate([o_edges[:2], end[:2]]),
    )
    sums = call(first_sums_kernel, table, name="first_sums")(o_edges, o_middle, mine, end, drive)
    steps = sum_steps()
    sums = summed(sums, steps[:2])
    o_low, o_high, sums = lax.optimization_barrier((o_low, o_high, sums))
    o_sides = y_sides(
        o_low[:2], o_edges[:AHEAD], o_middle, o_edges[AHEAD:], o_high[:2], o_low[2:], end, o_high[2:]
    )
    sums = summed(sums, steps[2:])
    near, tangent_wide = call(
        other_step_kernel, [block, outer], [room(nz + 4), room(nz + 2)], "other_step"
    )(o_edges, o_middle, end, o_low, o_high, o_sides)

    whole = jax.ShapeDtypeStruct(images.shape, images.dtype)
    moved, drive2, minus, base = call(
        second_step_kernel,
        [block] * 3 + [whole],
        [room(nz + 4), room(nz + 2), DMA],
        "second_step",
        in_specs=[VMEM] * 4,
        out_specs=[VMEM] * 3 + [ANY],
    )(sums, step, tangent_wide, end)

    o_sums = lax.ppermute(sums, "image", SWAP)
    sums = call(second_sums_kernel, table, name="second_sums")(
        o_sums, far, mine, near, minus, drive2
    )

    return call(
        functools.partial(last_kernel, cells),
        [whole, shape(2)],
        [pltpu.VMEM(block.shape, jnp.float32), DMA((nz // 2,))],
        "last",
        in_specs=[VMEM] * 6 + [ANY],
        out_specs=[ANY, SMEM],
        input_output_aliases={6: 0},
    )(summed(sums, sum_steps()), o_sums, far, mine, near, moved, base)


def body(images):
    layers = lax.axis_size("space")
    pair = lax.axis_size("image") == 2 and lax.axis_size("yslab") == 2 and images.shape[0] == 2
    pair = pair and layers & (layers - 1) == 0 and images.shape[1] % 4 == 0
    pair = pair and images.shape[1] > 2 * AHEAD and images.shape[2] % CHUNK == 0
    return body_pair(images) if pair else body_any(images)


def solution(mesh):
    in_specs = (P(("groups", "image"), "space", "yslab", None),)
    out_specs = (P(("groups", "image"), "space", "yslab", None), P(("groups", "image")))
    return jax.shard_map(body, mesh=mesh, in_specs=in_specs, out_specs=out_specs, check_vma=False)
```
